256 devices in a mesh: ctx: 128 (over y, z, x_hi, core), mp: 2 (over x_lo).
Axes of the slice: x: 4 (x_hi: 2, x_lo: 2; x = x_hi * 2 + x_lo), y: 4, z: 8, core: 2. Of those that a mesh axis runs over, the one named last changes fastest.
Arguments:
- queries: bfloat16 [98304, 512], P(('mp', 'ctx')), parts along dimension 0, may hold values from -27 to 27
- key_rows: bfloat16 [98304, 128], P(('mp', 'ctx')), parts along dimension 0, may hold values from -27 to 27
- value_rows: bfloat16 [98304, 128], P(('mp', 'ctx')), parts along dimension 0, may hold values from -6 to 6
- positions: int32 [49152], P('ctx'), may hold values from 0 to 49151, as said below
- latent_ids: int32 [98304, 8], P(('mp', 'ctx')), parts along dimension 0, may hold values from 0 to 511
- latent_acts: float32 [98304, 8], P(('mp', 'ctx')), parts along dimension 0, may hold values from 0.5 to 4
- latent_dirs: float32 [1024, 512], P('mp'), parts along dimension 0, may hold values from -2 to 2
Outputs:
- grad_queries: bfloat16 [98304, 512], P(('mp', 'ctx')), parts along dimension 0
- grad_keys: bfloat16 [98304, 128], P(('mp', 'ctx')), parts along dimension 0
- grad_values: bfloat16 [98304, 128], P(('mp', 'ctx')), parts along dimension 0
The draws below stay inside these ranges and needn't reach their ends.
There are 2 independent parts, one for each index of `mp`. The reference program is written for one: setup_inputs(seed, part) draws one part's arguments, and reference() takes and returns one part's arrays. A program takes and returns all parts, laid end to end along the dimension named above; an argument that names none is the same for every part. Nothing has to cross between parts.
Inputs may be any that keep to these rules, and one draw needn't show every extreme that they name: `positions`: the position of token i is (i - r) mod 49152 for one offset r of the draw.
All inputs are finite; a program needn't handle non-finite values.
Results may differ from the reference program's by a relative error of at most 0.019.
Values may be sent and summed in bfloat16 or wider, within the bound.
No kernel may reach another device: no remote copies, remote signals or barrier semaphores. Data moves between devices by JAX's collectives and lax.ppermute only.
A program may use at most 128 MiB of HBM per device.

```python
import math
import jax
import jax.numpy as jnp
from jax import lax

HEADS_Q = 4
HEAD_DIM = 128
WINDOW = 4096
LATENTS = 512
TOPK = 8
TOK_DEV = 384
SPAN = 11
TOKENS = 49152
N_CTX = 128


def shared_base(key):
    return jnp.clip(jax.random.normal(jax.random.fold_in(key, 11), (TOKENS, HEAD_DIM), jnp.float32), -6.0, 6.0)


def draw_key_rows(key, part):
    base = shared_base(key)
    result = base
    return result.astype(jnp.bfloat16)


def draw_queries(key, part):
    own_key = jax.random.fold_in(key, 21)
    normal_part = jnp.clip(jax.random.normal(own_key, (TOKENS, HEADS_Q * HEAD_DIM), jnp.float32), -6.0, 6.0)
    result = normal_part
    return result.astype(jnp.bfloat16)


def draw_positions(key, part):
    key = jax.random.fold_in(key, 31)
    offset = jax.random.randint(key, (), 0, TOKENS)
    return jnp.mod(jnp.arange(TOKENS, dtype=jnp.int32) - offset, TOKENS).astype(jnp.int32)


def touch_ends(values, key, smallest, high):
    longest = values.shape.index(max(values.shape))
    spots = []
    for shift in (0, 1):
        where = [jax.random.randint(jax.random.fold_in(key, axis), (), 0, length) for axis, length in enumerate(values.shape)]
        where[longest] = (where[longest] + shift) % values.shape[longest]
        spots.append(tuple(where))
    return values.at[spots[0]].set(smallest).at[spots[1]].set(high)


def block_scale(stream_key, dims, shards, low, largest):
    factor_of, own = 1.0, jax.random.fold_in(stream_key, 6)
    for dim, shards_of in shards:
        heights = jnp.exp(jax.random.uniform(jax.random.fold_in(own, dim), (shards_of,), jnp.float32, low / len(shards), largest / len(shards)))
        factor_of = factor_of * jnp.repeat(heights, dims[dim] // shards_of).reshape([-1 if axis == dim else 1 for axis in range(len(dims))])
    return factor_of


def scatter_about(key, shape, spread, limit, cuts=(), kind=jnp.bfloat16):
    level = block_scale(key, shape, cuts, -0.22, 0.18) if cuts else 1.0
    entries = jax.random.normal(key, shape, jnp.float32) * spread * level
    return jnp.minimum(jnp.maximum(entries, -limit), limit).astype(kind)


def setup_inputs(seed: int = 0, part: int = 0) -> dict:
    seeds = jax.random.split(jax.random.key(seed), 8)
    part_keys = jax.random.split(jax.random.fold_in(seeds[7], part), 8)
    queries = draw_queries(jax.random.fold_in(jax.random.fold_in(seeds[7], part), 71), part)
    key_rows = draw_key_rows(jax.random.fold_in(jax.random.fold_in(seeds[7], part), 71), part)
    value_rows = scatter_about(part_keys[2], (TOKENS, HEAD_DIM), 1.0, 6.0, ((0, 128),))
    positions = draw_positions(jax.random.fold_in(seeds[7], 71), part)
    latent_ids = touch_ends(jax.random.randint(part_keys[4], (TOKENS, TOPK), 0, LATENTS), jax.random.fold_in(part_keys[4], 1), 0, LATENTS - 1).astype(jnp.int32)
    latent_acts = jnp.clip(jnp.exp(math.log(4.0) - 2.0794415 * jax.random.uniform(part_keys[5], (TOKENS, TOPK), jnp.float32) ** block_scale(part_keys[5], (TOKENS, TOPK), ((0, 128),), -0.2, 0.2)), 0.5, 4.0)
    latent_dirs = scatter_about(part_keys[6], (LATENTS, HEADS_Q * HEAD_DIM), 0.35, 2.0, (), jnp.float32)
    return {"queries": queries, "key_rows": key_rows, "value_rows": value_rows, "positions": positions, "latent_ids": latent_ids, "latent_acts": latent_acts, "latent_dirs": latent_dirs}


def seed_block(latent_ids, latent_acts, latent_dirs):
    columns = jnp.arange(latent_dirs.shape[0], dtype=jnp.int32)
    onehot = (latent_ids[:, :, None] == columns[None, None, :]).astype(jnp.float32)
    mixing = lax.optimization_barrier(jnp.sum(latent_acts[:, :, None] * onehot, axis=1))
    return jnp.dot(mixing, latent_dirs, precision=lax.Precision.HIGHEST, preferred_element_type=jnp.float32).astype(jnp.bfloat16)

def block_grads(query_block, seed_rows, key_window, value_window, query_pos, key_pos):
    row_count = query_block.shape[0]
    head_size = key_window.shape[1]
    head_count = query_block.shape[1] // head_size
    factor = 1.0 / math.sqrt(head_size)
    offsets = query_pos[:, None] - key_pos[None, :]
    visible = (offsets >= 0) & (offsets < WINDOW)
    query_heads = query_block.reshape(row_count, head_count, head_size).transpose(1, 0, 2)
    seed_heads = seed_rows.reshape(row_count, head_count, head_size).transpose(1, 0, 2)

    def per_head(carry, inputs):
        query_one, seed_one = inputs
        scores = jnp.where(visible, jnp.dot(query_one, key_window.T, preferred_element_type=jnp.float32) * factor, -jnp.inf)
        maxima = lax.optimization_barrier(jnp.max(scores, axis=-1, keepdims=True))
        expos = jnp.exp(scores - maxima)
        totals = lax.optimization_barrier(jnp.sum(expos, axis=-1, keepdims=True))
        probs = expos / totals
        probs_b = probs.astype(jnp.bfloat16)
        dprobs = jnp.dot(seed_one, value_window.T, preferred_element_type=jnp.float32)
        deltas = lax.optimization_barrier(jnp.sum(probs * dprobs, axis=-1, keepdims=True))
        dscores = (probs * (dprobs - deltas) * factor).astype(jnp.bfloat16)
        grad_query = jnp.dot(dscores, key_window, preferred_element_type=jnp.float32)
        grad_key = jnp.dot(dscores.T, query_one, preferred_element_type=jnp.float32)
        grad_value = jnp.dot(probs_b.T, seed_one, preferred_element_type=jnp.float32)
        return ((carry[0] + grad_key, carry[1] + grad_value), grad_query)
    start_acc = jnp.zeros((key_window.shape[0], head_size), jnp.float32)
    (grad_keys, grad_values), grad_queries = lax.scan(per_head, (start_acc, start_acc), (query_heads, seed_heads))
    grad_queries = grad_queries.transpose(1, 0, 2).reshape(row_count, head_count * head_size)
    return (grad_queries, grad_keys, grad_values)

def reference(queries, key_rows, value_rows, positions, latent_ids, latent_acts, latent_dirs):
    span_rows = SPAN * TOK_DEV
    window_rows = span_rows + TOK_DEV
    head_size = key_rows.shape[1]
    key_pad = jnp.concatenate([key_rows[-span_rows:], key_rows], axis=0)
    value_pad = jnp.concatenate([value_rows[-span_rows:], value_rows], axis=0)
    pos_pad = jnp.concatenate([positions[-span_rows:], positions], axis=0)

    def step(carry, index):
        start = (index * TOK_DEV).astype(jnp.int32)
        query_block = lax.dynamic_slice_in_dim(queries, start, TOK_DEV, 0)
        seed_rows = seed_block(lax.dynamic_slice_in_dim(latent_ids, start, TOK_DEV, 0), lax.dynamic_slice_in_dim(latent_acts, start, TOK_DEV, 0), latent_dirs)
        key_window = lax.dynamic_slice_in_dim(key_pad, start, window_rows, 0)
        value_window = lax.dynamic_slice_in_dim(value_pad, start, window_rows, 0)
        key_pos = lax.dynamic_slice_in_dim(pos_pad, start, window_rows, 0)
        query_pos = lax.dynamic_slice_in_dim(positions, start, TOK_DEV, 0)
        grad_q, grad_k, grad_v = block_grads(query_block, seed_rows, key_window, value_window, query_pos, key_pos)
        acc_keys = lax.dynamic_update_slice_in_dim(carry[0], lax.dynamic_slice_in_dim(carry[0], start, window_rows, 0) + grad_k, start, 0)
        acc_values = lax.dynamic_update_slice_in_dim(carry[1], lax.dynamic_slice_in_dim(carry[1], start, window_rows, 0) + grad_v, start, 0)
        return ((acc_keys, acc_values), grad_q)
    start_acc = jnp.zeros((TOKENS + span_rows, head_size), jnp.float32)
    (acc_keys, acc_values), grad_blocks = lax.scan(step, (start_acc, start_acc), jnp.arange(N_CTX, dtype=jnp.int32))
    grad_queries = grad_blocks.reshape(TOKENS, queries.shape[1])
    grad_keys = acc_keys[span_rows:].at[TOKENS - span_rows:].add(acc_keys[:span_rows])
    grad_values = acc_values[span_rows:].at[TOKENS - span_rows:].add(acc_values[:span_rows])
    return (grad_queries.astype(jnp.bfloat16), grad_keys.astype(jnp.bfloat16), grad_values.astype(jnp.bfloat16))
```

```python
import functools
import math

import jax
import jax.numpy as jnp
from jax import lax
from jax.experimental import pallas as pl
from jax.experimental.pallas import tpu as pltpu
from jax.sharding import PartitionSpec as P

TEAM = 4
ROWS = 384
TILES = 3
TILE = 128
HEADS = 4
DIM = 128
WIDE = HEADS * TILE
WINDOW = 4096
FACTOR = 1.0 / math.sqrt(DIM)
SCALE = FACTOR * math.log2(math.e)
HIDE = -1e30
VMEM_LIMIT = 56 * 1024 * 1024

BF16 = jnp.bfloat16
F32 = jnp.float32


def permute(value, target):
    count = lax.axis_size("ctx")
    return lax.ppermute(value, "ctx", [(s, target(s) % count) for s in range(count)])


def dot(a, b):
    return jnp.dot(a, b, preferred_element_type=F32)


def seed_kernel(ids_ref, acts_ref, dirs_ref, seed_ref):
    latents = dirs_ref.shape[0]
    rows = ids_ref.shape[1]
    lane = lax.broadcasted_iota(jnp.int32, (latents, rows), 0)
    mixing = jnp.zeros((latents, rows), F32)
    for k in range(ids_ref.shape[0]):
        mixing = mixing + jnp.where(lane == ids_ref[k : k + 1, :], acts_ref[k : k + 1, :], 0.0)
    seed_ref[...] = lax.dot_general(
        mixing,
        dirs_ref[...],
        (((0,), (0,)), ((), ())),
        precision=lax.Precision.HIGHEST,
        preferred_element_type=F32,
    ).astype(BF16)


def seeds_of(latent_ids, latent_acts, latent_dirs):
    return pl.pallas_call(
        seed_kernel,
        out_shape=jax.ShapeDtypeStruct((latent_ids.shape[0], latent_dirs.shape[1]), BF16),
        compiler_params=pltpu.CompilerParams(vmem_limit_bytes=VMEM_LIMIT),
    )(latent_ids.T, latent_acts.T, latent_dirs)


HEAD_SCALARS = 8


def full_jobs():
    jobs = []
    for t in (2, 1, 0):
        for u in range(TEAM):
            for at in range(TILES):
                if (u, t) == (0, 0) or (u, t) == (3, 2) or (u, t, at) == (2, 2, 2):
                    continue
                jobs.append((u, at, t))
    return jobs


FULL = full_jobs()


def scalars_of(positions):
    member = lax.axis_index("ctx") % TEAM
    core = member % 2
    tokens = positions.shape[0] * lax.axis_size("ctx")
    first = positions[0]
    begin = jnp.where(first < tokens // 2, -first, tokens - first)
    slots = jnp.stack([0 * core, 1 + 2 * core, 0 * core + 2, 3 - 2 * core])
    wraps = (member + jnp.arange(TEAM) >= TEAM).astype(jnp.int32)
    jobs = jnp.array(FULL, jnp.int32)
    table = jnp.stack([slots[jobs[:, 0]], jobs[:, 1], jobs[:, 2] + wraps[jobs[:, 0]]], axis=1)
    head = jnp.concatenate([jnp.stack([begin, slots[1], slots[3], begin]), wraps])
    return jnp.concatenate([head, table.reshape(-1)]).astype(jnp.int32)


def masked_jobs(scal):
    jobs = [(0, at, 0, 0, (at + 1) * TILE, ("causal", at * TILE)) for at in range(TILES)]
    jobs.append((2, 2, 2 + scal[6], 0, ROWS, ("tail", 1)))
    jobs.append((scal[2], 0, 2 + scal[7], TILE, 2 * TILE, ("tail", 1)))
    jobs.append((scal[2], 1, 2 + scal[7], 2 * TILE, TILE, ("tail", 1)))
    return jobs


def mask_of(kind, keys):
    name, shift = kind
    key = lax.broadcasted_iota(jnp.int32, (keys, WIDE), 0)
    query = lax.broadcasted_iota(jnp.int32, (keys, WIDE), 1) % TILE
    if name == "causal":
        return key <= query + shift
    return key >= query + shift


def fill_keys(scal, kv_refs, kx_ref, vx_ref=None, kt_ref=None):
    lane = lax.broadcasted_iota(jnp.int32, (ROWS, DIM), 1)
    row = lax.broadcasted_iota(jnp.int32, (ROWS, DIM), 0)
    ones = jnp.where(lane < 3, 1.0, 0.0)
    for d, kv_ref in enumerate(kv_refs):
        before = row - TEAM * ROWS * d < scal[0]
        kx_ref[d, :, :DIM] = kv_ref[:ROWS]
        kx_ref[d, :, DIM:] = jnp.where((lane == 3) & before, HIDE, ones).astype(BF16)
        if vx_ref is not None:
            vx_ref[d, :, :DIM] = kv_ref[ROWS:]
            vx_ref[d, :, DIM:] = ones.astype(BF16)
        if kt_ref is not None:
            for j in range(TILES):
                kt_ref[d, :, j * TILE : (j + 1) * TILE] = kv_ref[j * TILE : (j + 1) * TILE].T


def row_flags(scal, slot, at):
    if slot == 0:
        offset = 0
    elif slot == 2:
        offset = 2 * ROWS - TEAM * ROWS * scal[6]
    else:
        is_one = scal[1] == slot
        offset = jnp.where(
            is_one, ROWS - TEAM * ROWS * scal[5], 3 * ROWS - TEAM * ROWS * scal[7]
        )
    query = lax.broadcasted_iota(jnp.int32, (1, WIDE), 1) % TILE
    return jnp.where(query + at * TILE + offset >= scal[0], 1.0, 0.0)


def stats_kernel(scal, *refs):
    q_refs, s_refs, kv_refs = refs[0:4], refs[4:8], refs[8:12]
    stat_ref, qt_ref, st_ref = refs[12:15]
    kx_ref, aug_ref, run_ref = refs[15:18]
    fill_keys(scal, kv_refs, kx_ref)
    aug_ref[...] = jnp.zeros_like(aug_ref)
    row8 = lax.broadcasted_iota(jnp.int32, (16, WIDE), 0)
    for slot in range(TEAM):
        for at in range(TILES):
            n = slot * TILES + at
            for h in range(HEADS):
                cut = (slice(at * TILE, (at + 1) * TILE), slice(h * DIM, (h + 1) * DIM))
                into = (n, slice(None), slice(h * TILE, (h + 1) * TILE))
                qt_ref[into] = q_refs[slot][cut].T
                st_ref[into] = s_refs[slot][cut].T
            aug_ref[n, :16] = jnp.where(row8 == 3, row_flags(scal, slot, at), 0.0).astype(BF16)
            run_ref[n, 0:1] = jnp.full((1, WIDE), 2 * HIDE, F32)
            run_ref[n, 1:3] = jnp.zeros((2, WIDE), F32)

    def job(slot, at, d, j0, keys, kind):
        n = slot * TILES + at
        qx = jnp.concatenate([qt_ref[n], aug_ref[n]], axis=0)
        s = dot(kx_ref[d, j0 : j0 + keys], qx)
        if kind is not None:
            s = jnp.where(mask_of(kind, keys), s, HIDE)
        if len(kv_refs) == 4:
            v = v_of(d, j0, keys)
        dp = dot(v, st_ref[n])
        old = run_ref[n, 0:1]
        new = jnp.maximum(old, jnp.max(s, axis=0, keepdims=True))
        p = jnp.exp2((s - new) * SCALE)
        fade = jnp.exp2((old - new) * SCALE)
        run_ref[n, 0:1] = new
        run_ref[n, 1:2] = run_ref[n, 1:2] * fade + jnp.sum(p, axis=0, keepdims=True)
        run_ref[n, 2:3] = run_ref[n, 2:3] * fade + jnp.sum(p * dp, axis=0, keepdims=True)

    v_ref = refs[18]
    for d in range(TEAM):
        v_ref[d] = kv_refs[d][ROWS:]

    def v_of(d, j0, keys):
        return v_ref[d, j0 : j0 + keys]

    def step(index, carry):
        base = HEAD_SCALARS + 3 * index
        job(scal[base], scal[base + 1], scal[base + 2], 0, ROWS, None)
        return carry

    lax.fori_loop(0, len(FULL), step, 0)
    for one in masked_jobs(scal):
        job(*one)
    for slot in range(TEAM):
        for at in range(TILES):
            n = slot * TILES + at
            total = run_ref[n, 1:2]
            stat_ref[slot, at : at + 1] = run_ref[n, 0:1] + jnp.log2(total) * (1.0 / SCALE)
            stat_ref[slot, 3 + at : 4 + at] = run_ref[n, 2:3] / total
        stat_ref[slot, 6:8] = jnp.zeros((2, WIDE), F32)


def stats_of(scal, q_slots, s_slots, kvs):
    smem = pl.BlockSpec(memory_space=pltpu.SMEM)
    vmem = pl.BlockSpec(memory_space=pltpu.VMEM)
    turned = jax.ShapeDtypeStruct((TEAM * TILES, DIM, WIDE), BF16)
    return pl.pallas_call(
        stats_kernel,
        out_shape=(jax.ShapeDtypeStruct((TEAM, 8, WIDE), F32), turned, turned),
        in_specs=[smem] + [vmem] * 12,
        out_specs=(vmem, vmem, vmem),
        scratch_shapes=[
            pltpu.VMEM((TEAM, ROWS, 2 * DIM), BF16),
            pltpu.VMEM((TEAM * TILES, DIM, WIDE), BF16),
            pltpu.VMEM((TEAM * TILES, 8, WIDE), F32),
            pltpu.VMEM((TEAM, ROWS, DIM), BF16),
        ],
        compiler_params=pltpu.CompilerParams(vmem_limit_bytes=VMEM_LIMIT),
    )(scal, *q_slots, *s_slots, *kvs)


def split3(value):
    high = value.astype(BF16)
    rest = value - high.astype(F32)
    mid = rest.astype(BF16)
    low = (rest - mid.astype(F32)).astype(BF16)
    return high, mid, low


def grads_kernel(scal, *refs):
    stat_refs, q_refs, s_refs, kv_refs = refs[0:4], refs[4:8], refs[8:12], refs[12:16]
    qt_ref, st_ref = refs[16:18]
    dq_own_ref, dq_far_ref, dq_core_ref, kv_own_ref = refs[18:22]
    kv_send_refs = refs[22:25]
    kx_ref, vx_ref, kt_ref, qn_ref, sn_ref, qa_ref, sa_ref, dq_ref, dk_ref, dv_ref = refs[25:35]
    fill_keys(scal, kv_refs, kx_ref, vx_ref, kt_ref)
    qa_ref[...] = jnp.zeros_like(qa_ref)
    sa_ref[...] = jnp.zeros_like(sa_ref)
    dq_ref[...] = jnp.zeros_like(dq_ref)
    dk_ref[...] = jnp.zeros_like(dk_ref)
    dv_ref[...] = jnp.zeros_like(dv_ref)
    row16 = lax.broadcasted_iota(jnp.int32, (16, WIDE), 0)

    def rows_of(values):
        out = jnp.zeros((16, WIDE), F32)
        for index, value in enumerate(values):
            out = jnp.where(row16 == index, value.astype(F32), out)
        return out.astype(BF16)

    for slot in range(TEAM):
        for at in range(TILES):
            n = slot * TILES + at
            for h in range(HEADS):
                cut = (slice(at * TILE, (at + 1) * TILE), slice(h * DIM, (h + 1) * DIM))
                qn_ref[n, h * TILE : (h + 1) * TILE] = q_refs[slot][cut]
                sn_ref[n, h * TILE : (h + 1) * TILE] = s_refs[slot][cut]
            sums = [stat_refs[e][slot ^ e, at : at + 1] for e in range(TEAM)]
            deltas = [stat_refs[e][slot ^ e, 3 + at : 4 + at] for e in range(TEAM)]
            top = functools.reduce(jnp.maximum, sums)
            weights = [jnp.exp2((one - top) * SCALE) for one in sums]
            total = sum(weights)
            whole = top + jnp.log2(total) * (1.0 / SCALE)
            delta = sum(w * x for w, x in zip(weights, deltas)) / total
            qa_ref[n, :16] = rows_of(split3(-whole) + (row_flags(scal, slot, at),))
            sa_ref[n, :16] = rows_of(split3(-delta))

    def job(slot, at, d, j0, keys, kind):
        n = slot * TILES + at
        part = slice(j0, j0 + keys)
        logits = dot(kx_ref[d, part], jnp.concatenate([qt_ref[n], qa_ref[n]], axis=0))
        p = jnp.exp2(logits * SCALE)
        if kind is not None:
            p = jnp.where(mask_of(kind, keys), p, 0.0)
        dp = dot(vx_ref[d, part], jnp.concatenate([st_ref[n], sa_ref[n]], axis=0))
        ds = (p * dp).astype(BF16)
        dv_ref[d, part] += dot(p.astype(BF16), sn_ref[n])
        dk_ref[d, part] += dot(ds, qn_ref[n])
        dq_ref[n] += dot(kt_ref[d, :, part], ds)

    def step(index, carry):
        base = HEAD_SCALARS + 3 * index
        job(scal[base], scal[base + 1], scal[base + 2], 0, ROWS, None)
        return carry

    lax.fori_loop(0, len(FULL), step, 0)
    for one in masked_jobs(scal):
        job(*one)

    outs = {0: dq_own_ref, 2: dq_far_ref, 1: dq_core_ref.at[0], 3: dq_core_ref.at[1]}
    for slot in range(TEAM):
        for at in range(TILES):
            for h in range(HEADS):
                block = dq_ref[slot * TILES + at, :, h * TILE : (h + 1) * TILE] * FACTOR
                outs[slot][at * TILE : (at + 1) * TILE, h * DIM : (h + 1) * DIM] = block.T.astype(
                    outs[slot].dtype
                )
    kv_own_ref[:ROWS] = dk_ref[0] * FACTOR
    kv_own_ref[ROWS:] = dv_ref[0]
    for d in range(1, TEAM):
        kv_send_refs[d - 1][:ROWS] = (dk_ref[d] * FACTOR).astype(BF16)
        kv_send_refs[d - 1][ROWS:] = dv_ref[d].astype(BF16)


def grads_of(scal, stats, q_slots, s_slots, kvs, turned_q, turned_s):
    smem = pl.BlockSpec(memory_space=pltpu.SMEM)
    vmem = pl.BlockSpec(memory_space=pltpu.VMEM)
    shape = jax.ShapeDtypeStruct
    blocks = TEAM * TILES
    return pl.pallas_call(
        grads_kernel,
        out_shape=(
            shape((ROWS, HEADS * DIM), F32),
            shape((ROWS, HEADS * DIM), F32),
            shape((2, ROWS, HEADS * DIM), BF16),
            shape((2 * ROWS, DIM), F32),
        )
        + (shape((2 * ROWS, DIM), BF16),) * 3,
        in_specs=[smem] + [vmem] * 18,
        out_specs=(vmem,) * 7,
        scratch_shapes=[
            pltpu.VMEM((TEAM, ROWS, 2 * DIM), BF16),
            pltpu.VMEM((TEAM, ROWS, 2 * DIM), BF16),
            pltpu.VMEM((TEAM, DIM, ROWS), BF16),
            pltpu.VMEM((blocks, WIDE, DIM), BF16),
            pltpu.VMEM((blocks, WIDE, DIM), BF16),
            pltpu.VMEM((blocks, DIM, WIDE), BF16),
            pltpu.VMEM((blocks, DIM, WIDE), BF16),
            pltpu.VMEM((blocks, DIM, WIDE), F32),
            pltpu.VMEM((TEAM, ROWS, DIM), F32),
            pltpu.VMEM((TEAM, ROWS, DIM), F32),
        ],
        compiler_params=pltpu.CompilerParams(vmem_limit_bytes=VMEM_LIMIT),
    )(scal, *stats, *q_slots, *s_slots, *kvs, turned_q, turned_s)


def team_slots(value):
    core = permute(value, lambda s: s ^ 1)
    far = permute(value, lambda s: s ^ 2)
    both = permute(far, lambda s: s ^ 1)
    return [value, core, far, both]


def per_device(queries, key_rows, value_rows, positions, latent_ids, latent_acts, latent_dirs):
    kv = jnp.concatenate([key_rows, value_rows], axis=0)
    kvs = [kv] + [permute(kv, lambda s, d=d: s + TEAM * d) for d in range(1, TEAM)]
    q_slots = team_slots(queries)
    s_slots = team_slots(seeds_of(latent_ids, latent_acts, latent_dirs))
    scal = scalars_of(positions)
    stat, turned_q, turned_s = stats_of(scal, q_slots, s_slots, kvs)
    stats = [stat] + [permute(stat, lambda s, e=e: s ^ e) for e in range(1, TEAM)]
    dq_own, dq_far, dq_core, kv_own, *kv_send = grads_of(
        scal, stats, q_slots, s_slots, kvs, turned_q, turned_s
    )
    kv_back = [
        permute(send, lambda s, d=d: s - TEAM * d) for d, send in enumerate(kv_send, 1)
    ]
    dq_near = permute(dq_core, lambda s: s ^ 1).astype(F32)
    dq_back = permute((dq_far + dq_near[1]).astype(BF16), lambda s: s ^ 2)
    grad_q = (dq_own + dq_near[0] + dq_back.astype(F32)).astype(BF16)
    grad_kv = kv_own + sum(part.astype(F32) for part in kv_back)
    grad_k = grad_kv[:ROWS].astype(BF16)
    grad_v = grad_kv[ROWS:].astype(BF16)
    return grad_q, grad_k, grad_v


def solution(mesh):
    in_specs = (
        P(("mp", "ctx"), None),
        P(("mp", "ctx"), None),
        P(("mp", "ctx"), None),
        P("ctx"),
        P(("mp", "ctx"), None),
        P(("mp", "ctx"), None),
        P("mp", None),
    )
    out_specs = (P(("mp", "ctx"), None), P(("mp", "ctx"), None), P(("mp", "ctx"), None))
    return jax.shard_map(
        per_device, mesh=mesh, in_specs=in_specs, out_specs=out_specs, check_vma=False
    )
```

```python
import functools
import math

import jax
import jax.numpy as jnp
from jax import lax
from jax.experimental import pallas as pl
from jax.experimental.pallas import tpu as pltpu
from jax.sharding import PartitionSpec as P

TEAM = 4
ROWS = 384
TILES = 3
TILE = 128
HEADS = 4
DIM = 128
WIDE = HEADS * TILE
WINDOW = 4096
FACTOR = 1.0 / math.sqrt(DIM)
SCALE = FACTOR * math.log2(math.e)
HIDE = -1e30
SMALL_LIMIT = 12 * 1024 * 1024
VMEM_LIMIT = 28 * 1024 * 1024

BF16 = jnp.bfloat16
F32 = jnp.float32


def permute(value, target):
    count = lax.axis_size("ctx")
    return lax.ppermute(value, "ctx", [(s, target(s) % count) for s in range(count)])


def dot(a, b):
    return jnp.dot(a, b, preferred_element_type=F32)


def dot_turned(a, b):
    return lax.dot_general(a, b, (((1,), (1,)), ((), ())), preferred_element_type=F32)


def cost(micros):
    return pl.CostEstimate(
        flops=int(micros * 1e9), bytes_accessed=int(micros * 2e6), transcendentals=0
    )


def seed_kernel(ids_ref, acts_ref, dirs_ref, seed_ref):
    latents = dirs_ref.shape[0]
    rows = ids_ref.shape[1]
    lane = lax.broadcasted_iota(jnp.int32, (latents, rows), 0)
    mixing = jnp.zeros((latents, rows), F32)
    for k in range(ids_ref.shape[0]):
        mixing = mixing + jnp.where(lane == ids_ref[k : k + 1, :], acts_ref[k : k + 1, :], 0.0)
    seed_ref[...] = lax.dot_general(
        mixing,
        dirs_ref[...],
        (((0,), (0,)), ((), ())),
        precision=lax.Precision.HIGHEST,
        preferred_element_type=F32,
    ).astype(BF16)


def seeds_of(latent_ids, latent_acts, latent_dirs):
    return pl.pallas_call(
        seed_kernel,
        out_shape=jax.ShapeDtypeStruct((latent_ids.shape[0], latent_dirs.shape[1]), BF16),
        compiler_params=pltpu.CompilerParams(vmem_limit_bytes=SMALL_LIMIT),
        cost_estimate=cost(4),
    )(latent_ids.T, latent_acts.T, latent_dirs)


class Place:
    def __init__(self, pos_ref):
        ctx = lax.axis_index("ctx")
        tokens = ROWS * lax.axis_size("ctx")
        first = pos_ref[0]
        member = ctx % TEAM
        self.core = member % 2
        self.begin = jnp.where(first < tokens // 2, -first, tokens - first)
        self.wrap = [jnp.where(member + u >= TEAM, 1, 0) for u in range(TEAM)]
        self.slot = [0, 1 + 2 * self.core, 2, 3 - 2 * self.core]

    def pick(self, u, values):
        out = values[0]
        for index in range(1, TEAM):
            out = jnp.where(u == index, values[index], out)
        return out

    def slot_wrap(self, slot):
        if slot == 0:
            return 0
        if slot == 2:
            return self.wrap[2]
        near, away = self.wrap[slot], self.wrap[TEAM - slot]
        return jnp.where(self.core == 0, near, away)

    def slot_offset(self, slot):
        if slot == 0:
            return 0
        member = 2 if slot == 2 else jnp.where(self.core == 0, slot, TEAM - slot)
        return ROWS * member - TEAM * ROWS * self.slot_wrap(slot)


def mask_of(kind, keys):
    name, shift = kind
    key = lax.broadcasted_iota(jnp.int32, (keys, WIDE), 0)
    query = lax.broadcasted_iota(jnp.int32, (keys, WIDE), 1) % TILE
    if name == "causal":
        return key <= query + shift
    return key >= query + shift


def block_jobs(u, t):
    if (u, t) == (0, 0):
        return [(at, 0, (at + 1) * TILE, ("causal", at * TILE)) for at in range(TILES)]
    if (u, t) == (2, 2):
        return [(0, 0, ROWS, None), (1, 0, ROWS, None), (2, 0, ROWS, ("tail", 1))]
    if (u, t) == (3, 2):
        return [(0, TILE, 2 * TILE, ("tail", 1)), (1, 2 * TILE, TILE, ("tail", 1))]
    return [(at, 0, ROWS, None) for at in range(TILES)]


def fill_keys(place, chunks, kv_refs, kx_ref, kt_ref=None):
    lane = lax.broadcasted_iota(jnp.int32, (ROWS, DIM), 1)
    row = lax.broadcasted_iota(jnp.int32, (ROWS, DIM), 0)
    for index, (d, kv_ref) in enumerate(zip(chunks, kv_refs)):
        before = row - TEAM * ROWS * d < place.begin
        kx_ref[index, :, :DIM] = kv_ref[:ROWS]
        kx_ref[index, :, DIM:] = jnp.where((lane == 0) & before, HIDE, 0.0).astype(BF16)
        if kt_ref is not None:
            for j in range(TILES):
                kt_ref[index, :, j * TILE : (j + 1) * TILE] = kv_ref[j * TILE : (j + 1) * TILE].T


def fill_queries(place, slots, q_refs, s_refs, qx_ref, sn_ref):
    lane = lax.broadcasted_iota(jnp.int32, (TILE, DIM), 1)
    row = lax.broadcasted_iota(jnp.int32, (TILE, DIM), 0)
    for index, slot in enumerate(slots):
        for at in range(TILES):
            n = index * TILES + at
            after = row + at * TILE + place.slot_offset(slot) >= place.begin
            flag = jnp.where((lane == 0) & after, 1.0, 0.0).astype(BF16)
            for h in range(HEADS):
                cut = (slice(at * TILE, (at + 1) * TILE), slice(h * DIM, (h + 1) * DIM))
                into = slice(h * TILE, (h + 1) * TILE)
                qx_ref[n, into, :DIM] = q_refs[index][cut]
                qx_ref[n, into, DIM:] = flag
                sn_ref[n, into] = s_refs[index][cut]


SMEM = pl.BlockSpec(memory_space=pltpu.SMEM)
VMEM = pl.BlockSpec(memory_space=pltpu.VMEM)


def stats_kernel(pos_ref, *refs):
    q_refs, s_refs, kv_refs = refs[0:4], refs[4:8], refs[8:12]
    stat_ref = refs[12]
    kx_ref, v_ref, qx_ref, sn_ref, run_ref = refs[13:18]
    place = Place(pos_ref)
    fill_keys(place, range(TEAM), kv_refs, kx_ref)
    fill_queries(place, range(TEAM), q_refs, s_refs, qx_ref, sn_ref)
    for d in range(TEAM):
        v_ref[d] = kv_refs[d][ROWS:]
    for n in range(TEAM * TILES):
        run_ref[n, 0:1] = jnp.full((1, WIDE), 2 * HIDE, F32)
        run_ref[n, 1:3] = jnp.zeros((2, WIDE), F32)

    def job(slot, d, at, j0, keys, kind):
        n = slot * TILES + at
        part = slice(j0, j0 + keys)
        s = dot_turned(kx_ref[d, part], qx_ref[n])
        if kind is not None:
            s = jnp.where(mask_of(kind, keys), s, HIDE)
        dp = dot_turned(v_ref[d, part], sn_ref[n])
        old = run_ref[n, 0:1]
        new = jnp.maximum(old, jnp.max(s, axis=0, keepdims=True))
        p = jnp.exp2((s - new) * SCALE)
        fade = jnp.exp2((old - new) * SCALE)
        run_ref[n, 0:1] = new
        run_ref[n, 1:2] = run_ref[n, 1:2] * fade + jnp.sum(p, axis=0, keepdims=True)
        run_ref[n, 2:3] = run_ref[n, 2:3] * fade + jnp.sum(p * dp, axis=0, keepdims=True)

    def step(k, carry):
        u = jnp.where(k >= 7, 3, jnp.where(k >= 5, 2, jnp.where(k >= 2, 1, 0)))
        t = k - place.pick(u, [-1, 2, 5, 7])
        slot = place.pick(u, place.slot)
        d = t + place.pick(u, place.wrap)
        for at in range(TILES):
            job(slot, d, at, 0, ROWS, None)
        return carry

    lax.fori_loop(0, 9, step, 0)
    for u, t in ((0, 0), (2, 2), (3, 2)):
        for one in block_jobs(u, t):
            job(place.slot[u], t + place.wrap[u], *one)
    for slot in range(TEAM):
        for at in range(TILES):
            n = slot * TILES + at
            total = run_ref[n, 1:2]
            stat_ref[slot, at : at + 1] = run_ref[n, 0:1] * SCALE + jnp.log2(total)
            stat_ref[slot, 3 + at : 4 + at] = run_ref[n, 2:3] / total
        stat_ref[slot, 6:8] = jnp.zeros((2, WIDE), F32)


def stats_of(positions, q_slots, s_slots, kvs):
    blocks = TEAM * TILES
    return pl.pallas_call(
        stats_kernel,
        out_shape=jax.ShapeDtypeStruct((TEAM, 8, WIDE), F32),
        in_specs=[SMEM] + [VMEM] * 12,
        out_specs=VMEM,
        scratch_shapes=[
            pltpu.VMEM((TEAM, ROWS, 2 * DIM), BF16),
            pltpu.VMEM((TEAM, ROWS, DIM), BF16),
            pltpu.VMEM((blocks, WIDE, 2 * DIM), BF16),
            pltpu.VMEM((blocks, WIDE, DIM), BF16),
            pltpu.VMEM((blocks, 8, WIDE), F32),
        ],
        compiler_params=pltpu.CompilerParams(vmem_limit_bytes=VMEM_LIMIT),
        cost_estimate=cost(14),
    )(positions, *q_slots, *s_slots, *kvs)


def fill_stats(slots, stat_refs, row_ref):
    for index, slot in enumerate(slots):
        for at in range(TILES):
            n = index * TILES + at
            sums = [stat_refs[e][slot ^ e, at : at + 1] for e in range(TEAM)]
            deltas = [stat_refs[e][slot ^ e, 3 + at : 4 + at] for e in range(TEAM)]
            top = functools.reduce(jnp.maximum, sums)
            weights = [jnp.exp2(one - top) for one in sums]
            total = sum(weights)
            row_ref[n, 0:1] = top + jnp.log2(total)
            row_ref[n, 1:2] = sum(w * x for w, x in zip(weights, deltas)) / total


def grad_job(refs, n, c, at, j0, keys, kind):
    kx_ref, v_ref, kt_ref, qx_ref, sn_ref, row_ref, dq_ref, dk_ref, dv_ref = refs
    part = slice(j0, j0 + keys)
    p = jnp.exp2(dot_turned(kx_ref[c, part], qx_ref[n]) * SCALE - row_ref[n, 0:1])
    if kind is not None:
        p = jnp.where(mask_of(kind, keys), p, 0.0)
    dp = dot_turned(v_ref[c, part], sn_ref[n]) - row_ref[n, 1:2]
    ds = (p * dp).astype(BF16)
    dv_ref[c, part] += dot(p.astype(BF16), sn_ref[n])
    dk_ref[c, part] += dot(ds, qx_ref[n, :, :DIM])
    dq_ref[n] += dot(kt_ref[c, :, part], ds)


def far_kernel(pos_ref, *refs):
    stat_refs, q_refs, s_refs, kv_refs = refs[0:4], refs[4:8], refs[8:12], refs[12:14]
    near_ref, away_ref = refs[14:16]
    send_refs = refs[16:18]
    work = refs[18:27]
    kx_ref, v_ref, kt_ref, qx_ref, sn_ref, row_ref, dq_ref, dk_ref, dv_ref = work
    place = Place(pos_ref)
    fill_keys(place, (2, 3), kv_refs, kx_ref, kt_ref)
    fill_queries(place, range(TEAM), q_refs, s_refs, qx_ref, sn_ref)
    fill_stats(range(TEAM), stat_refs, row_ref)
    for c in range(2):
        v_ref[c] = kv_refs[c][ROWS:]
    for ref in (dq_ref, dk_ref, dv_ref):
        ref[...] = jnp.zeros_like(ref)

    def block(u, t, c):
        for one in block_jobs(u, t):
            grad_job(work, place.slot[u] * TILES + one[0], c, *one)

    for u in range(TEAM):
        block(u, 2, place.wrap[u])
    for u in range(1, TEAM):
        pl.when(place.wrap[u] == 1)(functools.partial(block, u, 1, 0))
    near_ref[...] = dq_ref[: 2 * TILES]
    away_ref[...] = dq_ref[2 * TILES :]
    for c in range(2):
        send_refs[c][:ROWS] = (dk_ref[c] * FACTOR).astype(BF16)
        send_refs[c][ROWS:] = dv_ref[c].astype(BF16)


def near_kernel(slots, pos_ref, *refs):
    stat_refs, q_refs, s_refs, kv_refs = refs[0:4], refs[4:6], refs[6:8], refs[8:10]
    held_ref = refs[10]
    first = slots[0] != 0
    sums_ref = None if first else refs[11]
    outs = refs[11:14] if first else refs[12:16]
    work = refs[14:23] if first else refs[16:25]
    kx_ref, v_ref, kt_ref, qx_ref, sn_ref, row_ref, dq_ref, dk_ref, dv_ref = work
    place = Place(pos_ref)
    fill_keys(place, (0, 1), kv_refs, kx_ref, kt_ref)
    fill_queries(place, slots, q_refs, s_refs, qx_ref, sn_ref)
    fill_stats(slots, stat_refs, row_ref)
    for c in range(2):
        v_ref[c] = kv_refs[c][ROWS:]
    dq_ref[...] = held_ref[...]
    if first:
        dk_ref[...] = jnp.zeros_like(dk_ref)
        dv_ref[...] = jnp.zeros_like(dv_ref)
    else:
        dk_ref[...] = sums_ref[0:2]
        dv_ref[...] = sums_ref[2:4]

    def block(index, u, t, c):
        for one in block_jobs(u, t):
            grad_job(work, index * TILES + one[0], c, *one)

    for index, slot in enumerate(slots):
        block(index, 0 if slot == 0 else 1, 0, place.slot_wrap(slot))
    for index, slot in enumerate(slots):
        if slot == 0:
            block(index, 0, 1, 1)
        else:
            pl.when(place.slot_wrap(slot) == 0)(functools.partial(block, index, 1, 1, 1))

    for index in range(2):
        for at in range(TILES):
            for h in range(HEADS):
                part = dq_ref[index * TILES + at, :, h * TILE : (h + 1) * TILE] * FACTOR
                outs[index][at * TILE : (at + 1) * TILE, h * DIM : (h + 1) * DIM] = part.T.astype(
                    outs[index].dtype
                )
    if first:
        outs[2][0:2] = dk_ref[...]
        outs[2][2:4] = dv_ref[...]
    else:
        outs[2][:ROWS] = dk_ref[0] * FACTOR
        outs[2][ROWS:] = dv_ref[0]
        outs[3][:ROWS] = (dk_ref[1] * FACTOR).astype(BF16)
        outs[3][ROWS:] = dv_ref[1].astype(BF16)


def grad_scratch(chunks, blocks):
    return [
        pltpu.VMEM((chunks, ROWS, 2 * DIM), BF16),
        pltpu.VMEM((chunks, ROWS, DIM), BF16),
        pltpu.VMEM((chunks, DIM, ROWS), BF16),
        pltpu.VMEM((blocks, WIDE, 2 * DIM), BF16),
        pltpu.VMEM((blocks, WIDE, DIM), BF16),
        pltpu.VMEM((blocks, 8, WIDE), F32),
        pltpu.VMEM((blocks, DIM, WIDE), F32),
        pltpu.VMEM((chunks, ROWS, DIM), F32),
        pltpu.VMEM((chunks, ROWS, DIM), F32),
    ]


def grads_far(positions, stats, q_slots, s_slots, kvs):
    shape = jax.ShapeDtypeStruct
    held = shape((2 * TILES, DIM, WIDE), F32)
    send = shape((2 * ROWS, DIM), BF16)
    return pl.pallas_call(
        far_kernel,
        out_shape=(held, held, send, send),
        in_specs=[SMEM] + [VMEM] * 14,
        out_specs=(VMEM,) * 4,
        scratch_shapes=grad_scratch(2, TEAM * TILES),
        compiler_params=pltpu.CompilerParams(vmem_limit_bytes=VMEM_LIMIT),
        cost_estimate=cost(14),
    )(positions, *stats, *q_slots, *s_slots, *kvs)


def grads_near(positions, slots, stats, q_slots, s_slots, kvs, held, sums=None):
    shape = jax.ShapeDtypeStruct
    outs = (shape((ROWS, HEADS * DIM), F32), shape((ROWS, HEADS * DIM), BF16))
    if sums is None:
        outs += (shape((4, ROWS, DIM), F32),)
        extra = (held,)
    else:
        outs += (shape((2 * ROWS, DIM), F32), shape((2 * ROWS, DIM), BF16))
        extra = (held, sums)
    return pl.pallas_call(
        functools.partial(near_kernel, slots),
        out_shape=outs,
        in_specs=[SMEM] + [VMEM] * (10 + len(extra)),
        out_specs=(VMEM,) * len(outs),
        scratch_shapes=grad_scratch(2, 2 * TILES),
        compiler_params=pltpu.CompilerParams(vmem_limit_bytes=VMEM_LIMIT),
        cost_estimate=cost(8),
    )(positions, *stats, *q_slots, *s_slots, *kvs, *extra)


def team_slots(value):
    core = permute(value, lambda s: s ^ 1)
    far = permute(value, lambda s: s ^ 2)
    both = permute(far, lambda s: s ^ 1)
    return [value, core, far, both]


def per_device(queries, key_rows, value_rows, positions, latent_ids, latent_acts, latent_dirs):
    kv = jnp.concatenate([key_rows, value_rows], axis=0)
    kvs = [kv] + [permute(kv, lambda s, d=d: s + TEAM * d) for d in range(1, TEAM)]
    q = team_slots(queries)
    s = team_slots(seeds_of(latent_ids, latent_acts, latent_dirs))
    stat = stats_of(positions, q, s, kvs)
    stats = [stat] + [permute(stat, lambda s, e=e: s ^ e) for e in range(1, TEAM)]
    held_near, held_away, *sends = grads_far(positions, stats, q, s, kvs[2:])
    back2, back3 = [
        permute(send, lambda s, d=d: s - TEAM * d) for d, send in zip((2, 3), sends)
    ]
    dq_far, dq_both, sums = grads_near(
        positions, (2, 3), stats, q[2:], s[2:], kvs[:2], held_away
    )
    dq_far = dq_far + permute(dq_both, lambda s: s ^ 1).astype(F32)
    dq_far = permute(dq_far.astype(BF16), lambda s: s ^ 2)
    dq_own, dq_core, kv_own, send1 = grads_near(
        positions, (0, 1), stats, q[:2], s[:2], kvs[:2], held_near, sums
    )
    back1 = permute(send1, lambda s: s - TEAM)
    dq_core = permute(dq_core, lambda s: s ^ 1)
    grad_q = (dq_own + dq_core.astype(F32) + dq_far.astype(F32)).astype(BF16)
    grad_kv = kv_own + back1.astype(F32) + back2.astype(F32) + back3.astype(F32)
    return grad_q, grad_kv[:ROWS].astype(BF16), grad_kv[ROWS:].astype(BF16)


def solution(mesh):
    in_specs = (
        P(("mp", "ctx"), None),
        P(("mp", "ctx"), None),
        P(("mp", "ctx"), None),
        P("ctx"),
        P(("mp", "ctx"), None),
        P(("mp", "ctx"), None),
        P("mp", None),
    )
    out_specs = (P(("mp", "ctx"), None), P(("mp", "ctx"), None), P(("mp", "ctx"), None))
    return jax.shard_map(
        per_device, mesh=mesh, in_specs=in_specs, out_specs=out_specs, check_vma=False
    )
```

```python
import functools
import math

import jax
import jax.numpy as jnp
from jax import lax
from jax.experimental import pallas as pl
from jax.experimental.pallas import tpu as pltpu
from jax.sharding import PartitionSpec as P

TEAM = 4
ROWS = 384
TILES = 3
TILE = 128
HEADS = 4
DIM = 128
WIDE = HEADS * TILE
WINDOW = 4096
FACTOR = 1.0 / math.sqrt(DIM)
SCALE = FACTOR * math.log2(math.e)
HIDE = -1e30
VMEM_LIMIT = 28 * 1024 * 1024

KEYS_COST = 60

BF16 = jnp.bfloat16
F32 = jnp.float32


def permute(value, target):
    count = lax.axis_size("ctx")
    return lax.ppermute(value, "ctx", [(s, target(s) % count) for s in range(count)])


def dot(a, b):
    return jnp.dot(a, b, preferred_element_type=F32)


def dot_turned(a, b):
    return lax.dot_general(a, b, (((1,), (1,)), ((), ())), preferred_element_type=F32)


def cost(micros):
    return pl.CostEstimate(
        flops=int(micros * 1e9), bytes_accessed=int(micros * 2e6), transcendentals=0
    )


def seed_kernel(q_ref, ids_ref, acts_ref, dirs_ref, out_ref):
    latents = dirs_ref.shape[0]
    rows = ids_ref.shape[1]
    lane = lax.broadcasted_iota(jnp.int32, (latents, rows), 0)
    mixing = jnp.zeros((latents, rows), F32)
    for k in range(ids_ref.shape[0]):
        mixing = mixing + jnp.where(lane == ids_ref[k : k + 1, :], acts_ref[k : k + 1, :], 0.0)
    out_ref[:rows] = q_ref[...]
    out_ref[rows:] = lax.dot_general(
        mixing,
        dirs_ref[...],
        (((0,), (0,)), ((), ())),
        precision=lax.Precision.HIGHEST,
        preferred_element_type=F32,
    ).astype(BF16)


def with_seeds(queries, latent_ids, latent_acts, latent_dirs):
    return pl.pallas_call(
        seed_kernel,
        out_shape=jax.ShapeDtypeStruct((2 * queries.shape[0], queries.shape[1]), BF16),
        compiler_params=pltpu.CompilerParams(vmem_limit_bytes=VMEM_LIMIT),
        cost_estimate=cost(4),
    )(queries, latent_ids.T, latent_acts.T, latent_dirs)


class Place:
    def __init__(self, pos_ref):
        ctx = lax.axis_index("ctx")
        tokens = ROWS * lax.axis_size("ctx")
        first = pos_ref[0]
        member = ctx % TEAM
        self.core = member % 2
        self.begin = jnp.where(first < tokens // 2, -first, tokens - first)
        self.wrap = [jnp.where(member + u >= TEAM, 1, 0) for u in range(TEAM)]
        self.slot = [0, 1 + 2 * self.core, 2, 3 - 2 * self.core]

    def pick(self, u, values):
        out = values[0]
        for index in range(1, TEAM):
            out = jnp.where(u == index, values[index], out)
        return out

    def slot_wrap(self, slot):
        if slot == 0:
            return 0
        if slot == 2:
            return self.wrap[2]
        near, away = self.wrap[slot], self.wrap[TEAM - slot]
        return jnp.where(self.core == 0, near, away)

    def slot_offset(self, slot):
        if slot == 0:
            return 0
        member = 2 if slot == 2 else jnp.where(self.core == 0, slot, TEAM - slot)
        return ROWS * member - TEAM * ROWS * self.slot_wrap(slot)


def mask_of(kind, keys):
    name, shift = kind
    key = lax.broadcasted_iota(jnp.int32, (keys, WIDE), 0)
    query = lax.broadcasted_iota(jnp.int32, (keys, WIDE), 1) % TILE
    if name == "causal":
        return key <= query + shift
    return key >= query + shift


def block_jobs(u, t):
    if (u, t) == (0, 0):
        return [(at, 0, (at + 1) * TILE, ("causal", at * TILE)) for at in range(TILES)]
    if (u, t) == (2, 2):
        return [(0, 0, ROWS, None), (1, 0, ROWS, None), (2, 0, ROWS, ("tail", 1))]
    if (u, t) == (3, 2):
        return [(0, TILE, 2 * TILE, ("tail", 1)), (1, 2 * TILE, TILE, ("tail", 1))]
    return [(at, 0, ROWS, None) for at in range(TILES)]


def fill_queries(place, slots, qs_refs, qx_ref, sn_ref):
    lane = lax.broadcasted_iota(jnp.int32, (TILE, DIM), 1)
    row = lax.broadcasted_iota(jnp.int32, (TILE, DIM), 0)
    for index, slot in enumerate(slots):
        for at in range(TILES):
            n = index * TILES + at
            after = row + at * TILE + place.slot_offset(slot) >= place.begin
            flag = jnp.where((lane == 0) & after, 1.0, 0.0).astype(BF16)
            for h in range(HEADS):
                cut = (slice(at * TILE, (at + 1) * TILE), slice(h * DIM, (h + 1) * DIM))
                into = slice(h * TILE, (h + 1) * TILE)
                seed_cut = (slice(ROWS + at * TILE, ROWS + (at + 1) * TILE), cut[1])
                qx_ref[n, into, :DIM] = qs_refs[index][cut]
                qx_ref[n, into, DIM:] = flag
                sn_ref[n, into] = qs_refs[index][seed_cut]


SMEM = pl.BlockSpec(memory_space=pltpu.SMEM)
VMEM = pl.BlockSpec(memory_space=pltpu.VMEM)


def keys_kernel(pos_ref, *refs):
    kv_refs = refs[0:4]
    kx_ref, v_ref, kt_ref = refs[4:7]
    place = Place(pos_ref)
    lane = lax.broadcasted_iota(jnp.int32, (ROWS, DIM), 1)
    row = lax.broadcasted_iota(jnp.int32, (ROWS, DIM), 0)
    for d, kv_ref in enumerate(kv_refs):
        before = row - TEAM * ROWS * d < place.begin
        kx_ref[d, :, :DIM] = kv_ref[:ROWS]
        kx_ref[d, :, DIM:] = jnp.where((lane == 0) & before, HIDE, 0.0).astype(BF16)
        v_ref[d] = kv_ref[ROWS:]
        for j in range(TILES):
            kt_ref[d, :, j * TILE : (j + 1) * TILE] = kv_ref[j * TILE : (j + 1) * TILE].T


def keys_of(positions, kvs):
    shape = jax.ShapeDtypeStruct
    return pl.pallas_call(
        keys_kernel,
        out_shape=(
            shape((TEAM, ROWS, 2 * DIM), BF16),
            shape((TEAM, ROWS, DIM), BF16),
            shape((TEAM, DIM, ROWS), BF16),
        ),
        in_specs=[SMEM] + [VMEM] * 4,
        out_specs=(VMEM,) * 3,
        compiler_params=pltpu.CompilerParams(vmem_limit_bytes=VMEM_LIMIT),
        cost_estimate=cost(KEYS_COST),
    )(positions, *kvs)


def stats_kernel(pos_ref, *refs):
    qs_refs = refs[0:4]
    kx_ref, v_ref, stat_ref, qx_ref, sn_ref, run_ref = refs[4:10]
    place = Place(pos_ref)
    fill_queries(place, range(TEAM), qs_refs, qx_ref, sn_ref)
    for n in range(TEAM * TILES):
        run_ref[n, 0:1] = jnp.full((1, WIDE), 2 * HIDE, F32)
        run_ref[n, 1:3] = jnp.zeros((2, WIDE), F32)

    def job(slot, d, at, j0, keys, kind):
        n = slot * TILES + at
        part = slice(j0, j0 + keys)
        s = dot_turned(kx_ref[d, part], qx_ref[n])
        if kind is not None:
            s = jnp.where(mask_of(kind, keys), s, HIDE)
        dp = dot_turned(v_ref[d, part], sn_ref[n])
        old = run_ref[n, 0:1]
        new = jnp.maximum(old, jnp.max(s, axis=0, keepdims=True))
        p = jnp.exp2((s - new) * SCALE)
        fade = jnp.exp2((old - new) * SCALE)
        run_ref[n, 0:1] = new
        run_ref[n, 1:2] = run_ref[n, 1:2] * fade + jnp.sum(p, axis=0, keepdims=True)
        run_ref[n, 2:3] = run_ref[n, 2:3] * fade + jnp.sum(p * dp, axis=0, keepdims=True)

    def step(k, carry):
        u = jnp.where(k >= 7, 3, jnp.where(k >= 5, 2, jnp.where(k >= 2, 1, 0)))
        t = k - place.pick(u, [-1, 2, 5, 7])
        slot = place.pick(u, place.slot)
        d = t + place.pick(u, place.wrap)
        for at in range(TILES):
            job(slot, d, at, 0, ROWS, None)
        return carry

    lax.fori_loop(0, 9, step, 0)
    for u, t in ((0, 0), (2, 2), (3, 2)):
        for one in block_jobs(u, t):
            job(place.slot[u], t + place.wrap[u], *one)
    for slot in range(TEAM):
        for at in range(TILES):
            n = slot * TILES + at
            total = run_ref[n, 1:2]
            stat_ref[slot, at : at + 1] = run_ref[n, 0:1] * SCALE + jnp.log2(total)
            stat_ref[slot, 3 + at : 4 + at] = run_ref[n, 2:3] / total
        stat_ref[slot, 6:8] = jnp.zeros((2, WIDE), F32)


def stats_of(positions, slots, keys, values):
    blocks = TEAM * TILES
    return pl.pallas_call(
        stats_kernel,
        out_shape=jax.ShapeDtypeStruct((TEAM, 8, WIDE), F32),
        in_specs=[SMEM] + [VMEM] * 6,
        out_specs=VMEM,
        scratch_shapes=[
            pltpu.VMEM((blocks, WIDE, 2 * DIM), BF16),
            pltpu.VMEM((blocks, WIDE, DIM), BF16),
            pltpu.VMEM((blocks, 8, WIDE), F32),
        ],
        compiler_params=pltpu.CompilerParams(vmem_limit_bytes=VMEM_LIMIT),
        cost_estimate=cost(14),
    )(positions, *slots, keys, values)


def fill_stats(slots, stat_refs, row_ref):
    for index, slot in enumerate(slots):
        for at in range(TILES):
            n = index * TILES + at
            sums = [stat_refs[e][slot ^ e, at : at + 1] for e in range(TEAM)]
            deltas = [stat_refs[e][slot ^ e, 3 + at : 4 + at] for e in range(TEAM)]
            top = functools.reduce(jnp.maximum, sums)
            weights = [jnp.exp2(one - top) for one in sums]
            total = sum(weights)
            row_ref[n, 0:1] = top + jnp.log2(total)
            row_ref[n, 1:2] = sum(w * x for w, x in zip(weights, deltas)) / total


def grad_job(refs, base, n, d, at, j0, keys, kind):
    kx_ref, v_ref, kt_ref, qx_ref, sn_ref, row_ref, dq_ref, dk_ref, dv_ref = refs
    part = slice(j0, j0 + keys)
    p = jnp.exp2(dot_turned(kx_ref[d, part], qx_ref[n]) * SCALE - row_ref[n, 0:1])
    if kind is not None:
        p = jnp.where(mask_of(kind, keys), p, 0.0)
    dp = dot_turned(v_ref[d, part], sn_ref[n]) - row_ref[n, 1:2]
    ds = (p * dp).astype(BF16)
    dv_ref[d - base, part] += dot(p.astype(BF16), sn_ref[n])
    dk_ref[d - base, part] += dot(ds, qx_ref[n, :, :DIM])
    dq_ref[n] += dot(kt_ref[d, :, part], ds)


def put_sums(ref, dk, dv):
    ref[:ROWS] = (dk * FACTOR).astype(ref.dtype)
    ref[ROWS:] = dv.astype(ref.dtype)


def put_queries(ref, dq_ref, first):
    for at in range(TILES):
        for h in range(HEADS):
            part = dq_ref[first + at, :, h * TILE : (h + 1) * TILE] * FACTOR
            ref[at * TILE : (at + 1) * TILE, h * DIM : (h + 1) * DIM] = part.T.astype(ref.dtype)


def grad_call(body, positions, slots, ds, operands, outs, micros):
    blocks = len(slots) * TILES
    return pl.pallas_call(
        body,
        out_shape=outs,
        in_specs=[SMEM] + [VMEM] * len(operands),
        out_specs=(VMEM,) * len(outs),
        scratch_shapes=[
            pltpu.VMEM((blocks, WIDE, 2 * DIM), BF16),
            pltpu.VMEM((blocks, WIDE, DIM), BF16),
            pltpu.VMEM((blocks, 8, WIDE), F32),
            pltpu.VMEM((blocks, DIM, WIDE), F32),
            pltpu.VMEM((len(ds), ROWS, DIM), F32),
            pltpu.VMEM((len(ds), ROWS, DIM), F32),
        ],
        compiler_params=pltpu.CompilerParams(vmem_limit_bytes=VMEM_LIMIT),
        cost_estimate=cost(micros),
    )(positions, *operands)


HELD = jax.ShapeDtypeStruct((2 * TILES, DIM, WIDE), F32)
SUMS = jax.ShapeDtypeStruct((2, ROWS, DIM), F32)
SEND = jax.ShapeDtypeStruct((2 * ROWS, DIM), BF16)
ALL = tuple(range(TEAM))


def far_kernel(pos_ref, *refs):
    stat_refs, qs_refs, keys = refs[0:4], refs[4:8], refs[8:11]
    near_ref, away_ref = refs[11:13]
    send_refs = refs[13:15]
    work = keys + refs[15:21]
    qx_ref, sn_ref, row_ref, dq_ref, dk_ref, dv_ref = refs[15:21]
    place = Place(pos_ref)
    fill_queries(place, ALL, qs_refs, qx_ref, sn_ref)
    fill_stats(ALL, stat_refs, row_ref)
    for ref in (dq_ref, dk_ref, dv_ref):
        ref[...] = jnp.zeros_like(ref)

    def block(u, t, d):
        for one in block_jobs(u, t):
            grad_job(work, 2, place.slot[u] * TILES + one[0], d, *one)

    for u in ALL:
        block(u, 2, 2 + place.wrap[u])
    for u in ALL[1:]:
        pl.when(place.wrap[u] == 1)(functools.partial(block, u, 1, 2))
    near_ref[...] = dq_ref[: 2 * TILES]
    away_ref[...] = dq_ref[2 * TILES :]
    for c in range(2):
        put_sums(send_refs[c], dk_ref[c], dv_ref[c])


def away_kernel(pos_ref, *refs):
    stat_refs, qs_refs, keys = refs[0:4], refs[4:6], refs[6:9]
    held_ref, dq_far_ref, dq_both_ref, sums0_ref, sums1_ref = refs[9:14]
    work = keys + refs[14:20]
    qx_ref, sn_ref, row_ref, dq_ref, dk_ref, dv_ref = refs[14:20]
    place = Place(pos_ref)
    fill_queries(place, (2, 3), qs_refs, qx_ref, sn_ref)
    fill_stats((2, 3), stat_refs, row_ref)
    dq_ref[...] = held_ref[...]
    dk_ref[...] = jnp.zeros_like(dk_ref)
    dv_ref[...] = jnp.zeros_like(dv_ref)

    def block(index, d):
        for one in block_jobs(1, 0):
            grad_job(work, 0, index * TILES + one[0], d, *one)

    for index in range(2):
        block(index, 1)
    for index in range(2):
        pl.when(place.slot_wrap(2 + index) == 0)(functools.partial(block, index, 0))
    put_queries(dq_far_ref, dq_ref, 0)
    put_queries(dq_both_ref, dq_ref, TILES)
    for d, ref in enumerate((sums0_ref, sums1_ref)):
        ref[0] = dk_ref[d]
        ref[1] = dv_ref[d]


def near_kernel(pos_ref, *refs):
    stat_refs, qs_refs, keys = refs[0:4], refs[4:6], refs[6:9]
    held_ref, sums_ref, out_ref, send_ref = refs[9:13]
    work = keys + refs[13:19]
    qx_ref, sn_ref, row_ref, dq_ref, dk_ref, dv_ref = refs[13:19]
    place = Place(pos_ref)
    fill_queries(place, (0, 1), qs_refs, qx_ref, sn_ref)
    fill_stats((0, 1), stat_refs, row_ref)
    dq_ref[...] = held_ref[...]
    dk_ref[0] = sums_ref[0]
    dv_ref[0] = sums_ref[1]
    for index in range(2):
        for one in block_jobs(1, 0):
            grad_job(work, 1, index * TILES + one[0], 1, *one)
    out_ref[...] = dq_ref[...]
    put_sums(send_ref, dk_ref[0], dv_ref[0])


def own_kernel(pos_ref, *refs):
    stat_refs, qs_refs, keys = refs[0:4], refs[4:6], refs[6:9]
    held_ref, sums_ref, _, dq_own_ref, dq_core_ref, kv_ref = refs[9:15]
    work = keys + refs[15:21]
    qx_ref, sn_ref, row_ref, dq_ref, dk_ref, dv_ref = refs[15:21]
    place = Place(pos_ref)
    fill_queries(place, (0, 1), qs_refs, qx_ref, sn_ref)
    fill_stats((0, 1), stat_refs, row_ref)
    dq_ref[...] = held_ref[...]
    dk_ref[0] = sums_ref[0]
    dv_ref[0] = sums_ref[1]

    def other():
        for one in block_jobs(1, 0):
            grad_job(work, 0, TILES + one[0], 0, *one)

    for one in block_jobs(0, 0):
        grad_job(work, 0, one[0], 0, *one)
    pl.when(place.slot_wrap(1) == 0)(other)
    put_queries(dq_own_ref, dq_ref, 0)
    put_queries(dq_core_ref, dq_ref, TILES)
    put_sums(kv_ref, dk_ref[0], dv_ref[0])


def team_slots(value):
    core = permute(value, lambda s: s ^ 1)
    far = permute(value, lambda s: s ^ 2)
    both = permute(far, lambda s: s ^ 1)
    return [value, core, far, both]


def per_device(queries, key_rows, value_rows, positions, latent_ids, latent_acts, latent_dirs):
    kv = jnp.concatenate([key_rows, value_rows], axis=0)
    kvs = [kv] + [permute(kv, lambda s, d=d: s + TEAM * d) for d in range(1, TEAM)]
    qs = team_slots(with_seeds(queries, latent_ids, latent_acts, latent_dirs))
    keys = keys_of(positions, kvs)
    stat = stats_of(positions, qs, *keys[:2])
    stats = [stat] + [permute(stat, lambda s, e=e: s ^ e) for e in range(1, TEAM)]

    def call(body, slots, ds, extra, outs, micros):
        operands = [*stats, *[qs[slot] for slot in slots], *keys, *extra]
        return grad_call(body, positions, slots, ds, operands, outs, micros)

    shape = jax.ShapeDtypeStruct
    wide, thin = (ROWS, HEADS * DIM), (2 * ROWS, DIM)
    held_near, held_away, send2, send3 = call(
        far_kernel, ALL, (2, 3), (), (HELD, HELD, SEND, SEND), 10
    )
    back3 = permute(send3, lambda s: s - 3 * TEAM)
    back2 = permute(send2, lambda s: s - 2 * TEAM)
    dq_far, dq_both, sums0, sums1 = call(
        away_kernel, (2, 3), (0, 1), (held_away,), (shape(wide, F32), shape(wide, BF16), SUMS, SUMS), 7
    )
    dq_both = permute(dq_both, lambda s: s ^ 1)
    held_near, send1 = call(near_kernel, (0, 1), (1,), (held_near, sums1), (HELD, SEND), 5)
    back1 = permute(send1, lambda s: s - TEAM)
    dq_far = (dq_far + dq_both.astype(F32)).astype(BF16)
    dq_back = permute(dq_far, lambda s: s ^ 2)
    dq_own, dq_core, kv_own = call(
        own_kernel,
        (0, 1),
        (0,),
        (held_near, sums0, dq_far),
        (shape(wide, F32), shape(wide, BF16), shape(thin, F32)),
        5,
    )
    dq_core = permute(dq_core, lambda s: s ^ 1)
    grad_q = (dq_own + dq_core.astype(F32) + dq_back.astype(F32)).astype(BF16)
    grad_kv = kv_own + back1.astype(F32) + back2.astype(F32) + back3.astype(F32)
    return grad_q, grad_kv[:ROWS].astype(BF16), grad_kv[ROWS:].astype(BF16)


def solution(mesh):
    in_specs = (
        P(("mp", "ctx"), None),
        P(("mp", "ctx"), None),
        P(("mp", "ctx"), None),
        P("ctx"),
        P(("mp", "ctx"), None),
        P(("mp", "ctx"), None),
        P("mp", None),
    )
    out_specs = (P(("mp", "ctx"), None), P(("mp", "ctx"), None), P(("mp", "ctx"), None))
    return jax.shard_map(
        per_device, mesh=mesh, in_specs=in_specs, out_specs=out_specs, check_vma=False
    )
```

```python
import functools
import math

import jax
import jax.numpy as jnp
from jax import lax
from jax.experimental import pallas as pl
from jax.experimental.pallas import tpu as pltpu
from jax.sharding import PartitionSpec as P

TEAM = 4
ROWS = 384
TILES = 3
TILE = 128
HEADS = 4
DIM = 128
WIDE = HEADS * TILE
WINDOW = 4096
FACTOR = 1.0 / math.sqrt(DIM)
SCALE = FACTOR * math.log2(math.e)
HIDE = -1e30
VMEM_LIMIT = 28 * 1024 * 1024

EARLY_COST = 60
LATE_COST = 1
GRAD_COST = 5

BF16 = jnp.bfloat16
F32 = jnp.float32


def permute(value, target):
    count = lax.axis_size("ctx")
    return lax.ppermute(value, "ctx", [(s, target(s) % count) for s in range(count)])


def dot(a, b):
    return jnp.dot(a, b, preferred_element_type=F32)


def dot_turned(a, b):
    return lax.dot_general(a, b, (((1,), (1,)), ((), ())), preferred_element_type=F32)


def cost(micros):
    return pl.CostEstimate(
        flops=int(micros * 1e9), bytes_accessed=int(micros * 2e6), transcendentals=0
    )


def seed_kernel(q_ref, ids_ref, acts_ref, dirs_ref, out_ref):
    latents = dirs_ref.shape[0]
    rows = ids_ref.shape[1]
    lane = lax.broadcasted_iota(jnp.int32, (latents, rows), 0)
    mixing = jnp.zeros((latents, rows), F32)
    for k in range(ids_ref.shape[0]):
        mixing = mixing + jnp.where(lane == ids_ref[k : k + 1, :], acts_ref[k : k + 1, :], 0.0)
    out_ref[:rows] = q_ref[...]
    out_ref[rows:] = lax.dot_general(
        mixing,
        dirs_ref[...],
        (((0,), (0,)), ((), ())),
        precision=lax.Precision.HIGHEST,
        preferred_element_type=F32,
    ).astype(BF16)


def with_seeds(queries, latent_ids, latent_acts, latent_dirs):
    return pl.pallas_call(
        seed_kernel,
        out_shape=jax.ShapeDtypeStruct((2 * queries.shape[0], queries.shape[1]), BF16),
        compiler_params=pltpu.CompilerParams(vmem_limit_bytes=VMEM_LIMIT),
        cost_estimate=cost(4),
    )(queries, latent_ids.T, latent_acts.T, latent_dirs)


class Place:
    def __init__(self, pos_ref):
        ctx = lax.axis_index("ctx")
        tokens = ROWS * lax.axis_size("ctx")
        first = pos_ref[0]
        member = ctx % TEAM
        self.core = member % 2
        self.begin = jnp.where(first < tokens // 2, -first, tokens - first)
        self.wrap = [jnp.where(member + u >= TEAM, 1, 0) for u in range(TEAM)]
        self.slot = [0, 1 + 2 * self.core, 2, 3 - 2 * self.core]

    def pick(self, u, values):
        out = values[0]
        for index in range(1, TEAM):
            out = jnp.where(u == index, values[index], out)
        return out

    def slot_wrap(self, slot):
        if slot == 0:
            return 0
        if slot == 2:
            return self.wrap[2]
        near, away = self.wrap[slot], self.wrap[TEAM - slot]
        return jnp.where(self.core == 0, near, away)

    def slot_offset(self, slot):
        if slot == 0:
            return 0
        member = 2 if slot == 2 else jnp.where(self.core == 0, slot, TEAM - slot)
        return ROWS * member - TEAM * ROWS * self.slot_wrap(slot)


def mask_of(kind, keys):
    name, shift = kind
    key = lax.broadcasted_iota(jnp.int32, (keys, WIDE), 0)
    query = lax.broadcasted_iota(jnp.int32, (keys, WIDE), 1) % TILE
    if name == "causal":
        return key <= query + shift
    return key >= query + shift


def block_jobs(u, t):
    if (u, t) == (0, 0):
        return [(at, 0, (at + 1) * TILE, ("causal", at * TILE)) for at in range(TILES)]
    if (u, t) == (2, 2):
        return [(0, 0, ROWS, None), (1, 0, ROWS, None), (2, 0, ROWS, ("tail", 1))]
    if (u, t) == (3, 2):
        return [(0, TILE, 2 * TILE, ("tail", 1)), (1, 2 * TILE, TILE, ("tail", 1))]
    return [(at, 0, ROWS, None) for at in range(TILES)]


def fill_queries(place, slots, qs_refs, qx_ref, sn_ref):
    lane = lax.broadcasted_iota(jnp.int32, (TILE, DIM), 1)
    row = lax.broadcasted_iota(jnp.int32, (TILE, DIM), 0)
    for index, slot in enumerate(slots):
        for at in range(TILES):
            n = index * TILES + at
            after = row + at * TILE + place.slot_offset(slot) >= place.begin
            flag = jnp.where((lane == 0) & after, 1.0, 0.0).astype(BF16)
            for h in range(HEADS):
                cut = (slice(at * TILE, (at + 1) * TILE), slice(h * DIM, (h + 1) * DIM))
                into = slice(h * TILE, (h + 1) * TILE)
                seed_cut = (slice(ROWS + at * TILE, ROWS + (at + 1) * TILE), cut[1])
                qx_ref[n, into, :DIM] = qs_refs[index][cut]
                qx_ref[n, into, DIM:] = flag
                sn_ref[n, into] = qs_refs[index][seed_cut]


SMEM = pl.BlockSpec(memory_space=pltpu.SMEM)
VMEM = pl.BlockSpec(memory_space=pltpu.VMEM)
ANY = pl.BlockSpec(memory_space=pl.ANY)


def keys_kernel(ds, pos_ref, *refs):
    kv_refs = refs[: len(ds)]
    kx_ref, v_ref, kt_ref = refs[-3:]
    place = Place(pos_ref)
    lane = lax.broadcasted_iota(jnp.int32, (ROWS, DIM), 1)
    row = lax.broadcasted_iota(jnp.int32, (ROWS, DIM), 0)
    for c, (d, kv_ref) in enumerate(zip(ds, kv_refs)):
        before = row - TEAM * ROWS * d < place.begin
        kx_ref[c, :, :DIM] = kv_ref[:ROWS]
        kx_ref[c, :, DIM:] = jnp.where((lane == 0) & before, HIDE, 0.0).astype(BF16)
        v_ref[c] = kv_ref[ROWS:]
        for j in range(TILES):
            kt_ref[c, :, j * TILE : (j + 1) * TILE] = kv_ref[j * TILE : (j + 1) * TILE].T


def keys_of(positions, ds, kvs, micros, after=()):
    shape = jax.ShapeDtypeStruct
    return pl.pallas_call(
        functools.partial(keys_kernel, ds),
        out_shape=(
            shape((len(ds), ROWS, 2 * DIM), BF16),
            shape((len(ds), ROWS, DIM), BF16),
            shape((len(ds), DIM, ROWS), BF16),
        ),
        in_specs=[SMEM] + [VMEM] * len(ds) + [ANY] * len(after),
        out_specs=(VMEM,) * 3,
        compiler_params=pltpu.CompilerParams(vmem_limit_bytes=VMEM_LIMIT),
        cost_estimate=cost(micros),
    )(positions, *[kvs[d] for d in ds], *after)


def stat_job(refs, slot, c, at, j0, keys, kind):
    kx_ref, v_ref, qx_ref, sn_ref, run_ref = refs
    n = slot * TILES + at
    part = slice(j0, j0 + keys)
    s = dot_turned(kx_ref[c, part], qx_ref[n])
    if kind is not None:
        s = jnp.where(mask_of(kind, keys), s, HIDE)
    dp = dot_turned(v_ref[c, part], sn_ref[n])
    old = run_ref[n, 0:1]
    new = jnp.maximum(old, jnp.max(s, axis=0, keepdims=True))
    p = jnp.exp2((s - new) * SCALE)
    fade = jnp.exp2((old - new) * SCALE)
    run_ref[n, 0:1] = new
    run_ref[n, 1:2] = run_ref[n, 1:2] * fade + jnp.sum(p, axis=0, keepdims=True)
    run_ref[n, 2:3] = run_ref[n, 2:3] * fade + jnp.sum(p * dp, axis=0, keepdims=True)


def early_kernel(pos_ref, *refs):
    qs_refs = refs[0:4]
    kx_ref, v_ref, qx_ref, sn_ref, run_ref = refs[4:9]
    work = refs[4:9]
    place = Place(pos_ref)
    fill_queries(place, range(TEAM), qs_refs, qx_ref, sn_ref)
    for n in range(TEAM * TILES):
        run_ref[n, 0:1] = jnp.full((1, WIDE), 2 * HIDE, F32)
        run_ref[n, 1:8] = jnp.zeros((7, WIDE), F32)

    def block(u, t):
        for one in block_jobs(u, t):
            stat_job(work, place.slot[u], t + place.wrap[u], *one)

    def step(k, carry):
        u, t = (k + 1) // 2, (k + 1) % 2
        slot = place.pick(u, place.slot)
        d = t + place.pick(u, place.wrap)
        for at in range(TILES):
            stat_job(work, slot, d, at, 0, ROWS, None)
        return carry

    lax.fori_loop(0, 7, step, 0)
    block(0, 0)
    block(0, 2)
    for u in range(1, TEAM):
        pl.when(place.wrap[u] == 0)(functools.partial(block, u, 2))


def late_kernel(pos_ref, *refs):
    kx_ref, v_ref, qx_ref, sn_ref, begun_ref, stat_ref, run_ref = refs
    work = (kx_ref, v_ref, qx_ref, sn_ref, run_ref)
    place = Place(pos_ref)
    run_ref[...] = begun_ref[...]

    def block(u):
        for one in block_jobs(u, 2):
            stat_job(work, place.slot[u], 1, *one)

    for u in range(1, TEAM):
        pl.when(place.wrap[u] == 1)(functools.partial(block, u))
    for slot in range(TEAM):
        for at in range(TILES):
            n = slot * TILES + at
            total = run_ref[n, 1:2]
            stat_ref[slot, at : at + 1] = run_ref[n, 0:1] * SCALE + jnp.log2(total)
            stat_ref[slot, 3 + at : 4 + at] = run_ref[n, 2:3] / total
        stat_ref[slot, 6:8] = jnp.zeros((2, WIDE), F32)


def early_stats(positions, slots, keys, values):
    shape = jax.ShapeDtypeStruct
    blocks = TEAM * TILES
    return pl.pallas_call(
        early_kernel,
        out_shape=(
            shape((blocks, WIDE, 2 * DIM), BF16),
            shape((blocks, WIDE, DIM), BF16),
            shape((blocks, 8, WIDE), F32),
        ),
        in_specs=[SMEM] + [VMEM] * 6,
        out_specs=(VMEM,) * 3,
        compiler_params=pltpu.CompilerParams(vmem_limit_bytes=VMEM_LIMIT),
        cost_estimate=cost(12),
    )(positions, *slots, keys, values)


def late_stats(positions, keys, values, qx, sn, run):
    return pl.pallas_call(
        late_kernel,
        out_shape=jax.ShapeDtypeStruct((TEAM, 8, WIDE), F32),
        in_specs=[SMEM] + [VMEM] * 5,
        out_specs=VMEM,
        scratch_shapes=[pltpu.VMEM((TEAM * TILES, 8, WIDE), F32)],
        compiler_params=pltpu.CompilerParams(vmem_limit_bytes=VMEM_LIMIT),
        cost_estimate=cost(4),
    )(positions, keys, values, qx, sn, run)


def fill_stats(slots, stat_refs, row_ref):
    for index, slot in enumerate(slots):
        for at in range(TILES):
            n = index * TILES + at
            sums = [stat_refs[e][slot ^ e, at : at + 1] for e in range(TEAM)]
            deltas = [stat_refs[e][slot ^ e, 3 + at : 4 + at] for e in range(TEAM)]
            top = functools.reduce(jnp.maximum, sums)
            weights = [jnp.exp2(one - top) for one in sums]
            total = sum(weights)
            row_ref[n, 0:1] = top + jnp.log2(total)
            row_ref[n, 1:2] = sum(w * x for w, x in zip(weights, deltas)) / total


def grad_job(refs, base, first, n, d, at, j0, keys, kind):
    kx_ref, v_ref, kt_ref, qx_ref, sn_ref, row_ref, dq_ref, dk_ref, dv_ref = refs
    part = slice(j0, j0 + keys)
    p = jnp.exp2(dot_turned(kx_ref[d, part], qx_ref[n]) * SCALE - row_ref[n, 0:1])
    if kind is not None:
        p = jnp.where(mask_of(kind, keys), p, 0.0)
    dp = dot_turned(v_ref[d, part], sn_ref[n]) - row_ref[n, 1:2]
    ds = (p * dp).astype(BF16)
    dv_ref[d - base, part] += dot(p.astype(BF16), sn_ref[n])
    dk_ref[d - base, part] += dot(ds, qx_ref[n, :, :DIM])
    dq_ref[n - first] += dot(kt_ref[d, :, part], ds)


def put_sums(ref, dk, dv):
    ref[:ROWS] = (dk * FACTOR).astype(ref.dtype)
    ref[ROWS:] = dv.astype(ref.dtype)


def put_queries(ref, dq_ref, first):
    for at in range(TILES):
        for h in range(HEADS):
            part = dq_ref[first + at, :, h * TILE : (h + 1) * TILE] * FACTOR
            ref[at * TILE : (at + 1) * TILE, h * DIM : (h + 1) * DIM] = part.T.astype(ref.dtype)


def grad_call(body, positions, blocks, shards, operands, outs, micros, refill=0):
    return pl.pallas_call(
        body,
        out_shape=outs,
        in_specs=[SMEM] + [VMEM] * len(operands),
        out_specs=(VMEM,) * len(outs),
        scratch_shapes=[
            pltpu.VMEM((blocks, DIM, WIDE), F32),
            pltpu.VMEM((shards, ROWS, DIM), F32),
            pltpu.VMEM((shards, ROWS, DIM), F32),
        ]
        + [
            pltpu.VMEM((blocks, WIDE, 2 * DIM), BF16),
            pltpu.VMEM((blocks, WIDE, DIM), BF16),
        ]
        * refill,
        compiler_params=pltpu.CompilerParams(vmem_limit_bytes=VMEM_LIMIT),
        cost_estimate=cost(micros),
    )(positions, *operands)


HALF = 2 * TILES
HELD = jax.ShapeDtypeStruct((HALF, DIM, WIDE), F32)
SUMS = jax.ShapeDtypeStruct((2, ROWS, DIM), F32)
SEND = jax.ShapeDtypeStruct((2 * ROWS, DIM), BF16)
ROW = jax.ShapeDtypeStruct((TEAM * TILES, 8, WIDE), F32)


def far_kernel(pos_ref, *refs):
    stat_refs, keys, (qx_ref, sn_ref) = refs[0:4], refs[4:7], refs[7:9]
    near_ref, away_ref, send2_ref, send3_ref, row_ref = refs[9:14]
    dq_ref, dk_ref, dv_ref = sums = refs[14:17]
    work = (*keys, qx_ref, sn_ref, row_ref, *sums)
    place = Place(pos_ref)
    fill_stats(range(TEAM), stat_refs, row_ref)
    for ref in sums:
        ref[...] = jnp.zeros_like(ref)

    def block(u, t, c):
        for one in block_jobs(u, t):
            grad_job(work, 0, 0, place.slot[u] * TILES + one[0], c, *one)

    for u in range(TEAM):
        block(u, 2, place.wrap[u])
    for u in range(1, TEAM):
        pl.when(place.wrap[u] == 1)(functools.partial(block, u, 1, 0))
    near_ref[...] = dq_ref[:HALF]
    away_ref[...] = dq_ref[HALF:]
    put_sums(send2_ref, dk_ref[0], dv_ref[0])
    put_sums(send3_ref, dk_ref[1], dv_ref[1])


def away_kernel(pos_ref, *refs):
    keys, qs_refs, row_ref = refs[0:3], refs[3:5], refs[5]
    held_ref, dq_far_ref, dq_both_ref, sums0_ref, sums1_ref = refs[6:11]
    dq_ref, dk_ref, dv_ref, qx_ref, sn_ref = refs[11:16]
    work = (*keys, qx_ref, sn_ref, row_ref.at[HALF:], dq_ref, dk_ref, dv_ref)
    place = Place(pos_ref)
    fill_queries(place, (2, 3), qs_refs, qx_ref, sn_ref)
    dq_ref[...] = held_ref[...]
    dk_ref[...] = jnp.zeros_like(dk_ref)
    dv_ref[...] = jnp.zeros_like(dv_ref)

    def block(index, d):
        for one in block_jobs(1, 0):
            grad_job(work, 0, 0, index * TILES + one[0], d, *one)

    for index in range(2):
        block(index, 1)
    for index in range(2):
        pl.when(place.slot_wrap(2 + index) == 0)(functools.partial(block, index, 0))
    put_queries(dq_far_ref, dq_ref, 0)
    put_queries(dq_both_ref, dq_ref, TILES)
    for d, ref in enumerate((sums0_ref, sums1_ref)):
        ref[0] = dk_ref[d]
        ref[1] = dv_ref[d]


def near_kernel(pos_ref, *refs):
    keys, qs_refs, row_ref = refs[0:3], refs[3:5], refs[5]
    held_ref, sums_ref, out_ref, send_ref = refs[6:10]
    dq_ref, dk_ref, dv_ref, qx_ref, sn_ref = refs[10:15]
    work = (*keys, qx_ref, sn_ref, row_ref, dq_ref, dk_ref, dv_ref)
    fill_queries(Place(pos_ref), (0, 1), qs_refs, qx_ref, sn_ref)
    dq_ref[...] = held_ref[...]
    dk_ref[0] = sums_ref[0]
    dv_ref[0] = sums_ref[1]
    for index in range(2):
        for one in block_jobs(1, 0):
            grad_job(work, 1, 0, index * TILES + one[0], 1, *one)
    out_ref[...] = dq_ref[...]
    put_sums(send_ref, dk_ref[0], dv_ref[0])


def own_kernel(pos_ref, *refs):
    keys, qs_refs, row_ref = refs[0:3], refs[3:5], refs[5]
    held_ref, sums_ref, _, dq_own_ref, dq_core_ref, kv_ref = refs[6:12]
    dq_ref, dk_ref, dv_ref, qx_ref, sn_ref = refs[12:17]
    work = (*keys, qx_ref, sn_ref, row_ref, dq_ref, dk_ref, dv_ref)
    place = Place(pos_ref)
    fill_queries(place, (0, 1), qs_refs, qx_ref, sn_ref)
    dq_ref[...] = held_ref[...]
    dk_ref[0] = sums_ref[0]
    dv_ref[0] = sums_ref[1]

    def other():
        for one in block_jobs(1, 0):
            grad_job(work, 0, 0, TILES + one[0], 0, *one)

    for one in block_jobs(0, 0):
        grad_job(work, 0, 0, one[0], 0, *one)
    pl.when(place.slot_wrap(1) == 0)(other)
    put_queries(dq_own_ref, dq_ref, 0)
    put_queries(dq_core_ref, dq_ref, TILES)
    put_sums(kv_ref, dk_ref[0], dv_ref[0])


def team_slots(value):
    core = permute(value, lambda s: s ^ 1)
    far = permute(value, lambda s: s ^ 2)
    both = permute(far, lambda s: s ^ 1)
    return [value, core, far, both]


def per_device(queries, key_rows, value_rows, positions, latent_ids, latent_acts, latent_dirs):
    kv = jnp.concatenate([key_rows, value_rows], axis=0)
    kvs = [kv] + [permute(kv, lambda s, d=d: s + TEAM * d) for d in range(1, TEAM)]
    qs = team_slots(with_seeds(queries, latent_ids, latent_acts, latent_dirs))
    early = keys_of(positions, (0, 1, 2), kvs, EARLY_COST)
    qx, sn, run = early_stats(positions, qs, *early[:2])
    late = keys_of(positions, (2, 3), kvs, LATE_COST, (run,))
    stat = late_stats(positions, *late[:2], qx, sn, run)
    stats = [stat] + [permute(stat, lambda s, e=e: s ^ e) for e in range(1, TEAM)]

    shape = jax.ShapeDtypeStruct
    wide, thin = (ROWS, HEADS * DIM), (2 * ROWS, DIM)
    held_near, held_away, send2, send3, rows = grad_call(
        far_kernel,
        positions,
        TEAM * TILES,
        2,
        (*stats, *late, qx, sn),
        (HELD, HELD, SEND, SEND, ROW),
        10,
    )

    def call(body, shards, extra, outs, micros):
        slots = qs[2:] if body is away_kernel else qs[:2]
        operands = (*early, *slots, rows, *extra)
        return grad_call(body, positions, HALF, shards, operands, outs, micros, refill=1)

    back3 = permute(send3, lambda s: s - 3 * TEAM)
    back2 = permute(send2, lambda s: s - 2 * TEAM)
    dq_far, dq_both, sums0, sums1 = call(
        away_kernel, 2, (held_away,), (shape(wide, F32), shape(wide, BF16), SUMS, SUMS), GRAD_COST
    )
    dq_both = permute(dq_both, lambda s: s ^ 1)
    held_near, send1 = call(near_kernel, 1, (held_near, sums1), (HELD, SEND), GRAD_COST)
    back1 = permute(send1, lambda s: s - TEAM)
    dq_far = (dq_far + dq_both.astype(F32)).astype(BF16)
    dq_back = permute(dq_far, lambda s: s ^ 2)
    dq_own, dq_core, kv_own = call(
        own_kernel,
        1,
        (held_near, sums0, dq_far),
        (shape(wide, F32), shape(wide, BF16), shape(thin, F32)),
        GRAD_COST,
    )
    dq_core = permute(dq_core, lambda s: s ^ 1)
    grad_q = (dq_own + dq_core.astype(F32) + dq_back.astype(F32)).astype(BF16)
    grad_kv = kv_own + back1.astype(F32) + back2.astype(F32) + back3.astype(F32)
    return grad_q, grad_kv[:ROWS].astype(BF16), grad_kv[ROWS:].astype(BF16)


def solution(mesh):
    in_specs = (
        P(("mp", "ctx"), None),
        P(("mp", "ctx"), None),
        P(("mp", "ctx"), None),
        P("ctx"),
        P(("mp", "ctx"), None),
        P(("mp", "ctx"), None),
        P("mp", None),
    )
    out_specs = (P(("mp", "ctx"), None), P(("mp", "ctx"), None), P(("mp", "ctx"), None))
    return jax.shard_map(
        per_device, mesh=mesh, in_specs=in_specs, out_specs=out_specs, check_vma=False
    )
```

```python
import functools
import math

import jax
import jax.numpy as jnp
from jax import lax
from jax.experimental import pallas as pl
from jax.experimental.pallas import tpu as pltpu
from jax.sharding import PartitionSpec as P

TEAM = 4
ROWS = 384
TILES = 3
TILE = 128
HEADS = 4
DIM = 128
WIDE = HEADS * TILE
WINDOW = 4096
FACTOR = 1.0 / math.sqrt(DIM)
SCALE = FACTOR * math.log2(math.e)
HIDE = -1e30
VMEM_LIMIT = 28 * 1024 * 1024
SEED_LIMIT = 60 * 1024 * 1024

EARLY_COST = 60
LATE_COST = 1
GRAD_COST = 5
FAR_COST = 5

BF16 = jnp.bfloat16
F32 = jnp.float32


def permute(value, target):
    count = lax.axis_size("ctx")
    return lax.ppermute(value, "ctx", [(s, target(s) % count) for s in range(count)])


def dot(a, b):
    return jnp.dot(a, b, preferred_element_type=F32)


def dot_turned(a, b):
    return lax.dot_general(a, b, (((1,), (1,)), ((), ())), preferred_element_type=F32)


def cost(micros):
    return pl.CostEstimate(
        flops=int(micros * 1e9), bytes_accessed=int(micros * 2e6), transcendentals=0
    )


def seed_kernel(q_ref, ids_ref, acts_ref, dirs_ref, out_ref):
    latents = dirs_ref.shape[0]
    rows = ids_ref.shape[1]
    lane = lax.broadcasted_iota(jnp.int32, (latents, rows), 0)
    mixing = jnp.zeros((latents, rows), F32)
    for k in range(ids_ref.shape[0]):
        mixing = mixing + jnp.where(lane == ids_ref[k : k + 1, :], acts_ref[k : k + 1, :], 0.0)
    out_ref[:rows] = q_ref[...]
    out_ref[rows:] = lax.dot_general(
        mixing,
        dirs_ref[...],
        (((0,), (0,)), ((), ())),
        precision=lax.Precision.HIGHEST,
        preferred_element_type=F32,
    ).astype(BF16)


def with_seeds(queries, latent_ids, latent_acts, latent_dirs):
    return pl.pallas_call(
        seed_kernel,
        out_shape=jax.ShapeDtypeStruct((2 * queries.shape[0], queries.shape[1]), BF16),
        compiler_params=pltpu.CompilerParams(vmem_limit_bytes=SEED_LIMIT),
        cost_estimate=cost(4),
    )(queries, latent_ids.T, latent_acts.T, latent_dirs)


class Place:
    def __init__(self, pos_ref):
        ctx = lax.axis_index("ctx")
        tokens = ROWS * lax.axis_size("ctx")
        first = pos_ref[0]
        member = ctx % TEAM
        self.core = member % 2
        self.begin = jnp.where(first < tokens // 2, -first, tokens - first)
        self.wrap = [jnp.where(member + u >= TEAM, 1, 0) for u in range(TEAM)]
        self.slot = [0, 1 + 2 * self.core, 2, 3 - 2 * self.core]

    def pick(self, u, values):
        out = values[0]
        for index in range(1, TEAM):
            out = jnp.where(u == index, values[index], out)
        return out

    def slot_wrap(self, slot):
        if slot == 0:
            return 0
        if slot == 2:
            return self.wrap[2]
        near, away = self.wrap[slot], self.wrap[TEAM - slot]
        return jnp.where(self.core == 0, near, away)

    def slot_offset(self, slot):
        if slot == 0:
            return 0
        member = 2 if slot == 2 else jnp.where(self.core == 0, slot, TEAM - slot)
        return ROWS * member - TEAM * ROWS * self.slot_wrap(slot)


def mask_of(kind, keys):
    name, shift = kind
    key = lax.broadcasted_iota(jnp.int32, (keys, WIDE), 0)
    query = lax.broadcasted_iota(jnp.int32, (keys, WIDE), 1) % TILE
    if name == "causal":
        return key <= query + shift
    return key >= query + shift


def block_jobs(u, t):
    if (u, t) == (0, 0):
        return [(at, 0, (at + 1) * TILE, ("causal", at * TILE)) for at in range(TILES)]
    if (u, t) == (2, 2):
        return [(0, 0, ROWS, None), (1, 0, ROWS, None), (2, 0, ROWS, ("tail", 1))]
    if (u, t) == (3, 2):
        return [(0, TILE, 2 * TILE, ("tail", 1)), (1, 2 * TILE, TILE, ("tail", 1))]
    return [(at, 0, ROWS, None) for at in range(TILES)]


def fill_queries(place, slots, qs_refs, qx_ref, sn_ref):
    lane = lax.broadcasted_iota(jnp.int32, (TILE, DIM), 1)
    row = lax.broadcasted_iota(jnp.int32, (TILE, DIM), 0)
    for index, slot in enumerate(slots):
        for at in range(TILES):
            n = index * TILES + at
            after = row + at * TILE + place.slot_offset(slot) >= place.begin
            flag = jnp.where((lane == 0) & after, 1.0, 0.0).astype(BF16)
            for h in range(HEADS):
                cut = (slice(at * TILE, (at + 1) * TILE), slice(h * DIM, (h + 1) * DIM))
                into = slice(h * TILE, (h + 1) * TILE)
                seed_cut = (slice(ROWS + at * TILE, ROWS + (at + 1) * TILE), cut[1])
                qx_ref[n, into, :DIM] = qs_refs[index][cut]
                qx_ref[n, into, DIM:] = flag
                sn_ref[n, into] = qs_refs[index][seed_cut]


SMEM = pl.BlockSpec(memory_space=pltpu.SMEM)
VMEM = pl.BlockSpec(memory_space=pltpu.VMEM)
ANY = pl.BlockSpec(memory_space=pl.ANY)


def keys_kernel(ds, pos_ref, *refs):
    kv_refs = refs[: len(ds)]
    kx_ref, v_ref, kt_ref = refs[-3:]
    place = Place(pos_ref)
    lane = lax.broadcasted_iota(jnp.int32, (ROWS, DIM), 1)
    row = lax.broadcasted_iota(jnp.int32, (ROWS, DIM), 0)
    for c, (d, kv_ref) in enumerate(zip(ds, kv_refs)):
        before = row - TEAM * ROWS * d < place.begin
        kx_ref[c, :, :DIM] = kv_ref[:ROWS]
        kx_ref[c, :, DIM:] = jnp.where((lane == 0) & before, HIDE, 0.0).astype(BF16)
        v_ref[c] = kv_ref[ROWS:]
        for j in range(TILES):
            kt_ref[c, :, j * TILE : (j + 1) * TILE] = kv_ref[j * TILE : (j + 1) * TILE].T


def keys_of(positions, ds, kvs, micros, after=()):
    shape = jax.ShapeDtypeStruct
    return pl.pallas_call(
        functools.partial(keys_kernel, ds),
        out_shape=(
            shape((len(ds), ROWS, 2 * DIM), BF16),
            shape((len(ds), ROWS, DIM), BF16),
            shape((len(ds), DIM, ROWS), BF16),
        ),
        in_specs=[SMEM] + [VMEM] * len(ds) + [ANY] * len(after),
        out_specs=(VMEM,) * 3,
        compiler_params=pltpu.CompilerParams(vmem_limit_bytes=VMEM_LIMIT),
        cost_estimate=cost(micros),
    )(positions, *[kvs[d] for d in ds], *after)


def stat_job(refs, slot, c, at, j0, keys, kind):
    kx_ref, v_ref, qx_ref, sn_ref, run_ref = refs
    n = slot * TILES + at
    part = slice(j0, j0 + keys)
    s = dot_turned(kx_ref[c, part], qx_ref[n])
    if kind is not None:
        s = jnp.where(mask_of(kind, keys), s, HIDE)
    dp = dot_turned(v_ref[c, part], sn_ref[n])
    old = run_ref[n, 0:1]
    new = jnp.maximum(old, jnp.max(s, axis=0, keepdims=True))
    p = jnp.exp2((s - new) * SCALE)
    fade = jnp.exp2((old - new) * SCALE)
    run_ref[n, 0:1] = new
    run_ref[n, 1:2] = run_ref[n, 1:2] * fade + jnp.sum(p, axis=0, keepdims=True)
    run_ref[n, 2:3] = run_ref[n, 2:3] * fade + jnp.sum(p * dp, axis=0, keepdims=True)


def early_kernel(pos_ref, *refs):
    qs_refs = refs[0:4]
    kx_ref, v_ref, qx_ref, sn_ref, run_ref = refs[4:9]
    work = refs[4:9]
    place = Place(pos_ref)
    fill_queries(place, range(TEAM), qs_refs, qx_ref, sn_ref)
    for n in range(TEAM * TILES):
        run_ref[n, 0:1] = jnp.full((1, WIDE), 2 * HIDE, F32)
        run_ref[n, 1:8] = jnp.zeros((7, WIDE), F32)

    def block(u, t):
        for one in block_jobs(u, t):
            stat_job(work, place.slot[u], t + place.wrap[u], *one)

    def step(k, carry):
        u, t = (k + 1) // 2, (k + 1) % 2
        slot = place.pick(u, place.slot)
        d = t + place.pick(u, place.wrap)
        for at in range(TILES):
            stat_job(work, slot, d, at, 0, ROWS, None)
        return carry

    lax.fori_loop(0, 7, step, 0)
    block(0, 0)
    block(0, 2)
    for u in range(1, TEAM):
        pl.when(place.wrap[u] == 0)(functools.partial(block, u, 2))


def late_kernel(pos_ref, *refs):
    kx_ref, v_ref, qx_ref, sn_ref, begun_ref, stat_ref, run_ref = refs
    work = (kx_ref, v_ref, qx_ref, sn_ref, run_ref)
    place = Place(pos_ref)
    run_ref[...] = begun_ref[...]

    def block(u):
        for one in block_jobs(u, 2):
            stat_job(work, place.slot[u], 1, *one)

    for u in range(1, TEAM):
        pl.when(place.wrap[u] == 1)(functools.partial(block, u))
    for slot in range(TEAM):
        for at in range(TILES):
            n = slot * TILES + at
            total = run_ref[n, 1:2]
            stat_ref[slot, at : at + 1] = run_ref[n, 0:1] * SCALE + jnp.log2(total)
            stat_ref[slot, 3 + at : 4 + at] = run_ref[n, 2:3] / total
        stat_ref[slot, 6:8] = jnp.zeros((2, WIDE), F32)


def early_stats(positions, slots, keys, values):
    shape = jax.ShapeDtypeStruct
    blocks = TEAM * TILES
    return pl.pallas_call(
        early_kernel,
        out_shape=(
            shape((blocks, WIDE, 2 * DIM), BF16),
            shape((blocks, WIDE, DIM), BF16),
            shape((blocks, 8, WIDE), F32),
        ),
        in_specs=[SMEM] + [VMEM] * 6,
        out_specs=(VMEM,) * 3,
        compiler_params=pltpu.CompilerParams(vmem_limit_bytes=VMEM_LIMIT),
        cost_estimate=cost(12),
    )(positions, *slots, keys, values)


def late_stats(positions, keys, values, qx, sn, run):
    return pl.pallas_call(
        late_kernel,
        out_shape=jax.ShapeDtypeStruct((TEAM, 8, WIDE), F32),
        in_specs=[SMEM] + [VMEM] * 5,
        out_specs=VMEM,
        scratch_shapes=[pltpu.VMEM((TEAM * TILES, 8, WIDE), F32)],
        compiler_params=pltpu.CompilerParams(vmem_limit_bytes=VMEM_LIMIT),
        cost_estimate=cost(4),
    )(positions, keys, values, qx, sn, run)


def fill_stats(slots, stat_refs, row_ref):
    for index, slot in enumerate(slots):
        for at in range(TILES):
            n = index * TILES + at
            sums = [stat_refs[e][slot ^ e, at : at + 1] for e in range(TEAM)]
            deltas = [stat_refs[e][slot ^ e, 3 + at : 4 + at] for e in range(TEAM)]
            top = functools.reduce(jnp.maximum, sums)
            weights = [jnp.exp2(one - top) for one in sums]
            total = sum(weights)
            row_ref[n, 0:1] = top + jnp.log2(total)
            row_ref[n, 1:2] = sum(w * x for w, x in zip(weights, deltas)) / total


def grad_job(refs, base, first, n, d, at, j0, keys, kind):
    kx_ref, v_ref, kt_ref, qx_ref, sn_ref, row_ref, dq_ref, dk_ref, dv_ref = refs
    part = slice(j0, j0 + keys)
    p = jnp.exp2(dot_turned(kx_ref[d, part], qx_ref[n]) * SCALE - row_ref[n, 0:1])
    if kind is not None:
        p = jnp.where(mask_of(kind, keys), p, 0.0)
    dp = dot_turned(v_ref[d, part], sn_ref[n]) - row_ref[n, 1:2]
    ds = (p * dp).astype(BF16)
    dv_ref[d - base, part] += dot(p.astype(BF16), sn_ref[n])
    dk_ref[d - base, part] += dot(ds, qx_ref[n, :, :DIM])
    dq_ref[n - first] += dot(kt_ref[d, :, part], ds)


def put_sums(ref, dk, dv):
    ref[:ROWS] = (dk * FACTOR).astype(ref.dtype)
    ref[ROWS:] = dv.astype(ref.dtype)


def put_queries(ref, dq_ref, first):
    for at in range(TILES):
        for h in range(HEADS):
            part = dq_ref[first + at, :, h * TILE : (h + 1) * TILE] * FACTOR
            ref[at * TILE : (at + 1) * TILE, h * DIM : (h + 1) * DIM] = part.T.astype(ref.dtype)


def grad_call(body, positions, blocks, shards, operands, outs, micros, refill=0):
    return pl.pallas_call(
        body,
        out_shape=outs,
        in_specs=[SMEM] + [VMEM] * len(operands),
        out_specs=(VMEM,) * len(outs),
        scratch_shapes=[
            pltpu.VMEM((blocks, DIM, WIDE), F32),
            pltpu.VMEM((shards, ROWS, DIM), F32),
            pltpu.VMEM((shards, ROWS, DIM), F32),
        ]
        + [
            pltpu.VMEM((blocks, WIDE, 2 * DIM), BF16),
            pltpu.VMEM((blocks, WIDE, DIM), BF16),
        ]
        * refill,
        compiler_params=pltpu.CompilerParams(vmem_limit_bytes=VMEM_LIMIT),
        cost_estimate=cost(micros),
    )(positions, *operands)


HALF = 2 * TILES
HELD = jax.ShapeDtypeStruct((HALF, DIM, WIDE), F32)
SUMS = jax.ShapeDtypeStruct((2, ROWS, DIM), F32)
SEND = jax.ShapeDtypeStruct((2 * ROWS, DIM), BF16)
ROW = jax.ShapeDtypeStruct((TEAM * TILES, 8, WIDE), F32)


def farthest_kernel(pos_ref, *refs):
    stat_refs, keys, (qx_ref, sn_ref) = refs[0:4], refs[4:7], refs[7:9]
    send_ref, row_ref, dq_ref = refs[9:12]
    dk_ref, dv_ref = refs[12:14]
    work = (*keys, qx_ref, sn_ref, row_ref, dq_ref, dk_ref, dv_ref)
    place = Place(pos_ref)
    fill_stats(range(TEAM), stat_refs, row_ref)
    for ref in (dq_ref, dk_ref, dv_ref):
        ref[...] = jnp.zeros_like(ref)

    def block(u):
        for one in block_jobs(u, 2):
            grad_job(work, 1, 0, place.slot[u] * TILES + one[0], 1, *one)

    for u in range(1, TEAM):
        pl.when(place.wrap[u] == 1)(functools.partial(block, u))
    put_sums(send_ref, dk_ref[0], dv_ref[0])


def far_kernel(pos_ref, *refs):
    keys, (qx_ref, sn_ref, row_ref, held_ref) = refs[0:3], refs[3:7]
    near_ref, away_ref, send_ref = refs[7:10]
    dq_ref, dk_ref, dv_ref = refs[10:13]
    work = (*keys, qx_ref, sn_ref, row_ref, dq_ref, dk_ref, dv_ref)
    place = Place(pos_ref)
    dq_ref[...] = held_ref[...]
    dk_ref[...] = jnp.zeros_like(dk_ref)
    dv_ref[...] = jnp.zeros_like(dv_ref)

    def block(u, t):
        for one in block_jobs(u, t):
            grad_job(work, 0, 0, place.slot[u] * TILES + one[0], 0, *one)

    block(0, 2)
    for u in range(1, TEAM):
        pl.when(place.wrap[u] == 0)(functools.partial(block, u, 2))
        pl.when(place.wrap[u] == 1)(functools.partial(block, u, 1))
    near_ref[...] = dq_ref[:HALF]
    away_ref[...] = dq_ref[HALF:]
    put_sums(send_ref, dk_ref[0], dv_ref[0])


def away_kernel(pos_ref, *refs):
    keys, qs_refs, row_ref = refs[0:3], refs[3:5], refs[5]
    held_ref, dq_far_ref, dq_both_ref, sums0_ref, sums1_ref = refs[6:11]
    dq_ref, dk_ref, dv_ref, qx_ref, sn_ref = refs[11:16]
    work = (*keys, qx_ref, sn_ref, row_ref.at[HALF:], dq_ref, dk_ref, dv_ref)
    place = Place(pos_ref)
    fill_queries(place, (2, 3), qs_refs, qx_ref, sn_ref)
    dq_ref[...] = held_ref[...]
    dk_ref[...] = jnp.zeros_like(dk_ref)
    dv_ref[...] = jnp.zeros_like(dv_ref)

    def block(index, d):
        for one in block_jobs(1, 0):
            grad_job(work, 0, 0, index * TILES + one[0], d, *one)

    for index in range(2):
        block(index, 1)
    for index in range(2):
        pl.when(place.slot_wrap(2 + index) == 0)(functools.partial(block, index, 0))
    put_queries(dq_far_ref, dq_ref, 0)
    put_queries(dq_both_ref, dq_ref, TILES)
    for d, ref in enumerate((sums0_ref, sums1_ref)):
        ref[0] = dk_ref[d]
        ref[1] = dv_ref[d]


def near_kernel(pos_ref, *refs):
    keys, qs_refs, row_ref = refs[0:3], refs[3:5], refs[5]
    held_ref, sums_ref, _, out_ref, send_ref = refs[6:11]
    dq_ref, dk_ref, dv_ref, qx_ref, sn_ref = refs[11:16]
    work = (*keys, qx_ref, sn_ref, row_ref, dq_ref, dk_ref, dv_ref)
    fill_queries(Place(pos_ref), (0, 1), qs_refs, qx_ref, sn_ref)
    dq_ref[...] = held_ref[...]
    dk_ref[0] = sums_ref[0]
    dv_ref[0] = sums_ref[1]
    for index in range(2):
        for one in block_jobs(1, 0):
            grad_job(work, 1, 0, index * TILES + one[0], 1, *one)
    out_ref[...] = dq_ref[...]
    put_sums(send_ref, dk_ref[0], dv_ref[0])


def own_kernel(pos_ref, *refs):
    keys, qs_refs, row_ref = refs[0:3], refs[3:5], refs[5]
    held_ref, sums_ref, _, dq_own_ref, dq_core_ref, kv_ref = refs[6:12]
    dq_ref, dk_ref, dv_ref, qx_ref, sn_ref = refs[12:17]
    work = (*keys, qx_ref, sn_ref, row_ref, dq_ref, dk_ref, dv_ref)
    place = Place(pos_ref)
    fill_queries(place, (0, 1), qs_refs, qx_ref, sn_ref)
    dq_ref[...] = held_ref[...]
    dk_ref[0] = sums_ref[0]
    dv_ref[0] = sums_ref[1]

    def other():
        for one in block_jobs(1, 0):
            grad_job(work, 0, 0, TILES + one[0], 0, *one)

    for one in block_jobs(0, 0):
        grad_job(work, 0, 0, one[0], 0, *one)
    pl.when(place.slot_wrap(1) == 0)(other)
    put_queries(dq_own_ref, dq_ref, 0)
    put_queries(dq_core_ref, dq_ref, TILES)
    put_sums(kv_ref, dk_ref[0], dv_ref[0])


def team_slots(value):
    core = permute(value, lambda s: s ^ 1)
    far = permute(value, lambda s: s ^ 2)
    both = permute(far, lambda s: s ^ 1)
    return [value, core, far, both]


def per_device(queries, key_rows, value_rows, positions, latent_ids, latent_acts, latent_dirs):
    kv = jnp.concatenate([key_rows, value_rows], axis=0)
    kvs = [kv] + [permute(kv, lambda s, d=d: s + TEAM * d) for d in (1, 2)]
    kvs.append(permute(kvs[2], lambda s: s + TEAM))
    qs = team_slots(with_seeds(queries, latent_ids, latent_acts, latent_dirs))
    early = keys_of(positions, (0, 1, 2), kvs, EARLY_COST)
    qx, sn, run = early_stats(positions, qs, *early[:2])
    late = keys_of(positions, (2, 3), kvs, LATE_COST, (run,))
    stat = late_stats(positions, *late[:2], qx, sn, run)
    stats = [stat] + [permute(stat, lambda s, e=e: s ^ e) for e in range(1, TEAM)]

    shape = jax.ShapeDtypeStruct
    wide, thin = (ROWS, HEADS * DIM), (2 * ROWS, DIM)
    send3, rows, held = pl.pallas_call(
        farthest_kernel,
        out_shape=(SEND, ROW, shape((TEAM * TILES, DIM, WIDE), F32)),
        in_specs=[SMEM] + [VMEM] * 9,
        out_specs=(VMEM,) * 3,
        scratch_shapes=[pltpu.VMEM((1, ROWS, DIM), F32)] * 2,
        compiler_params=pltpu.CompilerParams(vmem_limit_bytes=VMEM_LIMIT),
        cost_estimate=cost(FAR_COST),
    )(positions, *stats, *late, qx, sn)
    held_near, held_away, send2 = grad_call(
        far_kernel,
        positions,
        TEAM * TILES,
        1,
        (*late, qx, sn, rows, held),
        (HELD, HELD, shape(thin, F32)),
        FAR_COST,
    )

    def call(body, shards, extra, outs, micros):
        slots = qs[2:] if body is away_kernel else qs[:2]
        operands = (*early, *slots, rows, *extra)
        return grad_call(body, positions, HALF, shards, operands, outs, micros, refill=1)

    send3 = permute(send3, lambda s: s - TEAM)
    send2 = (send2 + send3.astype(F32)).astype(BF16)
    back2 = permute(send2, lambda s: s - 2 * TEAM)
    dq_far, dq_both, sums0, sums1 = call(
        away_kernel, 2, (held_away,), (shape(wide, F32), shape(wide, BF16), SUMS, SUMS), GRAD_COST
    )
    dq_both = permute(dq_both, lambda s: s ^ 1)
    held_near, send1 = call(near_kernel, 1, (held_near, sums1, send2), (HELD, SEND), GRAD_COST)
    back1 = permute(send1, lambda s: s - TEAM)
    dq_far = (dq_far + dq_both.astype(F32)).astype(BF16)
    dq_back = permute(dq_far, lambda s: s ^ 2)
    dq_own, dq_core, kv_own = call(
        own_kernel,
        1,
        (held_near, sums0, dq_far),
        (shape(wide, F32), shape(wide, BF16), shape(thin, F32)),
        GRAD_COST,
    )
    dq_core = permute(dq_core, lambda s: s ^ 1)
    grad_q = (dq_own + dq_core.astype(F32) + dq_back.astype(F32)).astype(BF16)
    grad_kv = kv_own + back1.astype(F32) + back2.astype(F32)
    return grad_q, grad_kv[:ROWS].astype(BF16), grad_kv[ROWS:].astype(BF16)


def solution(mesh):
    in_specs = (
        P(("mp", "ctx"), None),
        P(("mp", "ctx"), None),
        P(("mp", "ctx"), None),
        P("ctx"),
        P(("mp", "ctx"), None),
        P(("mp", "ctx"), None),
        P("mp", None),
    )
    out_specs = (P(("mp", "ctx"), None), P(("mp", "ctx"), None), P(("mp", "ctx"), None))
    return jax.shard_map(
        per_device, mesh=mesh, in_specs=in_specs, out_specs=out_specs, check_vma=False
    )
```

```python
import functools
import math

import jax
import jax.numpy as jnp
from jax import lax
from jax.experimental import pallas as pl
from jax.experimental.pallas import tpu as pltpu
from jax.sharding import PartitionSpec as P

TEAM = 4
ROWS = 384
TILES = 3
TILE = 128
HEADS = 4
DIM = 128
WIDE = HEADS * TILE
WINDOW = 4096
FACTOR = 1.0 / math.sqrt(DIM)
SCALE = FACTOR * math.log2(math.e)
HIDE = -1e30
VMEM_LIMIT = 28 * 1024 * 1024
SEED_LIMIT = 60 * 1024 * 1024

EARLY_COST = 60
LATE_COST = 1
GRAD_COST = 5
FAR_COST = 5

BF16 = jnp.bfloat16
F32 = jnp.float32


def permute(value, target):
    count = lax.axis_size("ctx")
    return lax.ppermute(value, "ctx", [(s, target(s) % count) for s in range(count)])


def dot(a, b):
    return jnp.dot(a, b, preferred_element_type=F32)


def dot_turned(a, b):
    return lax.dot_general(a, b, (((1,), (1,)), ((), ())), preferred_element_type=F32)


def cost(micros):
    return pl.CostEstimate(
        flops=int(micros * 1e9), bytes_accessed=int(micros * 2e6), transcendentals=0
    )


def halves(value):
    high = value.astype(BF16)
    return high, (value - high.astype(F32)).astype(BF16)


def seed_kernel(q_ref, ids_ref, acts_ref, dirs_ref, out_ref, table_ref, sems):
    latents = dirs_ref.shape[0]
    rows = ids_ref.shape[1]
    fetch = pltpu.make_async_copy(dirs_ref, table_ref, sems.at[0])
    fetch.start()
    place = pltpu.make_async_copy(q_ref, out_ref.at[:rows], sems.at[1])
    place.start()
    lane = lax.broadcasted_iota(jnp.int32, (latents, rows), 0)
    mixing = jnp.zeros((latents, rows), F32)
    for k in range(ids_ref.shape[0]):
        mixing = mixing + jnp.where(lane == ids_ref[k : k + 1, :], acts_ref[k : k + 1, :], 0.0)
    mix_high, mix_low = halves(mixing.T)
    fetch.wait()
    dir_high, dir_low = halves(table_ref[...])
    seeds = dot(mix_high, dir_low) + dot(mix_low, dir_high) + dot(mix_high, dir_high)
    out_ref[rows:] = seeds.astype(BF16)
    place.wait()


def with_seeds(queries, latent_ids, latent_acts, latent_dirs):
    vmem = pl.BlockSpec(memory_space=pltpu.VMEM)
    hbm = pl.BlockSpec(memory_space=pl.ANY)
    return pl.pallas_call(
        seed_kernel,
        out_shape=jax.ShapeDtypeStruct((2 * queries.shape[0], queries.shape[1]), BF16),
        in_specs=[hbm, vmem, vmem, hbm],
        out_specs=vmem,
        scratch_shapes=[
            pltpu.VMEM(latent_dirs.shape, F32),
            pltpu.SemaphoreType.DMA((2,)),
        ],
        compiler_params=pltpu.CompilerParams(vmem_limit_bytes=SEED_LIMIT),
        cost_estimate=cost(4),
    )(queries, latent_ids.T, latent_acts.T, latent_dirs)


class Place:
    def __init__(self, pos_ref):
        ctx = lax.axis_index("ctx")
        tokens = ROWS * lax.axis_size("ctx")
        first = pos_ref[0]
        member = ctx % TEAM
        self.core = member % 2
        self.begin = jnp.where(first < tokens // 2, -first, tokens - first)
        self.wrap = [jnp.where(member + u >= TEAM, 1, 0) for u in range(TEAM)]
        self.slot = [0, 1 + 2 * self.core, 2, 3 - 2 * self.core]

    def pick(self, u, values):
        out = values[0]
        for index in range(1, TEAM):
            out = jnp.where(u == index, values[index], out)
        return out

    def slot_wrap(self, slot):
        if slot == 0:
            return 0
        if slot == 2:
            return self.wrap[2]
        near, away = self.wrap[slot], self.wrap[TEAM - slot]
        return jnp.where(self.core == 0, near, away)

    def slot_offset(self, slot):
        if slot == 0:
            return 0
        member = 2 if slot == 2 else jnp.where(self.core == 0, slot, TEAM - slot)
        return ROWS * member - TEAM * ROWS * self.slot_wrap(slot)


def mask_of(kind, keys):
    name, shift = kind
    key = lax.broadcasted_iota(jnp.int32, (keys, WIDE), 0)
    query = lax.broadcasted_iota(jnp.int32, (keys, WIDE), 1) % TILE
    if name == "causal":
        return key <= query + shift
    return key >= query + shift


def block_jobs(u, t):
    if (u, t) == (0, 0):
        return [(at, 0, (at + 1) * TILE, ("causal", at * TILE)) for at in range(TILES)]
    if (u, t) == (2, 2):
        return [(0, 0, ROWS, None), (1, 0, ROWS, None), (2, 0, ROWS, ("tail", 1))]
    if (u, t) == (3, 2):
        return [(0, TILE, 2 * TILE, ("tail", 1)), (1, 2 * TILE, TILE, ("tail", 1))]
    return [(at, 0, ROWS, None) for at in range(TILES)]


def fill_queries(place, slots, qs_refs, qx_ref, sn_ref):
    lane = lax.broadcasted_iota(jnp.int32, (TILE, DIM), 1)
    row = lax.broadcasted_iota(jnp.int32, (TILE, DIM), 0)
    for index, slot in enumerate(slots):
        for at in range(TILES):
            n = index * TILES + at
            after = row + at * TILE + place.slot_offset(slot) >= place.begin
            flag = jnp.where((lane == 0) & after, 1.0, 0.0).astype(BF16)
            for h in range(HEADS):
                cut = (slice(at * TILE, (at + 1) * TILE), slice(h * DIM, (h + 1) * DIM))
                into = slice(h * TILE, (h + 1) * TILE)
                seed_cut = (slice(ROWS + at * TILE, ROWS + (at + 1) * TILE), cut[1])
                qx_ref[n, into, :DIM] = qs_refs[index][cut]
                qx_ref[n, into, DIM:] = flag
                sn_ref[n, into] = qs_refs[index][seed_cut]


SMEM = pl.BlockSpec(memory_space=pltpu.SMEM)
VMEM = pl.BlockSpec(memory_space=pltpu.VMEM)
ANY = pl.BlockSpec(memory_space=pl.ANY)


def keys_kernel(ds, pos_ref, *refs):
    kv_refs = refs[: len(ds)]
    kx_ref, v_ref, kt_ref = refs[-3:]
    place = Place(pos_ref)
    lane = lax.broadcasted_iota(jnp.int32, (ROWS, DIM), 1)
    row = lax.broadcasted_iota(jnp.int32, (ROWS, DIM), 0)
    for c, (d, kv_ref) in enumerate(zip(ds, kv_refs)):
        before = row - TEAM * ROWS * d < place.begin
        kx_ref[c, :, :DIM] = kv_ref[:ROWS]
        kx_ref[c, :, DIM:] = jnp.where((lane == 0) & before, HIDE, 0.0).astype(BF16)
        v_ref[c] = kv_ref[ROWS:]
        for j in range(TILES):
            kt_ref[c, :, j * TILE : (j + 1) * TILE] = kv_ref[j * TILE : (j + 1) * TILE].T


def keys_of(positions, ds, kvs, micros, after=()):
    shape = jax.ShapeDtypeStruct
    return pl.pallas_call(
        functools.partial(keys_kernel, ds),
        out_shape=(
            shape((len(ds), ROWS, 2 * DIM), BF16),
            shape((len(ds), ROWS, DIM), BF16),
            shape((len(ds), DIM, ROWS), BF16),
        ),
        in_specs=[SMEM] + [VMEM] * len(ds) + [ANY] * len(after),
        out_specs=(VMEM,) * 3,
        compiler_params=pltpu.CompilerParams(vmem_limit_bytes=VMEM_LIMIT),
        cost_estimate=cost(micros),
    )(positions, *[kvs[d] for d in ds], *after)


def stat_job(refs, slot, c, at, j0, keys, kind):
    kx_ref, v_ref, qx_ref, sn_ref, run_ref = refs
    n = slot * TILES + at
    part = slice(j0, j0 + keys)
    s = dot_turned(kx_ref[c, part], qx_ref[n])
    if kind is not None:
        s = jnp.where(mask_of(kind, keys), s, HIDE)
    stat_rows(run_ref, n, s, dot_turned(v_ref[c, part], sn_ref[n]))


def stat_rows(run_ref, n, s, dp):
    old = run_ref[n, 0:1]
    new = jnp.maximum(old, jnp.max(s, axis=0, keepdims=True))
    p = jnp.exp2((s - new) * SCALE)
    fade = jnp.exp2((old - new) * SCALE)
    run_ref[n, 0:1] = new
    run_ref[n, 1:2] = run_ref[n, 1:2] * fade + jnp.sum(p, axis=0, keepdims=True)
    run_ref[n, 2:3] = run_ref[n, 2:3] * fade + jnp.sum(p * dp, axis=0, keepdims=True)


def early_kernel(pos_ref, *refs):
    qs_refs = refs[0:4]
    kx_ref, v_ref, qx_ref, sn_ref, run_ref = refs[4:9]
    work = refs[4:9]
    place = Place(pos_ref)
    fill_queries(place, range(TEAM), qs_refs, qx_ref, sn_ref)
    for n in range(TEAM * TILES):
        run_ref[n, 0:1] = jnp.full((1, WIDE), 2 * HIDE, F32)
        run_ref[n, 1:8] = jnp.zeros((7, WIDE), F32)

    def block(u, t):
        for one in block_jobs(u, t):
            stat_job(work, place.slot[u], t + place.wrap[u], *one)

    def step(k, carry):
        u, t = (k + 1) // 2, (k + 1) % 2
        slot = place.pick(u, place.slot)
        d = t + place.pick(u, place.wrap)
        tiles = [slot * TILES + at for at in range(TILES)]
        scores = [dot_turned(kx_ref[d], qx_ref[n]) for n in tiles]
        dprobs = [dot_turned(v_ref[d], sn_ref[n]) for n in tiles]
        for n, s, dp in zip(tiles, scores, dprobs):
            stat_rows(run_ref, n, s, dp)
        return carry

    lax.fori_loop(0, 7, step, 0)
    block(0, 0)
    block(0, 2)
    for u in range(1, TEAM):
        pl.when(place.wrap[u] == 0)(functools.partial(block, u, 2))


def late_kernel(pos_ref, *refs):
    kx_ref, v_ref, qx_ref, sn_ref, begun_ref, stat_ref, run_ref = refs
    work = (kx_ref, v_ref, qx_ref, sn_ref, run_ref)
    place = Place(pos_ref)
    run_ref[...] = begun_ref[...]

    def block(u):
        for one in block_jobs(u, 2):
            stat_job(work, place.slot[u], 1, *one)

    for u in range(1, TEAM):
        pl.when(place.wrap[u] == 1)(functools.partial(block, u))
    for slot in range(TEAM):
        for at in range(TILES):
            n = slot * TILES + at
            total = run_ref[n, 1:2]
            stat_ref[slot, at : at + 1] = run_ref[n, 0:1] * SCALE + jnp.log2(total)
            stat_ref[slot, 3 + at : 4 + at] = run_ref[n, 2:3] / total
        stat_ref[slot, 6:8] = jnp.zeros((2, WIDE), F32)


def early_stats(positions, slots, keys, values):
    shape = jax.ShapeDtypeStruct
    blocks = TEAM * TILES
    return pl.pallas_call(
        early_kernel,
        out_shape=(
            shape((blocks, WIDE, 2 * DIM), BF16),
            shape((blocks, WIDE, DIM), BF16),
            shape((blocks, 8, WIDE), F32),
        ),
        in_specs=[SMEM] + [VMEM] * 6,
        out_specs=(VMEM,) * 3,
        compiler_params=pltpu.CompilerParams(vmem_limit_bytes=VMEM_LIMIT),
        cost_estimate=cost(12),
    )(positions, *slots, keys, values)


def late_stats(positions, keys, values, qx, sn, run):
    return pl.pallas_call(
        late_kernel,
        out_shape=jax.ShapeDtypeStruct((TEAM, 8, WIDE), F32),
        in_specs=[SMEM] + [VMEM] * 5,
        out_specs=VMEM,
        scratch_shapes=[pltpu.VMEM((TEAM * TILES, 8, WIDE), F32)],
        compiler_params=pltpu.CompilerParams(vmem_limit_bytes=VMEM_LIMIT),
        cost_estimate=cost(4),
    )(positions, keys, values, qx, sn, run)


def fill_stats(slots, stat_refs, row_ref):
    for index, slot in enumerate(slots):
        for at in range(TILES):
            n = index * TILES + at
            sums = [stat_refs[e][slot ^ e, at : at + 1] for e in range(TEAM)]
            deltas = [stat_refs[e][slot ^ e, 3 + at : 4 + at] for e in range(TEAM)]
            top = functools.reduce(jnp.maximum, sums)
            weights = [jnp.exp2(one - top) for one in sums]
            total = sum(weights)
            row_ref[n, 0:1] = top + jnp.log2(total)
            row_ref[n, 1:2] = sum(w * x for w, x in zip(weights, deltas)) / total


def grad_jobs(refs, base, jobs):
    kx_ref, v_ref, kt_ref, qx_ref, sn_ref, row_ref, dq_ref, dk_ref, dv_ref = refs

    def products(n, d, at, j0, keys, kind):
        part = slice(j0, j0 + keys)
        return dot_turned(kx_ref[d, part], qx_ref[n]), dot_turned(v_ref[d, part], sn_ref[n])

    ready = products(*jobs[0])
    dk = dv = None
    for index, (n, d, at, j0, keys, kind) in enumerate(jobs):
        part = slice(j0, j0 + keys)
        logits, dp = ready
        if index + 1 < len(jobs):
            ready = products(*jobs[index + 1])
        p = jnp.exp2(logits * SCALE - row_ref[n, 0:1])
        if kind is not None:
            p = jnp.where(mask_of(kind, keys), p, 0.0)
        ds = (p * (dp - row_ref[n, 1:2])).astype(BF16)
        more_v, more_k = dot(p.astype(BF16), sn_ref[n]), dot(ds, qx_ref[n, :, :DIM])
        dq_ref[n] += dot(kt_ref[d, :, part], ds)
        if keys == ROWS:
            dv = more_v if dv is None else dv + more_v
            dk = more_k if dk is None else dk + more_k
        else:
            dv_ref[d - base, part] += more_v
            dk_ref[d - base, part] += more_k
    if dv is not None:
        dv_ref[d - base] += dv
        dk_ref[d - base] += dk


def put_sums(ref, dk, dv):
    ref[:ROWS] = (dk * FACTOR).astype(ref.dtype)
    ref[ROWS:] = dv.astype(ref.dtype)


def put_queries(ref, dq_ref, first):
    for at in range(TILES):
        for h in range(HEADS):
            part = dq_ref[first + at, :, h * TILE : (h + 1) * TILE] * FACTOR
            ref[at * TILE : (at + 1) * TILE, h * DIM : (h + 1) * DIM] = part.T.astype(ref.dtype)


def grad_call(body, positions, blocks, shards, operands, outs, micros, refill=0):
    return pl.pallas_call(
        body,
        out_shape=outs,
        in_specs=[SMEM] + [VMEM] * len(operands),
        out_specs=(VMEM,) * len(outs),
        scratch_shapes=[
            pltpu.VMEM((blocks, DIM, WIDE), F32),
            pltpu.VMEM((shards, ROWS, DIM), F32),
            pltpu.VMEM((shards, ROWS, DIM), F32),
        ]
        + [
            pltpu.VMEM((blocks, WIDE, 2 * DIM), BF16),
            pltpu.VMEM((blocks, WIDE, DIM), BF16),
        ]
        * refill,
        compiler_params=pltpu.CompilerParams(vmem_limit_bytes=VMEM_LIMIT),
        cost_estimate=cost(micros),
    )(positions, *operands)


HALF = 2 * TILES
HELD = jax.ShapeDtypeStruct((HALF, DIM, WIDE), F32)
SUMS = jax.ShapeDtypeStruct((2, ROWS, DIM), F32)
SEND = jax.ShapeDtypeStruct((2 * ROWS, DIM), BF16)
ROW = jax.ShapeDtypeStruct((TEAM * TILES, 8, WIDE), F32)


def farthest_kernel(pos_ref, *refs):
    stat_refs, keys, (qx_ref, sn_ref) = refs[0:4], refs[4:7], refs[7:9]
    send_ref, row_ref, dq_ref = refs[9:12]
    dk_ref, dv_ref = refs[12:14]
    work = (*keys, qx_ref, sn_ref, row_ref, dq_ref, dk_ref, dv_ref)
    place = Place(pos_ref)
    fill_stats(range(TEAM), stat_refs, row_ref)
    for ref in (dq_ref, dk_ref, dv_ref):
        ref[...] = jnp.zeros_like(ref)

    def block(u):
        grad_jobs(work, 1, [(place.slot[u] * TILES + one[0], 1, *one) for one in block_jobs(u, 2)])

    for u in range(1, TEAM):
        pl.when(place.wrap[u] == 1)(functools.partial(block, u))
    put_sums(send_ref, dk_ref[0], dv_ref[0])


def far_kernel(pos_ref, *refs):
    keys, (qx_ref, sn_ref, row_ref, held_ref) = refs[0:3], refs[3:7]
    near_ref, away_ref, send_ref = refs[7:10]
    dq_ref, dk_ref, dv_ref = refs[10:13]
    work = (*keys, qx_ref, sn_ref, row_ref, dq_ref, dk_ref, dv_ref)
    place = Place(pos_ref)
    dq_ref[...] = held_ref[...]
    dk_ref[...] = jnp.zeros_like(dk_ref)
    dv_ref[...] = jnp.zeros_like(dv_ref)

    def block(u, t):
        grad_jobs(work, 0, [(place.slot[u] * TILES + one[0], 0, *one) for one in block_jobs(u, t)])

    block(0, 2)
    for u in range(1, TEAM):
        pl.when(place.wrap[u] == 0)(functools.partial(block, u, 2))
        pl.when(place.wrap[u] == 1)(functools.partial(block, u, 1))
    near_ref[...] = dq_ref[:HALF]
    away_ref[...] = dq_ref[HALF:]
    put_sums(send_ref, dk_ref[0], dv_ref[0])


def away_kernel(pos_ref, *refs):
    keys, qs_refs, row_ref = refs[0:3], refs[3:5], refs[5]
    held_ref, dq_far_ref, dq_both_ref, sums0_ref, sums1_ref = refs[6:11]
    dq_ref, dk_ref, dv_ref, qx_ref, sn_ref = refs[11:16]
    work = (*keys, qx_ref, sn_ref, row_ref.at[HALF:], dq_ref, dk_ref, dv_ref)
    place = Place(pos_ref)
    fill_queries(place, (2, 3), qs_refs, qx_ref, sn_ref)
    dq_ref[...] = held_ref[...]
    dk_ref[...] = jnp.zeros_like(dk_ref)
    dv_ref[...] = jnp.zeros_like(dv_ref)

    def block(index, d):
        grad_jobs(work, 0, [(index * TILES + one[0], d, *one) for one in block_jobs(1, 0)])

    for index in range(2):
        block(index, 1)
    for index in range(2):
        pl.when(place.slot_wrap(2 + index) == 0)(functools.partial(block, index, 0))
    put_queries(dq_far_ref, dq_ref, 0)
    put_queries(dq_both_ref, dq_ref, TILES)
    for d, ref in enumerate((sums0_ref, sums1_ref)):
        ref[0] = dk_ref[d]
        ref[1] = dv_ref[d]


def near_kernel(pos_ref, *refs):
    keys, qs_refs, row_ref = refs[0:3], refs[3:5], refs[5]
    held_ref, sums_ref, _, out_ref, send_ref = refs[6:11]
    dq_ref, dk_ref, dv_ref, qx_ref, sn_ref = refs[11:16]
    work = (*keys, qx_ref, sn_ref, row_ref, dq_ref, dk_ref, dv_ref)
    fill_queries(Place(pos_ref), (0, 1), qs_refs, qx_ref, sn_ref)
    dq_ref[...] = held_ref[...]
    dk_ref[0] = sums_ref[0]
    dv_ref[0] = sums_ref[1]
    for index in range(2):
        grad_jobs(work, 1, [(index * TILES + one[0], 1, *one) for one in block_jobs(1, 0)])
    out_ref[...] = dq_ref[...]
    put_sums(send_ref, dk_ref[0], dv_ref[0])


def own_kernel(pos_ref, *refs):
    keys, qs_refs, row_ref = refs[0:3], refs[3:5], refs[5]
    held_ref, sums_ref, _, dq_own_ref, dq_core_ref, kv_ref = refs[6:12]
    dq_ref, dk_ref, dv_ref, qx_ref, sn_ref = refs[12:17]
    work = (*keys, qx_ref, sn_ref, row_ref, dq_ref, dk_ref, dv_ref)
    place = Place(pos_ref)
    fill_queries(place, (0, 1), qs_refs, qx_ref, sn_ref)
    dq_ref[...] = held_ref[...]
    dk_ref[0] = sums_ref[0]
    dv_ref[0] = sums_ref[1]

    def other():
        grad_jobs(work, 0, [(TILES + one[0], 0, *one) for one in block_jobs(1, 0)])

    grad_jobs(work, 0, [(one[0], 0, *one) for one in block_jobs(0, 0)])
    pl.when(place.slot_wrap(1) == 0)(other)
    put_queries(dq_own_ref, dq_ref, 0)
    put_queries(dq_core_ref, dq_ref, TILES)
    put_sums(kv_ref, dk_ref[0], dv_ref[0])


def team_slots(value):
    core = permute(value, lambda s: s ^ 1)
    far = permute(value, lambda s: s ^ 2)
    both = permute(far, lambda s: s ^ 1)
    return [value, core, far, both]


def per_device(queries, key_rows, value_rows, positions, latent_ids, latent_acts, latent_dirs):
    kv = jnp.concatenate([key_rows, value_rows], axis=0)
    kvs = [kv] + [permute(kv, lambda s, d=d: s + TEAM * d) for d in (1, 2)]
    kvs.append(permute(kvs[2], lambda s: s + TEAM))
    qs = team_slots(with_seeds(queries, latent_ids, latent_acts, latent_dirs))
    early = keys_of(positions, (0, 1, 2), kvs, EARLY_COST)
    qx, sn, run = early_stats(positions, qs, *early[:2])
    late = keys_of(positions, (2, 3), kvs, LATE_COST, (run,))
    stat = late_stats(positions, *late[:2], qx, sn, run)
    stats = [stat] + [permute(stat, lambda s, e=e: s ^ e) for e in range(1, TEAM)]

    shape = jax.ShapeDtypeStruct
    wide, thin = (ROWS, HEADS * DIM), (2 * ROWS, DIM)
    send3, rows, held = pl.pallas_call(
        farthest_kernel,
        out_shape=(SEND, ROW, shape((TEAM * TILES, DIM, WIDE), F32)),
        in_specs=[SMEM] + [VMEM] * 9,
        out_specs=(VMEM,) * 3,
        scratch_shapes=[pltpu.VMEM((1, ROWS, DIM), F32)] * 2,
        compiler_params=pltpu.CompilerParams(vmem_limit_bytes=VMEM_LIMIT),
        cost_estimate=cost(FAR_COST),
    )(positions, *stats, *late, qx, sn)
    held_near, held_away, send2 = grad_call(
        far_kernel,
        positions,
        TEAM * TILES,
        1,
        (*late, qx, sn, rows, held),
        (HELD, HELD, shape(thin, F32)),
        FAR_COST,
    )

    def call(body, shards, extra, outs, micros):
        slots = qs[2:] if body is away_kernel else qs[:2]
        operands = (*early, *slots, rows, *extra)
        return grad_call(body, positions, HALF, shards, operands, outs, micros, refill=1)

    send3 = permute(send3, lambda s: s - TEAM)
    send2 = (send2 + send3.astype(F32)).astype(BF16)
    back2 = permute(send2, lambda s: s - 2 * TEAM)
    dq_far, dq_both, sums0, sums1 = call(
        away_kernel, 2, (held_away,), (shape(wide, F32), shape(wide, BF16), SUMS, SUMS), GRAD_COST
    )
    dq_both = permute(dq_both, lambda s: s ^ 1)
    held_near, send1 = call(near_kernel, 1, (held_near, sums1, send2), (HELD, SEND), GRAD_COST)
    back1 = permute(send1, lambda s: s - TEAM)
    dq_far = (dq_far + dq_both.astype(F32)).astype(BF16)
    dq_back = permute(dq_far, lambda s: s ^ 2)
    dq_own, dq_core, kv_own = call(
        own_kernel,
        1,
        (held_near, sums0, dq_far),
        (shape(wide, F32), shape(wide, BF16), shape(thin, F32)),
        GRAD_COST,
    )
    dq_core = permute(dq_core, lambda s: s ^ 1)
    grad_q = (dq_own + dq_core.astype(F32) + dq_back.astype(F32)).astype(BF16)
    grad_kv = kv_own + back1.astype(F32) + back2.astype(F32)
    return grad_q, grad_kv[:ROWS].astype(BF16), grad_kv[ROWS:].astype(BF16)


def solution(mesh):
    in_specs = (
        P(("mp", "ctx"), None),
        P(("mp", "ctx"), None),
        P(("mp", "ctx"), None),
        P("ctx"),
        P(("mp", "ctx"), None),
        P(("mp", "ctx"), None),
        P("mp", None),
    )
    out_specs = (P(("mp", "ctx"), None), P(("mp", "ctx"), None), P(("mp", "ctx"), None))
    return jax.shard_map(
        per_device, mesh=mesh, in_specs=in_specs, out_specs=out_specs, check_vma=False
    )
```

```python
import functools
import math

import jax
import jax.numpy as jnp
from jax import lax
from jax.experimental import pallas as pl
from jax.experimental.pallas import tpu as pltpu
from jax.sharding import PartitionSpec as P

TEAM = 4
ROWS = 384
TILES = 3
TILE = 128
HEADS = 4
DIM = 128
WIDE = HEADS * TILE
WINDOW = 4096
FACTOR = 1.0 / math.sqrt(DIM)
SCALE = FACTOR * math.log2(math.e)
HIDE = -1e30
VMEM_LIMIT = 28 * 1024 * 1024
SEED_LIMIT = 60 * 1024 * 1024

EARLY_COST = 60
LATE_COST = 1
GRAD_COST = 5
FAR_COST = 5

BF16 = jnp.bfloat16
F32 = jnp.float32


def permute(value, target, members=range(4)):
    count = lax.axis_size("ctx")
    pairs = [(s, target(s) % count) for s in range(count) if s % TEAM in members]
    return lax.ppermute(value, "ctx", pairs)


def dot(a, b):
    return jnp.dot(a, b, preferred_element_type=F32)


def dot_turned(a, b):
    return lax.dot_general(a, b, (((1,), (1,)), ((), ())), preferred_element_type=F32)


def cost(micros):
    return pl.CostEstimate(
        flops=int(micros * 1e9), bytes_accessed=int(micros * 2e6), transcendentals=0
    )


def halves(value):
    high = value.astype(BF16)
    return high, (value - high.astype(F32)).astype(BF16)


def seed_kernel(q_ref, ids_ref, acts_ref, dirs_ref, out_ref, table_ref, sems):
    latents = dirs_ref.shape[0]
    rows = ids_ref.shape[1]
    fetch = pltpu.make_async_copy(dirs_ref, table_ref, sems.at[0])
    fetch.start()
    place = pltpu.make_async_copy(q_ref, out_ref.at[:rows], sems.at[1])
    place.start()
    lane = lax.broadcasted_iota(jnp.int32, (latents, rows), 0)
    mixing = jnp.zeros((latents, rows), F32)
    for k in range(ids_ref.shape[0]):
        mixing = mixing + jnp.where(lane == ids_ref[k : k + 1, :], acts_ref[k : k + 1, :], 0.0)
    mix_high, mix_low = halves(mixing.T)
    fetch.wait()
    dir_high, dir_low = halves(table_ref[...])
    seeds = dot(mix_high, dir_low) + dot(mix_low, dir_high) + dot(mix_high, dir_high)
    out_ref[rows:] = seeds.astype(BF16)
    place.wait()


def with_seeds(queries, latent_ids, latent_acts, latent_dirs):
    vmem = pl.BlockSpec(memory_space=pltpu.VMEM)
    hbm = pl.BlockSpec(memory_space=pl.ANY)
    return pl.pallas_call(
        seed_kernel,
        out_shape=jax.ShapeDtypeStruct((2 * queries.shape[0], queries.shape[1]), BF16),
        in_specs=[hbm, vmem, vmem, hbm],
        out_specs=vmem,
        scratch_shapes=[
            pltpu.VMEM(latent_dirs.shape, F32),
            pltpu.SemaphoreType.DMA((2,)),
        ],
        compiler_params=pltpu.CompilerParams(vmem_limit_bytes=SEED_LIMIT),
        cost_estimate=cost(4),
    )(queries, latent_ids.T, latent_acts.T, latent_dirs)


class Place:
    def __init__(self, pos_ref):
        ctx = lax.axis_index("ctx")
        tokens = ROWS * lax.axis_size("ctx")
        first = pos_ref[0]
        member = ctx % TEAM
        self.core = member % 2
        self.begin = jnp.where(first < tokens // 2, -first, tokens - first)
        self.wrap = [jnp.where(member + u >= TEAM, 1, 0) for u in range(TEAM)]
        self.slot = [0, 1 + 2 * self.core, 2, 3 - 2 * self.core]

    def pick(self, u, values):
        out = values[0]
        for index in range(1, TEAM):
            out = jnp.where(u == index, values[index], out)
        return out

    def slot_wrap(self, slot):
        if slot == 0:
            return 0
        if slot == 2:
            return self.wrap[2]
        near, away = self.wrap[slot], self.wrap[TEAM - slot]
        return jnp.where(self.core == 0, near, away)

    def slot_offset(self, slot):
        if slot == 0:
            return 0
        member = 2 if slot == 2 else jnp.where(self.core == 0, slot, TEAM - slot)
        return ROWS * member - TEAM * ROWS * self.slot_wrap(slot)


def mask_of(kind, keys):
    name, shift = kind
    key = lax.broadcasted_iota(jnp.int32, (keys, WIDE), 0)
    query = lax.broadcasted_iota(jnp.int32, (keys, WIDE), 1) % TILE
    if name == "causal":
        return key <= query + shift
    return key >= query + shift


def block_jobs(u, t):
    if (u, t) == (0, 0):
        return [(at, 0, (at + 1) * TILE, ("causal", at * TILE)) for at in range(TILES)]
    if (u, t) == (2, 2):
        return [(0, 0, ROWS, None), (1, 0, ROWS, None), (2, 0, ROWS, ("tail", 1))]
    if (u, t) == (3, 2):
        return [(0, TILE, 2 * TILE, ("tail", 1)), (1, 2 * TILE, TILE, ("tail", 1))]
    return [(at, 0, ROWS, None) for at in range(TILES)]


def fill_queries(place, slots, qs_refs, qx_ref, sn_ref):
    lane = lax.broadcasted_iota(jnp.int32, (TILE, DIM), 1)
    row = lax.broadcasted_iota(jnp.int32, (TILE, DIM), 0)
    for index, slot in enumerate(slots):
        for at in range(TILES):
            n = index * TILES + at
            after = row + at * TILE + place.slot_offset(slot) >= place.begin
            flag = jnp.where((lane == 0) & after, 1.0, 0.0).astype(BF16)
            for h in range(HEADS):
                cut = (slice(at * TILE, (at + 1) * TILE), slice(h * DIM, (h + 1) * DIM))
                into = slice(h * TILE, (h + 1) * TILE)
                seed_cut = (slice(ROWS + at * TILE, ROWS + (at + 1) * TILE), cut[1])
                qx_ref[n, into, :DIM] = qs_refs[index][cut]
                qx_ref[n, into, DIM:] = flag
                sn_ref[n, into] = qs_refs[index][seed_cut]


SMEM = pl.BlockSpec(memory_space=pltpu.SMEM)
VMEM = pl.BlockSpec(memory_space=pltpu.VMEM)
ANY = pl.BlockSpec(memory_space=pl.ANY)


def keys_kernel(ds, pos_ref, *refs):
    kv_refs = refs[: len(ds)]
    kx_ref, v_ref, kt_ref = refs[-3:]
    place = Place(pos_ref)
    lane = lax.broadcasted_iota(jnp.int32, (ROWS, DIM), 1)
    row = lax.broadcasted_iota(jnp.int32, (ROWS, DIM), 0)
    for c, (d, kv_ref) in enumerate(zip(ds, kv_refs)):
        before = row - TEAM * ROWS * d < place.begin
        kx_ref[c, :, :DIM] = kv_ref[:ROWS]
        kx_ref[c, :, DIM:] = jnp.where((lane == 0) & before, HIDE, 0.0).astype(BF16)
        v_ref[c] = kv_ref[ROWS:]
        for j in range(TILES):
            kt_ref[c, :, j * TILE : (j + 1) * TILE] = kv_ref[j * TILE : (j + 1) * TILE].T


def keys_of(positions, ds, kvs, micros, after=()):
    shape = jax.ShapeDtypeStruct
    return pl.pallas_call(
        functools.partial(keys_kernel, ds),
        out_shape=(
            shape((len(ds), ROWS, 2 * DIM), BF16),
            shape((len(ds), ROWS, DIM), BF16),
            shape((len(ds), DIM, ROWS), BF16),
        ),
        in_specs=[SMEM] + [VMEM] * len(ds) + [ANY] * len(after),
        out_specs=(VMEM,) * 3,
        compiler_params=pltpu.CompilerParams(vmem_limit_bytes=VMEM_LIMIT),
        cost_estimate=cost(micros),
    )(positions, *[kvs[d] for d in ds], *after)


def stat_job(refs, slot, c, at, j0, keys, kind):
    kx_ref, v_ref, qx_ref, sn_ref, run_ref = refs
    n = slot * TILES + at
    part = slice(j0, j0 + keys)
    s = dot_turned(kx_ref[c, part], qx_ref[n])
    if kind is not None:
        s = jnp.where(mask_of(kind, keys), s, HIDE)
    stat_rows(run_ref, n, s, dot_turned(v_ref[c, part], sn_ref[n]))


def stat_rows(run_ref, n, s, dp):
    old = run_ref[n, 0:1]
    new = jnp.maximum(old, jnp.max(s, axis=0, keepdims=True))
    p = jnp.exp2((s - new) * SCALE)
    fade = jnp.exp2((old - new) * SCALE)
    run_ref[n, 0:1] = new
    run_ref[n, 1:2] = run_ref[n, 1:2] * fade + jnp.sum(p, axis=0, keepdims=True)
    run_ref[n, 2:3] = run_ref[n, 2:3] * fade + jnp.sum(p * dp, axis=0, keepdims=True)


def early_kernel(pos_ref, *refs):
    qs_refs = refs[0:4]
    kx_ref, v_ref, qx_ref, sn_ref, run_ref = refs[4:9]
    work = refs[4:9]
    place = Place(pos_ref)
    fill_queries(place, range(TEAM), qs_refs, qx_ref, sn_ref)
    for n in range(TEAM * TILES):
        run_ref[n, 0:1] = jnp.full((1, WIDE), 2 * HIDE, F32)
        run_ref[n, 1:8] = jnp.zeros((7, WIDE), F32)

    def block(u, t):
        for one in block_jobs(u, t):
            stat_job(work, place.slot[u], t + place.wrap[u], *one)

    def step(k, carry):
        u, t = (k + 1) // 2, (k + 1) % 2
        slot = place.pick(u, place.slot)
        d = t + place.pick(u, place.wrap)
        tiles = [slot * TILES + at for at in range(TILES)]
        scores = [dot_turned(kx_ref[d], qx_ref[n]) for n in tiles]
        dprobs = [dot_turned(v_ref[d], sn_ref[n]) for n in tiles]
        for n, s, dp in zip(tiles, scores, dprobs):
            stat_rows(run_ref, n, s, dp)
        return carry

    lax.fori_loop(0, 7, step, 0)
    block(0, 0)
    block(0, 2)
    for u in range(1, TEAM):
        pl.when(place.wrap[u] == 0)(functools.partial(block, u, 2))


def late_kernel(pos_ref, *refs):
    kx_ref, v_ref, qx_ref, sn_ref, begun_ref, stat_ref, run_ref = refs
    work = (kx_ref, v_ref, qx_ref, sn_ref, run_ref)
    place = Place(pos_ref)
    run_ref[...] = begun_ref[...]

    def block(u):
        for one in block_jobs(u, 2):
            stat_job(work, place.slot[u], 1, *one)

    for u in range(1, TEAM):
        pl.when(place.wrap[u] == 1)(functools.partial(block, u))
    for slot in range(TEAM):
        for at in range(TILES):
            n = slot * TILES + at
            total = run_ref[n, 1:2]
            stat_ref[slot, at : at + 1] = run_ref[n, 0:1] * SCALE + jnp.log2(total)
            stat_ref[slot, 3 + at : 4 + at] = run_ref[n, 2:3] / total
        stat_ref[slot, 6:8] = jnp.zeros((2, WIDE), F32)


def early_stats(positions, slots, keys, values):
    shape = jax.ShapeDtypeStruct
    blocks = TEAM * TILES
    return pl.pallas_call(
        early_kernel,
        out_shape=(
            shape((blocks, WIDE, 2 * DIM), BF16),
            shape((blocks, WIDE, DIM), BF16),
            shape((blocks, 8, WIDE), F32),
        ),
        in_specs=[SMEM] + [VMEM] * 6,
        out_specs=(VMEM,) * 3,
        compiler_params=pltpu.CompilerParams(vmem_limit_bytes=VMEM_LIMIT),
        cost_estimate=cost(12),
    )(positions, *slots, keys, values)


def late_stats(positions, keys, values, qx, sn, run):
    return pl.pallas_call(
        late_kernel,
        out_shape=jax.ShapeDtypeStruct((TEAM, 8, WIDE), F32),
        in_specs=[SMEM] + [VMEM] * 5,
        out_specs=VMEM,
        scratch_shapes=[pltpu.VMEM((TEAM * TILES, 8, WIDE), F32)],
        compiler_params=pltpu.CompilerParams(vmem_limit_bytes=VMEM_LIMIT),
        cost_estimate=cost(4),
    )(positions, keys, values, qx, sn, run)


def fill_stats(slots, stat_refs, row_ref):
    for index, slot in enumerate(slots):
        for at in range(TILES):
            n = index * TILES + at
            sums = [stat_refs[e][slot ^ e, at : at + 1] for e in range(TEAM)]
            deltas = [stat_refs[e][slot ^ e, 3 + at : 4 + at] for e in range(TEAM)]
            top = functools.reduce(jnp.maximum, sums)
            weights = [jnp.exp2(one - top) for one in sums]
            total = sum(weights)
            row_ref[n, 0:1] = top + jnp.log2(total)
            row_ref[n, 1:2] = sum(w * x for w, x in zip(weights, deltas)) / total


def grad_jobs(refs, base, jobs):
    kx_ref, v_ref, kt_ref, qx_ref, sn_ref, row_ref, dq_ref, dk_ref, dv_ref = refs

    def products(n, d, at, j0, keys, kind):
        part = slice(j0, j0 + keys)
        return dot_turned(kx_ref[d, part], qx_ref[n]), dot_turned(v_ref[d, part], sn_ref[n])

    ready = products(*jobs[0])
    dk = dv = None
    for index, (n, d, at, j0, keys, kind) in enumerate(jobs):
        part = slice(j0, j0 + keys)
        logits, dp = ready
        if index + 1 < len(jobs):
            ready = products(*jobs[index + 1])
        p = jnp.exp2(logits * SCALE - row_ref[n, 0:1])
        if kind is not None:
            p = jnp.where(mask_of(kind, keys), p, 0.0)
        ds = (p * (dp - row_ref[n, 1:2])).astype(BF16)
        more_v, more_k = dot(p.astype(BF16), sn_ref[n]), dot(ds, qx_ref[n, :, :DIM])
        dq_ref[n] += dot(kt_ref[d, :, part], ds)
        if keys == ROWS:
            dv = more_v if dv is None else dv + more_v
            dk = more_k if dk is None else dk + more_k
        else:
            dv_ref[d - base, part] += more_v
            dk_ref[d - base, part] += more_k
    if dv is not None:
        dv_ref[d - base] += dv
        dk_ref[d - base] += dk


def put_sums(ref, dk, dv):
    ref[:ROWS] = (dk * FACTOR).astype(ref.dtype)
    ref[ROWS:] = dv.astype(ref.dtype)


def put_queries(ref, dq_ref, first):
    for at in range(TILES):
        for h in range(HEADS):
            part = dq_ref[first + at, :, h * TILE : (h + 1) * TILE] * FACTOR
            ref[at * TILE : (at + 1) * TILE, h * DIM : (h + 1) * DIM] = part.T.astype(ref.dtype)


def grad_call(body, positions, blocks, shards, operands, outs, micros, refill=0):
    return pl.pallas_call(
        body,
        out_shape=outs,
        in_specs=[SMEM] + [VMEM] * len(operands),
        out_specs=(VMEM,) * len(outs),
        scratch_shapes=[
            pltpu.VMEM((blocks, DIM, WIDE), F32),
            pltpu.VMEM((shards, ROWS, DIM), F32),
            pltpu.VMEM((shards, ROWS, DIM), F32),
        ]
        + [
            pltpu.VMEM((blocks, WIDE, 2 * DIM), BF16),
            pltpu.VMEM((blocks, WIDE, DIM), BF16),
        ]
        * refill,
        compiler_params=pltpu.CompilerParams(vmem_limit_bytes=VMEM_LIMIT),
        cost_estimate=cost(micros),
    )(positions, *operands)


HALF = 2 * TILES
HELD = jax.ShapeDtypeStruct((HALF, DIM, WIDE), F32)
SUMS = jax.ShapeDtypeStruct((2, ROWS, DIM), F32)
SEND = jax.ShapeDtypeStruct((2 * ROWS, DIM), BF16)
ROW = jax.ShapeDtypeStruct((TEAM * TILES, 8, WIDE), F32)


def farthest_kernel(pos_ref, *refs):
    stat_refs, keys, (qx_ref, sn_ref) = refs[0:4], refs[4:7], refs[7:9]
    send_ref, row_ref, dq_ref = refs[9:12]
    dk_ref, dv_ref = refs[12:14]
    work = (*keys, qx_ref, sn_ref, row_ref, dq_ref, dk_ref, dv_ref)
    place = Place(pos_ref)
    fill_stats(range(TEAM), stat_refs, row_ref)
    for ref in (dq_ref, dk_ref, dv_ref):
        ref[...] = jnp.zeros_like(ref)

    def block(u):
        grad_jobs(work, 1, [(place.slot[u] * TILES + one[0], 1, *one) for one in block_jobs(u, 2)])

    for u in range(1, TEAM):
        pl.when(place.wrap[u] == 1)(functools.partial(block, u))
    put_sums(send_ref, dk_ref[0], dv_ref[0])


def far_kernel(pos_ref, *refs):
    keys, (qx_ref, sn_ref, row_ref, held_ref) = refs[0:3], refs[3:7]
    near_ref, away_ref, send_ref = refs[7:10]
    dq_ref, dk_ref, dv_ref = refs[10:13]
    work = (*keys, qx_ref, sn_ref, row_ref, dq_ref, dk_ref, dv_ref)
    place = Place(pos_ref)
    dq_ref[...] = held_ref[...]
    dk_ref[...] = jnp.zeros_like(dk_ref)
    dv_ref[...] = jnp.zeros_like(dv_ref)

    def block(u, t):
        grad_jobs(work, 0, [(place.slot[u] * TILES + one[0], 0, *one) for one in block_jobs(u, t)])

    block(0, 2)
    for u in range(1, TEAM):
        pl.when(place.wrap[u] == 0)(functools.partial(block, u, 2))
        pl.when(place.wrap[u] == 1)(functools.partial(block, u, 1))
    near_ref[...] = dq_ref[:HALF]
    away_ref[...] = dq_ref[HALF:]
    put_sums(send_ref, dk_ref[0], dv_ref[0])


def away_kernel(pos_ref, *refs):
    keys, qs_refs, row_ref = refs[0:3], refs[3:5], refs[5]
    held_ref, dq_far_ref, dq_both_ref, sums0_ref, sums1_ref = refs[6:11]
    dq_ref, dk_ref, dv_ref, qx_ref, sn_ref = refs[11:16]
    work = (*keys, qx_ref, sn_ref, row_ref.at[HALF:], dq_ref, dk_ref, dv_ref)
    place = Place(pos_ref)
    fill_queries(place, (2, 3), qs_refs, qx_ref, sn_ref)
    dq_ref[...] = held_ref[...]
    dk_ref[...] = jnp.zeros_like(dk_ref)
    dv_ref[...] = jnp.zeros_like(dv_ref)

    def block(index, d):
        grad_jobs(work, 0, [(index * TILES + one[0], d, *one) for one in block_jobs(1, 0)])

    for index in range(2):
        block(index, 1)
    for index in range(2):
        pl.when(place.slot_wrap(2 + index) == 0)(functools.partial(block, index, 0))
    put_queries(dq_far_ref, dq_ref, 0)
    put_queries(dq_both_ref, dq_ref, TILES)
    for d, ref in enumerate((sums0_ref, sums1_ref)):
        ref[0] = dk_ref[d]
        ref[1] = dv_ref[d]


def near_kernel(pos_ref, *refs):
    keys, qs_refs, row_ref = refs[0:3], refs[3:5], refs[5]
    held_ref, sums_ref, out_ref, send_ref = refs[6:10]
    dq_ref, dk_ref, dv_ref, qx_ref, sn_ref = refs[10:15]
    work = (*keys, qx_ref, sn_ref, row_ref, dq_ref, dk_ref, dv_ref)
    fill_queries(Place(pos_ref), (0, 1), qs_refs, qx_ref, sn_ref)
    dq_ref[...] = held_ref[...]
    dk_ref[0] = sums_ref[0]
    dv_ref[0] = sums_ref[1]
    for index in range(2):
        grad_jobs(work, 1, [(index * TILES + one[0], 1, *one) for one in block_jobs(1, 0)])
    out_ref[...] = dq_ref[...]
    put_sums(send_ref, dk_ref[0], dv_ref[0])


def own_kernel(pos_ref, *refs):
    keys, qs_refs, row_ref = refs[0:3], refs[3:5], refs[5]
    held_ref, sums_ref, _, dq_own_ref, dq_core_ref, kv_ref = refs[6:12]
    dq_ref, dk_ref, dv_ref, qx_ref, sn_ref = refs[12:17]
    work = (*keys, qx_ref, sn_ref, row_ref, dq_ref, dk_ref, dv_ref)
    place = Place(pos_ref)
    fill_queries(place, (0, 1), qs_refs, qx_ref, sn_ref)
    dq_ref[...] = held_ref[...]
    dk_ref[0] = sums_ref[0]
    dv_ref[0] = sums_ref[1]

    def other():
        grad_jobs(work, 0, [(TILES + one[0], 0, *one) for one in block_jobs(1, 0)])

    grad_jobs(work, 0, [(one[0], 0, *one) for one in block_jobs(0, 0)])
    pl.when(place.slot_wrap(1) == 0)(other)
    put_queries(dq_own_ref, dq_ref, 0)
    put_queries(dq_core_ref, dq_ref, TILES)
    put_sums(kv_ref, dk_ref[0], dv_ref[0])


def team_slots(value):
    core = permute(value, lambda s: s ^ 1)
    far = permute(value, lambda s: s ^ 2)
    both = permute(far, lambda s: s ^ 1)
    return [value, core, far, both]


def per_device(queries, key_rows, value_rows, positions, latent_ids, latent_acts, latent_dirs):
    kv = jnp.concatenate([key_rows, value_rows], axis=0)
    kvs = [kv] + [permute(kv, lambda s, d=d: s + TEAM * d) for d in (1, 2)]
    kvs.append(permute(kvs[2], lambda s: s + TEAM, (1, 2, 3)))
    qs = team_slots(with_seeds(queries, latent_ids, latent_acts, latent_dirs))
    early = keys_of(positions, (0, 1, 2), kvs, EARLY_COST)
    qx, sn, run = early_stats(positions, qs, *early[:2])
    late = keys_of(positions, (2, 3), kvs, LATE_COST, (run,))
    stat = late_stats(positions, *late[:2], qx, sn, run)
    stats = [stat] + [permute(stat, lambda s, e=e: s ^ e) for e in range(1, TEAM)]

    shape = jax.ShapeDtypeStruct
    wide, thin = (ROWS, HEADS * DIM), (2 * ROWS, DIM)
    send3, rows, held = pl.pallas_call(
        farthest_kernel,
        out_shape=(SEND, ROW, shape((TEAM * TILES, DIM, WIDE), F32)),
        in_specs=[SMEM] + [VMEM] * 9,
        out_specs=(VMEM,) * 3,
        scratch_shapes=[pltpu.VMEM((1, ROWS, DIM), F32)] * 2,
        compiler_params=pltpu.CompilerParams(vmem_limit_bytes=VMEM_LIMIT),
        cost_estimate=cost(FAR_COST),
    )(positions, *stats, *late, qx, sn)
    held_near, held_away, send2 = grad_call(
        far_kernel,
        positions,
        TEAM * TILES,
        1,
        (*late, qx, sn, rows, held),
        (HELD, HELD, shape(thin, F32)),
        FAR_COST,
    )

    def call(body, shards, extra, outs, micros):
        slots = qs[2:] if body is away_kernel else qs[:2]
        operands = (*early, *slots, rows, *extra)
        return grad_call(body, positions, HALF, shards, operands, outs, micros, refill=1)

    send3 = permute(send3, lambda s: s - TEAM, (1, 2, 3))
    send2 = (send2 + send3.astype(F32)).astype(BF16)
    back2 = permute(send2, lambda s: s - 2 * TEAM)
    dq_far, dq_both, sums0, sums1 = call(
        away_kernel, 2, (held_away,), (shape(wide, F32), shape(wide, BF16), SUMS, SUMS), GRAD_COST
    )
    dq_both = permute(dq_both, lambda s: s ^ 1)
    held_near, send1 = call(near_kernel, 1, (held_near, sums1), (HELD, SEND), GRAD_COST)
    back1 = permute(send1, lambda s: s - TEAM)
    dq_far = (dq_far + dq_both.astype(F32)).astype(BF16)
    dq_back = permute(dq_far, lambda s: s ^ 2)
    dq_own, dq_core, kv_own = call(
        own_kernel,
        1,
        (held_near, sums0, dq_far),
        (shape(wide, F32), shape(wide, BF16), shape(thin, F32)),
        GRAD_COST,
    )
    dq_core = permute(dq_core, lambda s: s ^ 1)
    grad_q = (dq_own + dq_core.astype(F32) + dq_back.astype(F32)).astype(BF16)
    grad_kv = kv_own + back1.astype(F32) + back2.astype(F32)
    return grad_q, grad_kv[:ROWS].astype(BF16), grad_kv[ROWS:].astype(BF16)


def solution(mesh):
    in_specs = (
        P(("mp", "ctx"), None),
        P(("mp", "ctx"), None),
        P(("mp", "ctx"), None),
        P("ctx"),
        P(("mp", "ctx"), None),
        P(("mp", "ctx"), None),
        P("mp", None),
    )
    out_specs = (P(("mp", "ctx"), None), P(("mp", "ctx"), None), P(("mp", "ctx"), None))
    return jax.shard_map(
        per_device, mesh=mesh, in_specs=in_specs, out_specs=out_specs, check_vma=False
    )
```

```python
import functools
import math

import jax
import jax.numpy as jnp
from jax import lax
from jax.experimental import pallas as pl
from jax.experimental.pallas import tpu as pltpu
from jax.sharding import PartitionSpec as P

TEAM = 4
ROWS = 384
TILES = 3
TILE = 128
HEADS = 4
DIM = 128
WIDE = HEADS * TILE
WINDOW = 4096
FACTOR = 1.0 / math.sqrt(DIM)
SCALE = FACTOR * math.log2(math.e)
HIDE = -1e30
VMEM_LIMIT = 28 * 1024 * 1024
SEED_LIMIT = 60 * 1024 * 1024

EARLY_COST = 60
LATE_COST = 1
GRAD_COST = 5
FAR_COST = 5

BF16 = jnp.bfloat16
F32 = jnp.float32


def permute(value, target):
    count = lax.axis_size("ctx")
    return lax.ppermute(value, "ctx", [(s, target(s) % count) for s in range(count)])


def dot(a, b):
    return jnp.dot(a, b, preferred_element_type=F32)


def dot_turned(a, b):
    return lax.dot_general(a, b, (((1,), (1,)), ((), ())), preferred_element_type=F32)


def cost(micros):
    return pl.CostEstimate(
        flops=int(micros * 1e9), bytes_accessed=int(micros * 2e6), transcendentals=0
    )


def halves(value):
    high = value.astype(BF16)
    return high, (value - high.astype(F32)).astype(BF16)


def seed_kernel(q_ref, ids_ref, acts_ref, dirs_ref, out_ref, table_ref, sems):
    latents = dirs_ref.shape[0]
    rows = ids_ref.shape[1]
    fetch = pltpu.make_async_copy(dirs_ref, table_ref, sems.at[0])
    fetch.start()
    place = pltpu.make_async_copy(q_ref, out_ref.at[:rows], sems.at[1])
    place.start()
    lane = lax.broadcasted_iota(jnp.int32, (latents, rows), 0)
    mixing = jnp.zeros((latents, rows), F32)
    for k in range(ids_ref.shape[0]):
        mixing = mixing + jnp.where(lane == ids_ref[k : k + 1, :], acts_ref[k : k + 1, :], 0.0)
    mix_high, mix_low = halves(mixing.T)
    fetch.wait()
    dir_high, dir_low = halves(table_ref[...])
    seeds = dot(mix_high, dir_low) + dot(mix_low, dir_high) + dot(mix_high, dir_high)
    out_ref[rows:] = seeds.astype(BF16)
    place.wait()


def with_seeds(queries, latent_ids, latent_acts, latent_dirs):
    vmem = pl.BlockSpec(memory_space=pltpu.VMEM)
    hbm = pl.BlockSpec(memory_space=pl.ANY)
    return pl.pallas_call(
        seed_kernel,
        out_shape=jax.ShapeDtypeStruct((2 * queries.shape[0], queries.shape[1]), BF16),
        in_specs=[hbm, vmem, vmem, hbm],
        out_specs=vmem,
        scratch_shapes=[
            pltpu.VMEM(latent_dirs.shape, F32),
            pltpu.SemaphoreType.DMA((2,)),
        ],
        compiler_params=pltpu.CompilerParams(vmem_limit_bytes=SEED_LIMIT),
        cost_estimate=cost(4),
    )(queries, latent_ids.T, latent_acts.T, latent_dirs)


class Place:
    def __init__(self, pos_ref):
        ctx = lax.axis_index("ctx")
        tokens = ROWS * lax.axis_size("ctx")
        first = pos_ref[0]
        member = ctx % TEAM
        self.core = member % 2
        self.begin = jnp.where(first < tokens // 2, -first, tokens - first)
        self.wrap = [jnp.where(member + u >= TEAM, 1, 0) for u in range(TEAM)]
        self.slot = [0, 1 + 2 * self.core, 2, 3 - 2 * self.core]

    def pick(self, u, values):
        out = values[0]
        for index in range(1, TEAM):
            out = jnp.where(u == index, values[index], out)
        return out

    def slot_wrap(self, slot):
        if slot == 0:
            return 0
        if slot == 2:
            return self.wrap[2]
        near, away = self.wrap[slot], self.wrap[TEAM - slot]
        return jnp.where(self.core == 0, near, away)

    def slot_offset(self, slot):
        if slot == 0:
            return 0
        member = 2 if slot == 2 else jnp.where(self.core == 0, slot, TEAM - slot)
        return ROWS * member - TEAM * ROWS * self.slot_wrap(slot)


def mask_of(kind, keys):
    name, shift = kind
    key = lax.broadcasted_iota(jnp.int32, (keys, WIDE), 0)
    query = lax.broadcasted_iota(jnp.int32, (keys, WIDE), 1) % TILE
    if name == "causal":
        return key <= query + shift
    return key >= query + shift


def block_jobs(u, t):
    if (u, t) == (0, 0):
        return [(at, 0, (at + 1) * TILE, ("causal", at * TILE)) for at in range(TILES)]
    if (u, t) == (2, 2):
        return [(0, 0, ROWS, None), (1, 0, ROWS, None), (2, 0, ROWS, ("tail", 1))]
    if (u, t) == (3, 2):
        return [(0, TILE, 2 * TILE, ("tail", 1)), (1, 2 * TILE, TILE, ("tail", 1))]
    return [(at, 0, ROWS, None) for at in range(TILES)]


def fill_queries(place, slots, qs_refs, qx_ref, sn_ref):
    lane = lax.broadcasted_iota(jnp.int32, (TILE, DIM), 1)
    row = lax.broadcasted_iota(jnp.int32, (TILE, DIM), 0)
    for index, slot in enumerate(slots):
        for at in range(TILES):
            n = index * TILES + at
            after = row + at * TILE + place.slot_offset(slot) >= place.begin
            flag = jnp.where((lane == 0) & after, 1.0, 0.0).astype(BF16)
            for h in range(HEADS):
                cut = (slice(at * TILE, (at + 1) * TILE), slice(h * DIM, (h + 1) * DIM))
                into = slice(h * TILE, (h + 1) * TILE)
                seed_cut = (slice(ROWS + at * TILE, ROWS + (at + 1) * TILE), cut[1])
                qx_ref[n, into, :DIM] = qs_refs[index][cut]
                qx_ref[n, into, DIM:] = flag
                sn_ref[n, into] = qs_refs[index][seed_cut]


SMEM = pl.BlockSpec(memory_space=pltpu.SMEM)
VMEM = pl.BlockSpec(memory_space=pltpu.VMEM)
ANY = pl.BlockSpec(memory_space=pl.ANY)


def keys_kernel(ds, pos_ref, *refs):
    kv_refs = refs[: len(ds)]
    kx_ref, v_ref, kt_ref = refs[-3:]
    place = Place(pos_ref)
    lane = lax.broadcasted_iota(jnp.int32, (ROWS, DIM), 1)
    row = lax.broadcasted_iota(jnp.int32, (ROWS, DIM), 0)
    for c, (d, kv_ref) in enumerate(zip(ds, kv_refs)):
        before = row - TEAM * ROWS * d < place.begin
        kx_ref[c, :, :DIM] = kv_ref[:ROWS]
        kx_ref[c, :, DIM:] = jnp.where((lane == 0) & before, HIDE, 0.0).astype(BF16)
        v_ref[c] = kv_ref[ROWS:]
        for j in range(TILES):
            kt_ref[c, :, j * TILE : (j + 1) * TILE] = kv_ref[j * TILE : (j + 1) * TILE].T


def keys_of(positions, ds, kvs, micros, after=()):
    shape = jax.ShapeDtypeStruct
    return pl.pallas_call(
        functools.partial(keys_kernel, ds),
        out_shape=(
            shape((len(ds), ROWS, 2 * DIM), BF16),
            shape((len(ds), ROWS, DIM), BF16),
            shape((len(ds), DIM, ROWS), BF16),
        ),
        in_specs=[SMEM] + [VMEM] * len(ds) + [ANY] * len(after),
        out_specs=(VMEM,) * 3,
        compiler_params=pltpu.CompilerParams(vmem_limit_bytes=VMEM_LIMIT),
        cost_estimate=cost(micros),
    )(positions, *[kvs[d] for d in ds], *after)


def stat_job(refs, slot, c, at, j0, keys, kind):
    kx_ref, v_ref, qx_ref, sn_ref, run_ref = refs
    n = slot * TILES + at
    part = slice(j0, j0 + keys)
    s = dot_turned(kx_ref[c, part], qx_ref[n])
    if kind is not None:
        s = jnp.where(mask_of(kind, keys), s, HIDE)
    stat_rows(run_ref, n, s, dot_turned(v_ref[c, part], sn_ref[n]))


def stat_rows(run_ref, n, s, dp):
    old = run_ref[n, 0:1]
    new = jnp.maximum(old, jnp.max(s, axis=0, keepdims=True))
    p = jnp.exp2((s - new) * SCALE)
    fade = jnp.exp2((old - new) * SCALE)
    run_ref[n, 0:1] = new
    run_ref[n, 1:2] = run_ref[n, 1:2] * fade + jnp.sum(p, axis=0, keepdims=True)
    run_ref[n, 2:3] = run_ref[n, 2:3] * fade + jnp.sum(p * dp, axis=0, keepdims=True)


def early_kernel(pos_ref, *refs):
    qs_refs = refs[0:4]
    kx_ref, v_ref, qx_ref, sn_ref, run_ref = refs[4:9]
    work = refs[4:9]
    place = Place(pos_ref)
    fill_queries(place, range(TEAM), qs_refs, qx_ref, sn_ref)
    for n in range(TEAM * TILES):
        run_ref[n, 0:1] = jnp.full((1, WIDE), 2 * HIDE, F32)
        run_ref[n, 1:8] = jnp.zeros((7, WIDE), F32)

    def block(u, t):
        for one in block_jobs(u, t):
            stat_job(work, place.slot[u], t + place.wrap[u], *one)

    def step(k, carry):
        u, t = (k + 1) // 2, (k + 1) % 2
        slot = place.pick(u, place.slot)
        d = t + place.pick(u, place.wrap)
        tiles = [slot * TILES + at for at in range(TILES)]
        scores = [dot_turned(kx_ref[d], qx_ref[n]) for n in tiles]
        dprobs = [dot_turned(v_ref[d], sn_ref[n]) for n in tiles]
        for n, s, dp in zip(tiles, scores, dprobs):
            stat_rows(run_ref, n, s, dp)
        return carry

    lax.fori_loop(0, 7, step, 0)
    block(0, 0)
    block(0, 2)
    for u in range(1, TEAM):
        pl.when(place.wrap[u] == 0)(functools.partial(block, u, 2))


def late_kernel(pos_ref, *refs):
    kx_ref, v_ref, qx_ref, sn_ref, begun_ref, stat_ref, run_ref = refs
    work = (kx_ref, v_ref, qx_ref, sn_ref, run_ref)
    place = Place(pos_ref)
    run_ref[...] = begun_ref[...]

    def block(u):
        for one in block_jobs(u, 2):
            stat_job(work, place.slot[u], 1, *one)

    for u in range(1, TEAM):
        pl.when(place.wrap[u] == 1)(functools.partial(block, u))
    for slot in range(TEAM):
        for at in range(TILES):
            n = slot * TILES + at
            total = run_ref[n, 1:2]
            stat_ref[slot, at : at + 1] = run_ref[n, 0:1] * SCALE + jnp.log2(total)
            stat_ref[slot, 3 + at : 4 + at] = run_ref[n, 2:3] / total
        stat_ref[slot, 6:8] = jnp.zeros((2, WIDE), F32)


def early_stats(positions, slots, keys, values):
    shape = jax.ShapeDtypeStruct
    blocks = TEAM * TILES
    return pl.pallas_call(
        early_kernel,
        out_shape=(
            shape((blocks, WIDE, 2 * DIM), BF16),
            shape((blocks, WIDE, DIM), BF16),
            shape((blocks, 8, WIDE), F32),
        ),
        in_specs=[SMEM] + [VMEM] * 6,
        out_specs=(VMEM,) * 3,
        compiler_params=pltpu.CompilerParams(vmem_limit_bytes=VMEM_LIMIT),
        cost_estimate=cost(12),
    )(positions, *slots, keys, values)


def late_stats(positions, keys, values, qx, sn, run):
    return pl.pallas_call(
        late_kernel,
        out_shape=jax.ShapeDtypeStruct((TEAM, 8, WIDE), F32),
        in_specs=[SMEM] + [VMEM] * 5,
        out_specs=VMEM,
        scratch_shapes=[pltpu.VMEM((TEAM * TILES, 8, WIDE), F32)],
        compiler_params=pltpu.CompilerParams(vmem_limit_bytes=VMEM_LIMIT),
        cost_estimate=cost(4),
    )(positions, keys, values, qx, sn, run)


def fill_stats(slots, stat_refs, row_ref):
    for index, slot in enumerate(slots):
        for at in range(TILES):
            n = index * TILES + at
            sums = [stat_refs[e][slot ^ e, at : at + 1] for e in range(TEAM)]
            deltas = [stat_refs[e][slot ^ e, 3 + at : 4 + at] for e in range(TEAM)]
            top = functools.reduce(jnp.maximum, sums)
            weights = [jnp.exp2(one - top) for one in sums]
            total = sum(weights)
            row_ref[n, 0:1] = top + jnp.log2(total)
            row_ref[n, 1:2] = sum(w * x for w, x in zip(weights, deltas)) / total


def grad_jobs(refs, base, jobs, first=0):
    kx_ref, v_ref, kt_ref, qx_ref, sn_ref, row_ref, dq_ref, dk_ref, dv_ref = refs

    def products(n, d, at, j0, keys, kind):
        part = slice(j0, j0 + keys)
        return dot_turned(kx_ref[d, part], qx_ref[n]), dot_turned(v_ref[d, part], sn_ref[n])

    ready = products(*jobs[0])
    dk = dv = None
    for index, (n, d, at, j0, keys, kind) in enumerate(jobs):
        part = slice(j0, j0 + keys)
        logits, dp = ready
        if index + 1 < len(jobs):
            ready = products(*jobs[index + 1])
        p = jnp.exp2(logits * SCALE - row_ref[n, 0:1])
        if kind is not None:
            p = jnp.where(mask_of(kind, keys), p, 0.0)
        ds = (p * (dp - row_ref[n, 1:2])).astype(BF16)
        more_v, more_k = dot(p.astype(BF16), sn_ref[n]), dot(ds, qx_ref[n, :, :DIM])
        dq_ref[n - first] += dot(kt_ref[d, :, part], ds)
        if keys == ROWS:
            dv = more_v if dv is None else dv + more_v
            dk = more_k if dk is None else dk + more_k
        else:
            dv_ref[d - base, part] += more_v
            dk_ref[d - base, part] += more_k
    if dv is not None:
        dv_ref[d - base] += dv
        dk_ref[d - base] += dk


def put_sums(ref, dk, dv):
    ref[:ROWS] = (dk * FACTOR).astype(ref.dtype)
    ref[ROWS:] = dv.astype(ref.dtype)


def put_queries(ref, dq_ref, first):
    for at in range(TILES):
        for h in range(HEADS):
            part = dq_ref[first + at, :, h * TILE : (h + 1) * TILE] * FACTOR
            ref[at * TILE : (at + 1) * TILE, h * DIM : (h + 1) * DIM] = part.T.astype(ref.dtype)


def grad_call(body, positions, blocks, shards, operands, outs, micros):
    return pl.pallas_call(
        body,
        out_shape=outs,
        in_specs=[SMEM] + [VMEM] * len(operands),
        out_specs=(VMEM,) * len(outs),
        scratch_shapes=[
            pltpu.VMEM((blocks, DIM, WIDE), F32),
            pltpu.VMEM((shards, ROWS, DIM), F32),
            pltpu.VMEM((shards, ROWS, DIM), F32),
        ],
        compiler_params=pltpu.CompilerParams(vmem_limit_bytes=VMEM_LIMIT),
        cost_estimate=cost(micros),
    )(positions, *operands)


HALF = 2 * TILES
HELD = jax.ShapeDtypeStruct((HALF, DIM, WIDE), F32)
SUMS = jax.ShapeDtypeStruct((2, ROWS, DIM), F32)
SEND = jax.ShapeDtypeStruct((2 * ROWS, DIM), BF16)
ROW = jax.ShapeDtypeStruct((TEAM * TILES, 8, WIDE), F32)


def farthest_kernel(pos_ref, *refs):
    stat_refs, keys, (qx_ref, sn_ref) = refs[0:4], refs[4:7], refs[7:9]
    send_ref, row_ref, dq_ref = refs[9:12]
    dk_ref, dv_ref = refs[12:14]
    work = (*keys, qx_ref, sn_ref, row_ref, dq_ref, dk_ref, dv_ref)
    place = Place(pos_ref)
    fill_stats(range(TEAM), stat_refs, row_ref)
    for ref in (dq_ref, dk_ref, dv_ref):
        ref[...] = jnp.zeros_like(ref)

    def block(u):
        grad_jobs(work, 1, [(place.slot[u] * TILES + one[0], 1, *one) for one in block_jobs(u, 2)])

    for u in range(1, TEAM):
        pl.when(place.wrap[u] == 1)(functools.partial(block, u))
    put_sums(send_ref, dk_ref[0], dv_ref[0])


def far_kernel(pos_ref, *refs):
    keys, (qx_ref, sn_ref, row_ref, held_ref) = refs[0:3], refs[3:7]
    near_ref, away_ref, send_ref = refs[7:10]
    dq_ref, dk_ref, dv_ref = refs[10:13]
    work = (*keys, qx_ref, sn_ref, row_ref, dq_ref, dk_ref, dv_ref)
    place = Place(pos_ref)
    dq_ref[...] = held_ref[...]
    dk_ref[...] = jnp.zeros_like(dk_ref)
    dv_ref[...] = jnp.zeros_like(dv_ref)

    def block(u, t):
        grad_jobs(work, 0, [(place.slot[u] * TILES + one[0], 0, *one) for one in block_jobs(u, t)])

    block(0, 2)
    for u in range(1, TEAM):
        pl.when(place.wrap[u] == 0)(functools.partial(block, u, 2))
        pl.when(place.wrap[u] == 1)(functools.partial(block, u, 1))
    near_ref[...] = dq_ref[:HALF]
    away_ref[...] = dq_ref[HALF:]
    put_sums(send_ref, dk_ref[0], dv_ref[0])


def away_kernel(pos_ref, *refs):
    held_ref, dq_far_ref, dq_both_ref, sums0_ref, sums1_ref = refs[6:11]
    dq_ref, dk_ref, dv_ref = refs[11:14]
    work = refs[0:6] + refs[11:14]
    place = Place(pos_ref)
    dq_ref[...] = held_ref[...]
    dk_ref[...] = jnp.zeros_like(dk_ref)
    dv_ref[...] = jnp.zeros_like(dv_ref)

    def block(index, d):
        jobs = [(HALF + index * TILES + one[0], d, *one) for one in block_jobs(1, 0)]
        grad_jobs(work, 0, jobs, HALF)

    for index in range(2):
        block(index, 1)
    for index in range(2):
        pl.when(place.slot_wrap(2 + index) == 0)(functools.partial(block, index, 0))
    put_queries(dq_far_ref, dq_ref, 0)
    put_queries(dq_both_ref, dq_ref, TILES)
    for d, ref in enumerate((sums0_ref, sums1_ref)):
        ref[0] = dk_ref[d]
        ref[1] = dv_ref[d]


def near_kernel(pos_ref, *refs):
    held_ref, sums_ref, _, out_ref, send_ref = refs[6:11]
    dq_ref, dk_ref, dv_ref = refs[11:14]
    work = refs[0:6] + refs[11:14]
    dq_ref[...] = held_ref[...]
    dk_ref[0] = sums_ref[0]
    dv_ref[0] = sums_ref[1]
    for index in range(2):
        grad_jobs(work, 1, [(index * TILES + one[0], 1, *one) for one in block_jobs(1, 0)])
    out_ref[...] = dq_ref[...]
    put_sums(send_ref, dk_ref[0], dv_ref[0])


def own_kernel(pos_ref, *refs):
    held_ref, sums_ref, _, dq_own_ref, dq_core_ref, kv_ref = refs[6:12]
    dq_ref, dk_ref, dv_ref = refs[12:15]
    work = refs[0:6] + refs[12:15]
    place = Place(pos_ref)
    dq_ref[...] = held_ref[...]
    dk_ref[0] = sums_ref[0]
    dv_ref[0] = sums_ref[1]

    def other():
        grad_jobs(work, 0, [(TILES + one[0], 0, *one) for one in block_jobs(1, 0)])

    grad_jobs(work, 0, [(one[0], 0, *one) for one in block_jobs(0, 0)])
    pl.when(place.slot_wrap(1) == 0)(other)
    put_queries(dq_own_ref, dq_ref, 0)
    put_queries(dq_core_ref, dq_ref, TILES)
    put_sums(kv_ref, dk_ref[0], dv_ref[0])


def team_slots(value):
    core = permute(value, lambda s: s ^ 1)
    far = permute(value, lambda s: s ^ 2)
    both = permute(far, lambda s: s ^ 1)
    return [value, core, far, both]


def per_device(queries, key_rows, value_rows, positions, latent_ids, latent_acts, latent_dirs):
    kv = jnp.concatenate([key_rows, value_rows], axis=0)
    kvs = [kv] + [permute(kv, lambda s, d=d: s + TEAM * d) for d in (1, 2)]
    kvs.append(permute(kvs[2], lambda s: s + TEAM))
    qs = team_slots(with_seeds(queries, latent_ids, latent_acts, latent_dirs))
    early = keys_of(positions, (0, 1, 2), kvs, EARLY_COST)
    qx, sn, run = early_stats(positions, qs, *early[:2])
    late = keys_of(positions, (2, 3), kvs, LATE_COST, (run,))
    stat = late_stats(positions, *late[:2], qx, sn, run)
    stats = [stat] + [permute(stat, lambda s, e=e: s ^ e) for e in range(1, TEAM)]

    shape = jax.ShapeDtypeStruct
    wide, thin = (ROWS, HEADS * DIM), (2 * ROWS, DIM)
    send3, rows, held = pl.pallas_call(
        farthest_kernel,
        out_shape=(SEND, ROW, shape((TEAM * TILES, DIM, WIDE), F32)),
        in_specs=[SMEM] + [VMEM] * 9,
        out_specs=(VMEM,) * 3,
        scratch_shapes=[pltpu.VMEM((1, ROWS, DIM), F32)] * 2,
        compiler_params=pltpu.CompilerParams(vmem_limit_bytes=VMEM_LIMIT),
        cost_estimate=cost(FAR_COST),
    )(positions, *stats, *late, qx, sn)
    held_near, held_away, send2 = grad_call(
        far_kernel,
        positions,
        TEAM * TILES,
        1,
        (*late, qx, sn, rows, held),
        (HELD, HELD, shape(thin, F32)),
        FAR_COST,
    )

    def call(body, shards, extra, outs, micros):
        operands = (*early, qx, sn, rows, *extra)
        return grad_call(body, positions, HALF, shards, operands, outs, micros)

    send3 = permute(send3, lambda s: s - TEAM)
    send2 = (send2 + send3.astype(F32)).astype(BF16)
    back2 = permute(send2, lambda s: s - 2 * TEAM)
    dq_far, dq_both, sums0, sums1 = call(
        away_kernel, 2, (held_away,), (shape(wide, F32), shape(wide, BF16), SUMS, SUMS), GRAD_COST
    )
    dq_both = permute(dq_both, lambda s: s ^ 1)
    held_near, send1 = call(near_kernel, 1, (held_near, sums1, send2), (HELD, SEND), GRAD_COST)
    back1 = permute(send1, lambda s: s - TEAM)
    dq_far = (dq_far + dq_both.astype(F32)).astype(BF16)
    dq_back = permute(dq_far, lambda s: s ^ 2)
    dq_own, dq_core, kv_own = call(
        own_kernel,
        1,
        (held_near, sums0, dq_far),
        (shape(wide, F32), shape(wide, BF16), shape(thin, F32)),
        GRAD_COST,
    )
    dq_core = permute(dq_core, lambda s: s ^ 1)
    grad_q = (dq_own + dq_core.astype(F32) + dq_back.astype(F32)).astype(BF16)
    grad_kv = kv_own + back1.astype(F32) + back2.astype(F32)
    return grad_q, grad_kv[:ROWS].astype(BF16), grad_kv[ROWS:].astype(BF16)


def solution(mesh):
    in_specs = (
        P(("mp", "ctx"), None),
        P(("mp", "ctx"), None),
        P(("mp", "ctx"), None),
        P("ctx"),
        P(("mp", "ctx"), None),
        P(("mp", "ctx"), None),
        P("mp", None),
    )
    out_specs = (P(("mp", "ctx"), None), P(("mp", "ctx"), None), P(("mp", "ctx"), None))
    return jax.shard_map(
        per_device, mesh=mesh, in_specs=in_specs, out_specs=out_specs, check_vma=False
    )
```

```python
import functools
import math

import jax
import jax.numpy as jnp
from jax import lax
from jax.experimental import pallas as pl
from jax.experimental.pallas import tpu as pltpu
from jax.sharding import PartitionSpec as P

TEAM = 4
ROWS = 384
TILES = 3
TILE = 128
HEADS = 4
DIM = 128
WIDE = HEADS * TILE
WINDOW = 4096
FACTOR = 1.0 / math.sqrt(DIM)
SCALE = FACTOR * math.log2(math.e)
HIDE = -1e30
VMEM_LIMIT = 28 * 1024 * 1024
SEED_LIMIT = 60 * 1024 * 1024

EARLY_COST = 60
LATE_COST = 1
GRAD_COST = 5
FAR_COST = 5

BF16 = jnp.bfloat16
F32 = jnp.float32


def permute(value, target, members=range(4)):
    count = lax.axis_size("ctx")
    pairs = [(s, target(s) % count) for s in range(count) if s % TEAM in members]
    return lax.ppermute(value, "ctx", pairs)


def dot(a, b):
    return jnp.dot(a, b, preferred_element_type=F32)


def dot_turned(a, b):
    return lax.dot_general(a, b, (((1,), (1,)), ((), ())), preferred_element_type=F32)


def cost(micros):
    return pl.CostEstimate(
        flops=int(micros * 1e9), bytes_accessed=int(micros * 2e6), transcendentals=0
    )


def halves(value):
    high = value.astype(BF16)
    return high, (value - high.astype(F32)).astype(BF16)


def seed_kernel(q_ref, ids_ref, acts_ref, dirs_ref, out_ref, table_ref, sems):
    latents = dirs_ref.shape[0]
    rows = ids_ref.shape[1]
    fetch = pltpu.make_async_copy(dirs_ref, table_ref, sems.at[0])
    fetch.start()
    place = pltpu.make_async_copy(q_ref, out_ref.at[:rows], sems.at[1])
    place.start()
    lane = lax.broadcasted_iota(jnp.int32, (latents, rows), 0)
    mixing = jnp.zeros((latents, rows), F32)
    for k in range(ids_ref.shape[0]):
        mixing = mixing + jnp.where(lane == ids_ref[k : k + 1, :], acts_ref[k : k + 1, :], 0.0)
    mix_high, mix_low = halves(mixing.T)
    fetch.wait()
    dir_high, dir_low = halves(table_ref[...])
    seeds = dot(mix_high, dir_low) + dot(mix_low, dir_high) + dot(mix_high, dir_high)
    out_ref[rows:] = seeds.astype(BF16)
    place.wait()


def with_seeds(queries, latent_ids, latent_acts, latent_dirs):
    vmem = pl.BlockSpec(memory_space=pltpu.VMEM)
    hbm = pl.BlockSpec(memory_space=pl.ANY)
    return pl.pallas_call(
        seed_kernel,
        out_shape=jax.ShapeDtypeStruct((2 * queries.shape[0], queries.shape[1]), BF16),
        in_specs=[hbm, vmem, vmem, hbm],
        out_specs=vmem,
        scratch_shapes=[
            pltpu.VMEM(latent_dirs.shape, F32),
            pltpu.SemaphoreType.DMA((2,)),
        ],
        compiler_params=pltpu.CompilerParams(vmem_limit_bytes=SEED_LIMIT),
        cost_estimate=cost(4),
    )(queries, latent_ids.T, latent_acts.T, latent_dirs)


class Place:
    def __init__(self, pos_ref):
        ctx = lax.axis_index("ctx")
        tokens = ROWS * lax.axis_size("ctx")
        first = pos_ref[0]
        member = ctx % TEAM
        self.core = member % 2
        self.begin = jnp.where(first < tokens // 2, -first, tokens - first)
        self.wrap = [jnp.where(member + u >= TEAM, 1, 0) for u in range(TEAM)]
        self.slot = [0, 1 + 2 * self.core, 2, 3 - 2 * self.core]

    def pick(self, u, values):
        out = values[0]
        for index in range(1, TEAM):
            out = jnp.where(u == index, values[index], out)
        return out

    def slot_wrap(self, slot):
        if slot == 0:
            return 0
        if slot == 2:
            return self.wrap[2]
        near, away = self.wrap[slot], self.wrap[TEAM - slot]
        return jnp.where(self.core == 0, near, away)

    def slot_offset(self, slot):
        if slot == 0:
            return 0
        member = 2 if slot == 2 else jnp.where(self.core == 0, slot, TEAM - slot)
        return ROWS * member - TEAM * ROWS * self.slot_wrap(slot)


def mask_of(kind, keys):
    name, shift = kind
    key = lax.broadcasted_iota(jnp.int32, (keys, WIDE), 0)
    query = lax.broadcasted_iota(jnp.int32, (keys, WIDE), 1) % TILE
    if name == "causal":
        return key <= query + shift
    return key >= query + shift


def block_jobs(u, t):
    if (u, t) == (0, 0):
        return [(at, 0, (at + 1) * TILE, ("causal", at * TILE)) for at in range(TILES)]
    if (u, t) == (2, 2):
        return [(0, 0, ROWS, None), (1, 0, ROWS, None), (2, 0, ROWS, ("tail", 1))]
    if (u, t) == (3, 2):
        return [(0, TILE, 2 * TILE, ("tail", 1)), (1, 2 * TILE, TILE, ("tail", 1))]
    return [(at, 0, ROWS, None) for at in range(TILES)]


def fill_queries(place, slots, qs_refs, qx_ref, sn_ref):
    lane = lax.broadcasted_iota(jnp.int32, (TILE, DIM), 1)
    row = lax.broadcasted_iota(jnp.int32, (TILE, DIM), 0)
    for index, slot in enumerate(slots):
        for at in range(TILES):
            n = index * TILES + at
            after = row + at * TILE + place.slot_offset(slot) >= place.begin
            flag = jnp.where((lane == 0) & after, 1.0, 0.0).astype(BF16)
            for h in range(HEADS):
                cut = (slice(at * TILE, (at + 1) * TILE), slice(h * DIM, (h + 1) * DIM))
                into = slice(h * TILE, (h + 1) * TILE)
                seed_cut = (slice(ROWS + at * TILE, ROWS + (at + 1) * TILE), cut[1])
                qx_ref[n, into, :DIM] = qs_refs[index][cut]
                qx_ref[n, into, DIM:] = flag
                sn_ref[n, into] = qs_refs[index][seed_cut]


SMEM = pl.BlockSpec(memory_space=pltpu.SMEM)
VMEM = pl.BlockSpec(memory_space=pltpu.VMEM)
ANY = pl.BlockSpec(memory_space=pl.ANY)


def keys_kernel(ds, pos_ref, *refs):
    kv_refs = refs[: len(ds)]
    kx_ref, v_ref, kt_ref = refs[-3:]
    place = Place(pos_ref)
    lane = lax.broadcasted_iota(jnp.int32, (ROWS, DIM), 1)
    row = lax.broadcasted_iota(jnp.int32, (ROWS, DIM), 0)
    for c, (d, kv_ref) in enumerate(zip(ds, kv_refs)):
        before = row - TEAM * ROWS * d < place.begin
        kx_ref[c, :, :DIM] = kv_ref[:ROWS]
        kx_ref[c, :, DIM:] = jnp.where((lane == 0) & before, HIDE, 0.0).astype(BF16)
        v_ref[c] = kv_ref[ROWS:]
        for j in range(TILES):
            kt_ref[c, :, j * TILE : (j + 1) * TILE] = kv_ref[j * TILE : (j + 1) * TILE].T


def keys_of(positions, ds, kvs, micros, after=()):
    shape = jax.ShapeDtypeStruct
    return pl.pallas_call(
        functools.partial(keys_kernel, ds),
        out_shape=(
            shape((len(ds), ROWS, 2 * DIM), BF16),
            shape((len(ds), ROWS, DIM), BF16),
            shape((len(ds), DIM, ROWS), BF16),
        ),
        in_specs=[SMEM] + [VMEM] * len(ds) + [ANY] * len(after),
        out_specs=(VMEM,) * 3,
        compiler_params=pltpu.CompilerParams(vmem_limit_bytes=VMEM_LIMIT),
        cost_estimate=cost(micros),
    )(positions, *[kvs[d] for d in ds], *after)


def stat_job(refs, slot, c, at, j0, keys, kind):
    kx_ref, v_ref, qx_ref, sn_ref, run_ref = refs
    n = slot * TILES + at
    part = slice(j0, j0 + keys)
    s = dot_turned(kx_ref[c, part], qx_ref[n])
    if kind is not None:
        s = jnp.where(mask_of(kind, keys), s, HIDE)
    stat_rows(run_ref, n, s, dot_turned(v_ref[c, part], sn_ref[n]))


def stat_rows(run_ref, n, s, dp):
    old = run_ref[n, 0:1]
    new = jnp.maximum(old, jnp.max(s, axis=0, keepdims=True))
    p = jnp.exp2((s - new) * SCALE)
    fade = jnp.exp2((old - new) * SCALE)
    run_ref[n, 0:1] = new
    run_ref[n, 1:2] = run_ref[n, 1:2] * fade + jnp.sum(p, axis=0, keepdims=True)
    run_ref[n, 2:3] = run_ref[n, 2:3] * fade + jnp.sum(p * dp, axis=0, keepdims=True)


def early_kernel(pos_ref, *refs):
    qs_refs = refs[0:4]
    kx_ref, v_ref, qx_ref, sn_ref, run_ref = refs[4:9]
    work = refs[4:9]
    place = Place(pos_ref)
    fill_queries(place, range(TEAM), qs_refs, qx_ref, sn_ref)
    for n in range(TEAM * TILES):
        run_ref[n, 0:1] = jnp.full((1, WIDE), 2 * HIDE, F32)
        run_ref[n, 1:8] = jnp.zeros((7, WIDE), F32)

    def block(u, t):
        for one in block_jobs(u, t):
            stat_job(work, place.slot[u], t + place.wrap[u], *one)

    def step(k, carry):
        u, t = (k + 1) // 2, (k + 1) % 2
        slot = place.pick(u, place.slot)
        d = t + place.pick(u, place.wrap)
        tiles = [slot * TILES + at for at in range(TILES)]
        scores = [dot_turned(kx_ref[d], qx_ref[n]) for n in tiles]
        dprobs = [dot_turned(v_ref[d], sn_ref[n]) for n in tiles]
        for n, s, dp in zip(tiles, scores, dprobs):
            stat_rows(run_ref, n, s, dp)
        return carry

    lax.fori_loop(0, 7, step, 0)
    block(0, 0)
    block(0, 2)
    for u in range(1, TEAM):
        pl.when(place.wrap[u] == 0)(functools.partial(block, u, 2))


def late_kernel(pos_ref, *refs):
    kx_ref, v_ref, qx_ref, sn_ref, begun_ref, stat_ref, run_ref = refs
    work = (kx_ref, v_ref, qx_ref, sn_ref, run_ref)
    place = Place(pos_ref)
    run_ref[...] = begun_ref[...]

    def block(u):
        for one in block_jobs(u, 2):
            stat_job(work, place.slot[u], 1, *one)

    for u in range(1, TEAM):
        pl.when(place.wrap[u] == 1)(functools.partial(block, u))
    for slot in range(TEAM):
        for at in range(TILES):
            n = slot * TILES + at
            total = run_ref[n, 1:2]
            stat_ref[slot, at : at + 1] = run_ref[n, 0:1] * SCALE + jnp.log2(total)
            stat_ref[slot, 3 + at : 4 + at] = run_ref[n, 2:3] / total
        stat_ref[slot, 6:8] = jnp.zeros((2, WIDE), F32)


def early_stats(positions, slots, keys, values):
    shape = jax.ShapeDtypeStruct
    blocks = TEAM * TILES
    return pl.pallas_call(
        early_kernel,
        out_shape=(
            shape((blocks, WIDE, 2 * DIM), BF16),
            shape((blocks, WIDE, DIM), BF16),
            shape((blocks, 8, WIDE), F32),
        ),
        in_specs=[SMEM] + [VMEM] * 6,
        out_specs=(VMEM,) * 3,
        compiler_params=pltpu.CompilerParams(vmem_limit_bytes=VMEM_LIMIT),
        cost_estimate=cost(12),
    )(positions, *slots, keys, values)


def late_stats(positions, keys, values, qx, sn, run):
    return pl.pallas_call(
        late_kernel,
        out_shape=jax.ShapeDtypeStruct((TEAM, 8, WIDE), F32),
        in_specs=[SMEM] + [VMEM] * 5,
        out_specs=VMEM,
        scratch_shapes=[pltpu.VMEM((TEAM * TILES, 8, WIDE), F32)],
        compiler_params=pltpu.CompilerParams(vmem_limit_bytes=VMEM_LIMIT),
        cost_estimate=cost(4),
    )(positions, keys, values, qx, sn, run)


def fill_stats(slots, stat_refs, row_ref):
    for index, slot in enumerate(slots):
        for at in range(TILES):
            n = index * TILES + at
            sums = [stat_refs[e][slot ^ e, at : at + 1] for e in range(TEAM)]
            deltas = [stat_refs[e][slot ^ e, 3 + at : 4 + at] for e in range(TEAM)]
            top = functools.reduce(jnp.maximum, sums)
            weights = [jnp.exp2(one - top) for one in sums]
            total = sum(weights)
            row_ref[n, 0:1] = top + jnp.log2(total)
            row_ref[n, 1:2] = sum(w * x for w, x in zip(weights, deltas)) / total


def grad_jobs(refs, base, jobs, first=0):
    kx_ref, v_ref, kt_ref, qx_ref, sn_ref, row_ref, dq_ref, dk_ref, dv_ref = refs

    def products(n, d, at, j0, keys, kind):
        part = slice(j0, j0 + keys)
        return dot_turned(kx_ref[d, part], qx_ref[n]), dot_turned(v_ref[d, part], sn_ref[n])

    ready = products(*jobs[0])
    dk = dv = None
    for index, (n, d, at, j0, keys, kind) in enumerate(jobs):
        part = slice(j0, j0 + keys)
        logits, dp = ready
        if index + 1 < len(jobs):
            ready = products(*jobs[index + 1])
        p = jnp.exp2(logits * SCALE - row_ref[n, 0:1])
        if kind is not None:
            p = jnp.where(mask_of(kind, keys), p, 0.0)
        ds = (p * (dp - row_ref[n, 1:2])).astype(BF16)
        more_v, more_k = dot(p.astype(BF16), sn_ref[n]), dot(ds, qx_ref[n, :, :DIM])
        dq_ref[n - first] += dot(kt_ref[d, :, part], ds)
        if keys == ROWS:
            dv = more_v if dv is None else dv + more_v
            dk = more_k if dk is None else dk + more_k
        else:
            dv_ref[d - base, part] += more_v
            dk_ref[d - base, part] += more_k
    if dv is not None:
        dv_ref[d - base] += dv
        dk_ref[d - base] += dk


def put_sums(ref, dk, dv):
    ref[:ROWS] = (dk * FACTOR).astype(ref.dtype)
    ref[ROWS:] = dv.astype(ref.dtype)


def put_queries(ref, dq_ref, first):
    for at in range(TILES):
        for h in range(HEADS):
            part = dq_ref[first + at, :, h * TILE : (h + 1) * TILE] * FACTOR
            ref[at * TILE : (at + 1) * TILE, h * DIM : (h + 1) * DIM] = part.T.astype(ref.dtype)


def grad_call(body, positions, blocks, shards, operands, outs, micros):
    return pl.pallas_call(
        body,
        out_shape=outs,
        in_specs=[SMEM] + [VMEM] * len(operands),
        out_specs=(VMEM,) * len(outs),
        scratch_shapes=[
            pltpu.VMEM((blocks, DIM, WIDE), F32),
            pltpu.VMEM((shards, ROWS, DIM), F32),
            pltpu.VMEM((shards, ROWS, DIM), F32),
        ],
        compiler_params=pltpu.CompilerParams(vmem_limit_bytes=VMEM_LIMIT),
        cost_estimate=cost(micros),
    )(positions, *operands)


HALF = 2 * TILES
HELD = jax.ShapeDtypeStruct((HALF, DIM, WIDE), F32)
SUMS = jax.ShapeDtypeStruct((2, ROWS, DIM), F32)
SEND = jax.ShapeDtypeStruct((2 * ROWS, DIM), BF16)
ROW = jax.ShapeDtypeStruct((TEAM * TILES, 8, WIDE), F32)


def farthest_kernel(pos_ref, *refs):
    stat_refs, keys, (qx_ref, sn_ref) = refs[0:4], refs[4:7], refs[7:9]
    send_ref, row_ref, dq_ref = refs[9:12]
    dk_ref, dv_ref = refs[12:14]
    work = (*keys, qx_ref, sn_ref, row_ref, dq_ref, dk_ref, dv_ref)
    place = Place(pos_ref)
    fill_stats(range(TEAM), stat_refs, row_ref)
    for ref in (dq_ref, dk_ref, dv_ref):
        ref[...] = jnp.zeros_like(ref)

    def block(u):
        grad_jobs(work, 1, [(place.slot[u] * TILES + one[0], 1, *one) for one in block_jobs(u, 2)])

    for u in range(1, TEAM):
        pl.when(place.wrap[u] == 1)(functools.partial(block, u))
    put_sums(send_ref, dk_ref[0], dv_ref[0])


def far_kernel(pos_ref, *refs):
    keys, (qx_ref, sn_ref, row_ref, held_ref) = refs[0:3], refs[3:7]
    near_ref, away_ref, send_ref = refs[7:10]
    dq_ref, dk_ref, dv_ref = refs[10:13]
    work = (*keys, qx_ref, sn_ref, row_ref, dq_ref, dk_ref, dv_ref)
    place = Place(pos_ref)
    dq_ref[...] = held_ref[...]
    dk_ref[...] = jnp.zeros_like(dk_ref)
    dv_ref[...] = jnp.zeros_like(dv_ref)

    def block(u, t):
        grad_jobs(work, 0, [(place.slot[u] * TILES + one[0], 0, *one) for one in block_jobs(u, t)])

    block(0, 2)
    for u in range(1, TEAM):
        pl.when(place.wrap[u] == 0)(functools.partial(block, u, 2))
        pl.when(place.wrap[u] == 1)(functools.partial(block, u, 1))
    near_ref[...] = dq_ref[:HALF]
    away_ref[...] = dq_ref[HALF:]
    put_sums(send_ref, dk_ref[0], dv_ref[0])


def away_kernel(pos_ref, *refs):
    held_ref, dq_far_ref, dq_both_ref, sums0_ref, sums1_ref = refs[6:11]
    dq_ref, dk_ref, dv_ref = refs[11:14]
    work = refs[0:6] + refs[11:14]
    place = Place(pos_ref)
    dq_ref[...] = held_ref[...]
    dk_ref[...] = jnp.zeros_like(dk_ref)
    dv_ref[...] = jnp.zeros_like(dv_ref)

    def block(index, d):
        jobs = [(HALF + index * TILES + one[0], d, *one) for one in block_jobs(1, 0)]
        grad_jobs(work, 0, jobs, HALF)

    for index in range(2):
        block(index, 1)
    for index in range(2):
        pl.when(place.slot_wrap(2 + index) == 0)(functools.partial(block, index, 0))
    put_queries(dq_far_ref, dq_ref, 0)
    put_queries(dq_both_ref, dq_ref, TILES)
    for d, ref in enumerate((sums0_ref, sums1_ref)):
        ref[0] = dk_ref[d]
        ref[1] = dv_ref[d]


def near_kernel(pos_ref, *refs):
    held_ref, sums_ref, _, out_ref, send_ref = refs[6:11]
    dq_ref, dk_ref, dv_ref = refs[11:14]
    work = refs[0:6] + refs[11:14]
    dq_ref[...] = held_ref[...]
    dk_ref[0] = sums_ref[0]
    dv_ref[0] = sums_ref[1]
    for index in range(2):
        grad_jobs(work, 1, [(index * TILES + one[0], 1, *one) for one in block_jobs(1, 0)])
    out_ref[...] = dq_ref[...]
    put_sums(send_ref, dk_ref[0], dv_ref[0])


def own_kernel(pos_ref, *refs):
    held_ref, sums_ref, _, dq_own_ref, dq_core_ref, kv_ref = refs[6:12]
    dq_ref, dk_ref, dv_ref = refs[12:15]
    work = refs[0:6] + refs[12:15]
    place = Place(pos_ref)
    dq_ref[...] = held_ref[...]
    dk_ref[0] = sums_ref[0]
    dv_ref[0] = sums_ref[1]

    def other():
        grad_jobs(work, 0, [(TILES + one[0], 0, *one) for one in block_jobs(1, 0)])

    grad_jobs(work, 0, [(one[0], 0, *one) for one in block_jobs(0, 0)])
    pl.when(place.slot_wrap(1) == 0)(other)
    put_queries(dq_own_ref, dq_ref, 0)
    put_queries(dq_core_ref, dq_ref, TILES)
    put_sums(kv_ref, dk_ref[0], dv_ref[0])


def team_slots(value):
    core = permute(value, lambda s: s ^ 1)
    far = permute(value, lambda s: s ^ 2)
    both = permute(far, lambda s: s ^ 1)
    return [value, core, far, both]


def per_device(queries, key_rows, value_rows, positions, latent_ids, latent_acts, latent_dirs):
    kv = jnp.concatenate([key_rows, value_rows], axis=0)
    kvs = [kv] + [permute(kv, lambda s, d=d: s + TEAM * d) for d in (1, 2)]
    kvs.append(permute(kvs[2], lambda s: s + TEAM, (1, 2, 3)))
    qs = team_slots(with_seeds(queries, latent_ids, latent_acts, latent_dirs))
    early = keys_of(positions, (0, 1, 2), kvs, EARLY_COST)
    qx, sn, run = early_stats(positions, qs, *early[:2])
    late = keys_of(positions, (2, 3), kvs, LATE_COST, (run,))
    stat = late_stats(positions, *late[:2], qx, sn, run)
    stats = [stat] + [permute(stat, lambda s, e=e: s ^ e) for e in range(1, TEAM)]

    shape = jax.ShapeDtypeStruct
    wide, thin = (ROWS, HEADS * DIM), (2 * ROWS, DIM)
    send3, rows, held = pl.pallas_call(
        farthest_kernel,
        out_shape=(SEND, ROW, shape((TEAM * TILES, DIM, WIDE), F32)),
        in_specs=[SMEM] + [VMEM] * 9,
        out_specs=(VMEM,) * 3,
        scratch_shapes=[pltpu.VMEM((1, ROWS, DIM), F32)] * 2,
        compiler_params=pltpu.CompilerParams(vmem_limit_bytes=VMEM_LIMIT),
        cost_estimate=cost(FAR_COST),
    )(positions, *stats, *late, qx, sn)
    held_near, held_away, send2 = grad_call(
        far_kernel,
        positions,
        TEAM * TILES,
        1,
        (*late, qx, sn, rows, held),
        (HELD, HELD, shape(thin, F32)),
        FAR_COST,
    )

    def call(body, shards, extra, outs, micros):
        operands = (*early, qx, sn, rows, *extra)
        return grad_call(body, positions, HALF, shards, operands, outs, micros)

    send3 = permute(send3, lambda s: s - TEAM, (1, 2, 3))
    send2 = (send2 + send3.astype(F32)).astype(BF16)
    back2 = permute(send2, lambda s: s - 2 * TEAM)
    dq_far, dq_both, sums0, sums1 = call(
        away_kernel, 2, (held_away,), (shape(wide, F32), shape(wide, BF16), SUMS, SUMS), GRAD_COST
    )
    dq_both = permute(dq_both, lambda s: s ^ 1)
    held_near, send1 = call(near_kernel, 1, (held_near, sums1, send2), (HELD, SEND), GRAD_COST)
    back1 = permute(send1, lambda s: s - TEAM)
    dq_far = (dq_far + dq_both.astype(F32)).astype(BF16)
    dq_back = permute(dq_far, lambda s: s ^ 2)
    dq_own, dq_core, kv_own = call(
        own_kernel,
        1,
        (held_near, sums0, dq_far),
        (shape(wide, F32), shape(wide, BF16), shape(thin, F32)),
        GRAD_COST,
    )
    dq_core = permute(dq_core, lambda s: s ^ 1)
    grad_q = (dq_own + dq_core.astype(F32) + dq_back.astype(F32)).astype(BF16)
    grad_kv = kv_own + back1.astype(F32) + back2.astype(F32)
    return grad_q, grad_kv[:ROWS].astype(BF16), grad_kv[ROWS:].astype(BF16)


def solution(mesh):
    in_specs = (
        P(("mp", "ctx"), None),
        P(("mp", "ctx"), None),
        P(("mp", "ctx"), None),
        P("ctx"),
        P(("mp", "ctx"), None),
        P(("mp", "ctx"), None),
        P("mp", None),
    )
    out_specs = (P(("mp", "ctx"), None), P(("mp", "ctx"), None), P(("mp", "ctx"), None))
    return jax.shard_map(
        per_device, mesh=mesh, in_specs=in_specs, out_specs=out_specs, check_vma=False
    )
```

```python
import functools
import math

import jax
import jax.numpy as jnp
from jax import lax
from jax.experimental import pallas as pl
from jax.experimental.pallas import tpu as pltpu
from jax.sharding import PartitionSpec as P

TEAM = 4
ROWS = 384
TILES = 3
TILE = 128
HEADS = 4
DIM = 128
WIDE = HEADS * TILE
WINDOW = 4096
FACTOR = 1.0 / math.sqrt(DIM)
SCALE = FACTOR * math.log2(math.e)
HIDE = -1e30
VMEM_LIMIT = 28 * 1024 * 1024
SEED_LIMIT = 60 * 1024 * 1024

EARLY_COST = 60
LATE_COST = 1
GRAD_COST = 5
FAR_COST = 5

BF16 = jnp.bfloat16
F32 = jnp.float32


def permute(value, target):
    count = lax.axis_size("ctx")
    return lax.ppermute(value, "ctx", [(s, target(s) % count) for s in range(count)])


def dot(a, b):
    return jnp.dot(a, b, preferred_element_type=F32)


def dot_turned(a, b):
    return lax.dot_general(a, b, (((1,), (1,)), ((), ())), preferred_element_type=F32)


def cost(micros):
    return pl.CostEstimate(
        flops=int(micros * 1e9), bytes_accessed=int(micros * 2e6), transcendentals=0
    )


def halves(value):
    high = value.astype(BF16)
    return high, (value - high.astype(F32)).astype(BF16)


def seed_kernel(q_ref, ids_ref, acts_ref, dirs_ref, out_ref, table_ref, sems):
    latents = dirs_ref.shape[0]
    rows = ids_ref.shape[1]
    fetch = pltpu.make_async_copy(dirs_ref, table_ref, sems.at[0])
    fetch.start()
    place = pltpu.make_async_copy(q_ref, out_ref.at[:rows], sems.at[1])
    place.start()
    lane = lax.broadcasted_iota(jnp.int32, (latents, rows), 0)
    mixing = jnp.zeros((latents, rows), F32)
    for k in range(ids_ref.shape[0]):
        mixing = mixing + jnp.where(lane == ids_ref[k : k + 1, :], acts_ref[k : k + 1, :], 0.0)
    mix_high, mix_low = halves(mixing.T)
    fetch.wait()
    dir_high, dir_low = halves(table_ref[...])
    seeds = dot(mix_high, dir_low) + dot(mix_low, dir_high) + dot(mix_high, dir_high)
    out_ref[rows:] = seeds.astype(BF16)
    place.wait()


def with_seeds(queries, latent_ids, latent_acts, latent_dirs):
    vmem = pl.BlockSpec(memory_space=pltpu.VMEM)
    hbm = pl.BlockSpec(memory_space=pl.ANY)
    return pl.pallas_call(
        seed_kernel,
        out_shape=jax.ShapeDtypeStruct((2 * queries.shape[0], queries.shape[1]), BF16),
        in_specs=[hbm, vmem, vmem, hbm],
        out_specs=vmem,
        scratch_shapes=[
            pltpu.VMEM(latent_dirs.shape, F32),
            pltpu.SemaphoreType.DMA((2,)),
        ],
        compiler_params=pltpu.CompilerParams(vmem_limit_bytes=SEED_LIMIT),
        cost_estimate=cost(4),
    )(queries, latent_ids.T, latent_acts.T, latent_dirs)


class Place:
    def __init__(self, pos_ref):
        ctx = lax.axis_index("ctx")
        tokens = ROWS * lax.axis_size("ctx")
        first = pos_ref[0]
        member = ctx % TEAM
        self.core = member % 2
        self.begin = jnp.where(first < tokens // 2, -first, tokens - first)
        self.wrap = [jnp.where(member + u >= TEAM, 1, 0) for u in range(TEAM)]
        self.slot = [0, 1 + 2 * self.core, 2, 3 - 2 * self.core]

    def pick(self, u, values):
        out = values[0]
        for index in range(1, TEAM):
            out = jnp.where(u == index, values[index], out)
        return out

    def slot_wrap(self, slot):
        if slot == 0:
            return 0
        if slot == 2:
            return self.wrap[2]
        near, away = self.wrap[slot], self.wrap[TEAM - slot]
        return jnp.where(self.core == 0, near, away)

    def slot_offset(self, slot):
        if slot == 0:
            return 0
        member = 2 if slot == 2 else jnp.where(self.core == 0, slot, TEAM - slot)
        return ROWS * member - TEAM * ROWS * self.slot_wrap(slot)


def mask_of(kind, keys):
    name, shift = kind
    key = lax.broadcasted_iota(jnp.int32, (keys, WIDE), 0)
    query = lax.broadcasted_iota(jnp.int32, (keys, WIDE), 1) % TILE
    if name == "causal":
        return key <= query + shift
    return key >= query + shift


def block_jobs(u, t):
    if (u, t) == (0, 0):
        return [(at, 0, (at + 1) * TILE, ("causal", at * TILE)) for at in range(TILES)]
    if (u, t) == (2, 2):
        return [(0, 0, ROWS, None), (1, 0, ROWS, None), (2, 0, ROWS, ("tail", 1))]
    if (u, t) == (3, 2):
        return [(0, TILE, 2 * TILE, ("tail", 1)), (1, 2 * TILE, TILE, ("tail", 1))]
    return [(at, 0, ROWS, None) for at in range(TILES)]


def fill_queries(place, slots, qs_refs, qx_ref, sn_ref):
    lane = lax.broadcasted_iota(jnp.int32, (TILE, DIM), 1)
    row = lax.broadcasted_iota(jnp.int32, (TILE, DIM), 0)
    for index, slot in enumerate(slots):
        for at in range(TILES):
            n = index * TILES + at
            after = row + at * TILE + place.slot_offset(slot) >= place.begin
            flag = jnp.where((lane == 0) & after, 1.0, 0.0).astype(BF16)
            for h in range(HEADS):
                cut = (slice(at * TILE, (at + 1) * TILE), slice(h * DIM, (h + 1) * DIM))
                into = slice(h * TILE, (h + 1) * TILE)
                seed_cut = (slice(ROWS + at * TILE, ROWS + (at + 1) * TILE), cut[1])
                qx_ref[n, into, :DIM] = qs_refs[index][cut]
                qx_ref[n, into, DIM:] = flag
                sn_ref[n, into] = qs_refs[index][seed_cut]


SMEM = pl.BlockSpec(memory_space=pltpu.SMEM)
VMEM = pl.BlockSpec(memory_space=pltpu.VMEM)
ANY = pl.BlockSpec(memory_space=pl.ANY)


def keys_kernel(ds, pos_ref, *refs):
    kv_refs = refs[: len(ds)]
    kx_ref, v_ref, kt_ref = refs[-3:]
    place = Place(pos_ref)
    lane = lax.broadcasted_iota(jnp.int32, (ROWS, DIM), 1)
    row = lax.broadcasted_iota(jnp.int32, (ROWS, DIM), 0)
    for c, (d, kv_ref) in enumerate(zip(ds, kv_refs)):
        before = row - TEAM * ROWS * d < place.begin
        kx_ref[c, :, :DIM] = kv_ref[:ROWS]
        kx_ref[c, :, DIM:] = jnp.where((lane == 0) & before, HIDE, 0.0).astype(BF16)
        v_ref[c] = kv_ref[ROWS:]
        for j in range(TILES):
            kt_ref[c, :, j * TILE : (j + 1) * TILE] = kv_ref[j * TILE : (j + 1) * TILE].T


def keys_of(positions, ds, kvs, micros, after=()):
    shape = jax.ShapeDtypeStruct
    return pl.pallas_call(
        functools.partial(keys_kernel, ds),
        out_shape=(
            shape((len(ds), ROWS, 2 * DIM), BF16),
            shape((len(ds), ROWS, DIM), BF16),
            shape((len(ds), DIM, ROWS), BF16),
        ),
        in_specs=[SMEM] + [VMEM] * len(ds) + [ANY] * len(after),
        out_specs=(VMEM,) * 3,
        compiler_params=pltpu.CompilerParams(vmem_limit_bytes=VMEM_LIMIT),
        cost_estimate=cost(micros),
    )(positions, *[kvs[d] for d in ds], *after)


def stat_job(refs, slot, c, at, j0, keys, kind):
    kx_ref, v_ref, qx_ref, sn_ref, run_ref = refs
    n = slot * TILES + at
    part = slice(j0, j0 + keys)
    s = dot_turned(kx_ref[c, part], qx_ref[n])
    if kind is not None:
        s = jnp.where(mask_of(kind, keys), s, HIDE)
    stat_rows(run_ref, n, s, dot_turned(v_ref[c, part], sn_ref[n]))


def stat_rows(run_ref, n, s, dp):
    old = run_ref[n, 0:1]
    new = jnp.maximum(old, jnp.max(s, axis=0, keepdims=True))
    p = jnp.exp2((s - new) * SCALE)
    fade = jnp.exp2((old - new) * SCALE)
    run_ref[n, 0:1] = new
    run_ref[n, 1:2] = run_ref[n, 1:2] * fade + jnp.sum(p, axis=0, keepdims=True)
    run_ref[n, 2:3] = run_ref[n, 2:3] * fade + jnp.sum(p * dp, axis=0, keepdims=True)


def early_kernel(pos_ref, *refs):
    qs_refs = refs[0:4]
    kx_ref, v_ref, qx_ref, sn_ref, run_ref = refs[4:9]
    work = refs[4:9]
    place = Place(pos_ref)
    fill_queries(place, range(TEAM), qs_refs, qx_ref, sn_ref)
    for n in range(TEAM * TILES):
        run_ref[n, 0:1] = jnp.full((1, WIDE), 2 * HIDE, F32)
        run_ref[n, 1:8] = jnp.zeros((7, WIDE), F32)

    def block(u, t):
        for one in block_jobs(u, t):
            stat_job(work, place.slot[u], t + place.wrap[u], *one)

    def step(k, carry):
        u, t = (k + 1) // 2, (k + 1) % 2
        slot = place.pick(u, place.slot)
        d = t + place.pick(u, place.wrap)
        tiles = [slot * TILES + at for at in range(TILES)]
        scores = [dot_turned(kx_ref[d], qx_ref[n]) for n in tiles]
        dprobs = [dot_turned(v_ref[d], sn_ref[n]) for n in tiles]
        for n, s, dp in zip(tiles, scores, dprobs):
            stat_rows(run_ref, n, s, dp)
        return carry

    lax.fori_loop(0, 7, step, 0)
    block(0, 0)
    block(0, 2)
    for u in range(1, TEAM):
        pl.when(place.wrap[u] == 0)(functools.partial(block, u, 2))


def late_kernel(pos_ref, *refs):
    kx_ref, v_ref, qx_ref, sn_ref, begun_ref, stat_ref, run_ref = refs
    work = (kx_ref, v_ref, qx_ref, sn_ref, run_ref)
    place = Place(pos_ref)
    run_ref[...] = begun_ref[...]

    def block(u):
        for one in block_jobs(u, 2):
            stat_job(work, place.slot[u], 0, *one)

    for u in range(1, TEAM):
        pl.when(place.wrap[u] == 1)(functools.partial(block, u))
    for slot in range(TEAM):
        for at in range(TILES):
            n = slot * TILES + at
            total = run_ref[n, 1:2]
            stat_ref[slot, at : at + 1] = run_ref[n, 0:1] * SCALE + jnp.log2(total)
            stat_ref[slot, 3 + at : 4 + at] = run_ref[n, 2:3] / total
        stat_ref[slot, 6:8] = jnp.zeros((2, WIDE), F32)


def early_stats(positions, slots, keys, values):
    shape = jax.ShapeDtypeStruct
    blocks = TEAM * TILES
    return pl.pallas_call(
        early_kernel,
        out_shape=(
            shape((blocks, WIDE, 2 * DIM), BF16),
            shape((blocks, WIDE, DIM), BF16),
            shape((blocks, 8, WIDE), F32),
        ),
        in_specs=[SMEM] + [VMEM] * 6,
        out_specs=(VMEM,) * 3,
        compiler_params=pltpu.CompilerParams(vmem_limit_bytes=VMEM_LIMIT),
        cost_estimate=cost(12),
    )(positions, *slots, keys, values)


def late_stats(positions, keys, values, qx, sn, run):
    return pl.pallas_call(
        late_kernel,
        out_shape=jax.ShapeDtypeStruct((TEAM, 8, WIDE), F32),
        in_specs=[SMEM] + [VMEM] * 5,
        out_specs=VMEM,
        scratch_shapes=[pltpu.VMEM((TEAM * TILES, 8, WIDE), F32)],
        compiler_params=pltpu.CompilerParams(vmem_limit_bytes=VMEM_LIMIT),
        cost_estimate=cost(4),
    )(positions, keys, values, qx, sn, run)


def fill_stats(slots, stat_refs, row_ref):
    for index, slot in enumerate(slots):
        for at in range(TILES):
            n = index * TILES + at
            sums = [stat_refs[e][slot ^ e, at : at + 1] for e in range(TEAM)]
            deltas = [stat_refs[e][slot ^ e, 3 + at : 4 + at] for e in range(TEAM)]
            top = functools.reduce(jnp.maximum, sums)
            weights = [jnp.exp2(one - top) for one in sums]
            total = sum(weights)
            row_ref[n, 0:1] = top + jnp.log2(total)
            row_ref[n, 1:2] = sum(w * x for w, x in zip(weights, deltas)) / total


def grad_jobs(refs, base, jobs, first=0):
    kx_ref, v_ref, kt_ref, qx_ref, sn_ref, row_ref, dq_ref, dk_ref, dv_ref = refs

    def products(n, d, at, j0, keys, kind):
        part = slice(j0, j0 + keys)
        return dot_turned(kx_ref[d, part], qx_ref[n]), dot_turned(v_ref[d, part], sn_ref[n])

    ready = products(*jobs[0])
    dk = dv = None
    for index, (n, d, at, j0, keys, kind) in enumerate(jobs):
        part = slice(j0, j0 + keys)
        logits, dp = ready
        if index + 1 < len(jobs):
            ready = products(*jobs[index + 1])
        p = jnp.exp2(logits * SCALE - row_ref[n, 0:1])
        if kind is not None:
            p = jnp.where(mask_of(kind, keys), p, 0.0)
        ds = (p * (dp - row_ref[n, 1:2])).astype(BF16)
        more_v, more_k = dot(p.astype(BF16), sn_ref[n]), dot(ds, qx_ref[n, :, :DIM])
        dq_ref[n - first] += dot(kt_ref[d, :, part], ds)
        if keys == ROWS:
            dv = more_v if dv is None else dv + more_v
            dk = more_k if dk is None else dk + more_k
        else:
            dv_ref[d - base, part] += more_v
            dk_ref[d - base, part] += more_k
    if dv is not None:
        dv_ref[d - base] += dv
        dk_ref[d - base] += dk


def put_sums(ref, dk, dv):
    ref[:ROWS] = (dk * FACTOR).astype(ref.dtype)
    ref[ROWS:] = dv.astype(ref.dtype)


def put_queries(ref, dq_ref, first):
    for at in range(TILES):
        for h in range(HEADS):
            part = dq_ref[first + at, :, h * TILE : (h + 1) * TILE] * FACTOR
            ref[at * TILE : (at + 1) * TILE, h * DIM : (h + 1) * DIM] = part.T.astype(ref.dtype)


def grad_call(body, positions, blocks, shards, operands, outs, micros):
    return pl.pallas_call(
        body,
        out_shape=outs,
        in_specs=[SMEM] + [VMEM] * len(operands),
        out_specs=(VMEM,) * len(outs),
        scratch_shapes=[
            pltpu.VMEM((blocks, DIM, WIDE), F32),
            pltpu.VMEM((shards, ROWS, DIM), F32),
            pltpu.VMEM((shards, ROWS, DIM), F32),
        ],
        compiler_params=pltpu.CompilerParams(vmem_limit_bytes=VMEM_LIMIT),
        cost_estimate=cost(micros),
    )(positions, *operands)


HALF = 2 * TILES
HELD = jax.ShapeDtypeStruct((HALF, DIM, WIDE), F32)
SUMS = jax.ShapeDtypeStruct((2, ROWS, DIM), F32)
SEND = jax.ShapeDtypeStruct((2 * ROWS, DIM), BF16)
ROW = jax.ShapeDtypeStruct((TEAM * TILES, 8, WIDE), F32)


def farthest_kernel(pos_ref, *refs):
    stat_refs, keys, (qx_ref, sn_ref) = refs[0:4], refs[4:7], refs[7:9]
    send_ref, row_ref, dq_ref = refs[9:12]
    dk_ref, dv_ref = refs[12:14]
    work = (*keys, qx_ref, sn_ref, row_ref, dq_ref, dk_ref, dv_ref)
    place = Place(pos_ref)
    fill_stats(range(TEAM), stat_refs, row_ref)
    for ref in (dq_ref, dk_ref, dv_ref):
        ref[...] = jnp.zeros_like(ref)

    def block(u):
        grad_jobs(work, 0, [(place.slot[u] * TILES + one[0], 0, *one) for one in block_jobs(u, 2)])

    for u in range(1, TEAM):
        pl.when(place.wrap[u] == 1)(functools.partial(block, u))
    put_sums(send_ref, dk_ref[0], dv_ref[0])


def far_kernel(pos_ref, *refs):
    keys, (qx_ref, sn_ref, row_ref, held_ref) = refs[0:3], refs[3:7]
    near_ref, away_ref, send_ref = refs[7:10]
    dq_ref, dk_ref, dv_ref = refs[10:13]
    work = (*keys, qx_ref, sn_ref, row_ref, dq_ref, dk_ref, dv_ref)
    place = Place(pos_ref)
    dq_ref[...] = held_ref[...]
    dk_ref[...] = jnp.zeros_like(dk_ref)
    dv_ref[...] = jnp.zeros_like(dv_ref)

    def block(u, t):
        grad_jobs(work, 2, [(place.slot[u] * TILES + one[0], 2, *one) for one in block_jobs(u, t)])

    block(0, 2)
    for u in range(1, TEAM):
        pl.when(place.wrap[u] == 0)(functools.partial(block, u, 2))
        pl.when(place.wrap[u] == 1)(functools.partial(block, u, 1))
    near_ref[...] = dq_ref[:HALF]
    away_ref[...] = dq_ref[HALF:]
    put_sums(send_ref, dk_ref[0], dv_ref[0])


def away_kernel(pos_ref, *refs):
    held_ref, dq_far_ref, dq_both_ref, sums0_ref, sums1_ref = refs[6:11]
    dq_ref, dk_ref, dv_ref = refs[11:14]
    work = refs[0:6] + refs[11:14]
    place = Place(pos_ref)
    dq_ref[...] = held_ref[...]
    dk_ref[...] = jnp.zeros_like(dk_ref)
    dv_ref[...] = jnp.zeros_like(dv_ref)

    def block(index, d):
        jobs = [(HALF + index * TILES + one[0], d, *one) for one in block_jobs(1, 0)]
        grad_jobs(work, 0, jobs, HALF)

    for index in range(2):
        block(index, 1)
    for index in range(2):
        pl.when(place.slot_wrap(2 + index) == 0)(functools.partial(block, index, 0))
    put_queries(dq_far_ref, dq_ref, 0)
    put_queries(dq_both_ref, dq_ref, TILES)
    for d, ref in enumerate((sums0_ref, sums1_ref)):
        ref[0] = dk_ref[d]
        ref[1] = dv_ref[d]


def near_kernel(pos_ref, *refs):
    held_ref, sums_ref, _, out_ref, send_ref = refs[6:11]
    dq_ref, dk_ref, dv_ref = refs[11:14]
    work = refs[0:6] + refs[11:14]
    dq_ref[...] = held_ref[...]
    dk_ref[0] = sums_ref[0]
    dv_ref[0] = sums_ref[1]
    for index in range(2):
        grad_jobs(work, 1, [(index * TILES + one[0], 1, *one) for one in block_jobs(1, 0)])
    out_ref[...] = dq_ref[...]
    put_sums(send_ref, dk_ref[0], dv_ref[0])


def own_kernel(pos_ref, *refs):
    held_ref, sums_ref, _, dq_own_ref, dq_core_ref, kv_ref = refs[6:12]
    dq_ref, dk_ref, dv_ref = refs[12:15]
    work = refs[0:6] + refs[12:15]
    place = Place(pos_ref)
    dq_ref[...] = held_ref[...]
    dk_ref[0] = sums_ref[0]
    dv_ref[0] = sums_ref[1]

    def other():
        grad_jobs(work, 0, [(TILES + one[0], 0, *one) for one in block_jobs(1, 0)])

    grad_jobs(work, 0, [(one[0], 0, *one) for one in block_jobs(0, 0)])
    pl.when(place.slot_wrap(1) == 0)(other)
    put_queries(dq_own_ref, dq_ref, 0)
    put_queries(dq_core_ref, dq_ref, TILES)
    put_sums(kv_ref, dk_ref[0], dv_ref[0])


def team_slots(value):
    core = permute(value, lambda s: s ^ 1)
    far = permute(value, lambda s: s ^ 2)
    both = permute(far, lambda s: s ^ 1)
    return [value, core, far, both]


def per_device(queries, key_rows, value_rows, positions, latent_ids, latent_acts, latent_dirs):
    kv = jnp.concatenate([key_rows, value_rows], axis=0)
    kvs = [kv] + [permute(kv, lambda s, d=d: s + TEAM * d) for d in (1, 2)]
    kvs.append(permute(kvs[2], lambda s: s + TEAM))
    qs = team_slots(with_seeds(queries, latent_ids, latent_acts, latent_dirs))
    early = keys_of(positions, (0, 1, 2), kvs, EARLY_COST)
    qx, sn, run = early_stats(positions, qs, *early[:2])
    late = keys_of(positions, (3,), kvs, LATE_COST, (run,))
    stat = late_stats(positions, *late[:2], qx, sn, run)
    stats = [stat] + [permute(stat, lambda s, e=e: s ^ e) for e in range(1, TEAM)]

    shape = jax.ShapeDtypeStruct
    wide, thin = (ROWS, HEADS * DIM), (2 * ROWS, DIM)
    send3, rows, held = pl.pallas_call(
        farthest_kernel,
        out_shape=(SEND, ROW, shape((TEAM * TILES, DIM, WIDE), F32)),
        in_specs=[SMEM] + [VMEM] * 9,
        out_specs=(VMEM,) * 3,
        scratch_shapes=[pltpu.VMEM((1, ROWS, DIM), F32)] * 2,
        compiler_params=pltpu.CompilerParams(vmem_limit_bytes=VMEM_LIMIT),
        cost_estimate=cost(FAR_COST),
    )(positions, *stats, *late, qx, sn)
    held_near, held_away, send2 = grad_call(
        far_kernel,
        positions,
        TEAM * TILES,
        1,
        (*early, qx, sn, rows, held),
        (HELD, HELD, shape(thin, F32)),
        FAR_COST,
    )

    def call(body, shards, extra, outs, micros):
        operands = (*early, qx, sn, rows, *extra)
        return grad_call(body, positions, HALF, shards, operands, outs, micros)

    send3 = permute(send3, lambda s: s - TEAM)
    send2 = (send2 + send3.astype(F32)).astype(BF16)
    back2 = permute(send2, lambda s: s - 2 * TEAM)
    dq_far, dq_both, sums0, sums1 = call(
        away_kernel, 2, (held_away,), (shape(wide, F32), shape(wide, BF16), SUMS, SUMS), GRAD_COST
    )
    dq_both = permute(dq_both, lambda s: s ^ 1)
    held_near, send1 = call(near_kernel, 1, (held_near, sums1, send2), (HELD, SEND), GRAD_COST)
    back1 = permute(send1, lambda s: s - TEAM)
    dq_far = (dq_far + dq_both.astype(F32)).astype(BF16)
    dq_back = permute(dq_far, lambda s: s ^ 2)
    dq_own, dq_core, kv_own = call(
        own_kernel,
        1,
        (held_near, sums0, dq_far),
        (shape(wide, F32), shape(wide, BF16), shape(thin, F32)),
        GRAD_COST,
    )
    dq_core = permute(dq_core, lambda s: s ^ 1)
    grad_q = (dq_own + dq_core.astype(F32) + dq_back.astype(F32)).astype(BF16)
    grad_kv = kv_own + back1.astype(F32) + back2.astype(F32)
    return grad_q, grad_kv[:ROWS].astype(BF16), grad_kv[ROWS:].astype(BF16)


def solution(mesh):
    in_specs = (
        P(("mp", "ctx"), None),
        P(("mp", "ctx"), None),
        P(("mp", "ctx"), None),
        P("ctx"),
        P(("mp", "ctx"), None),
        P(("mp", "ctx"), None),
        P("mp", None),
    )
    out_specs = (P(("mp", "ctx"), None), P(("mp", "ctx"), None), P(("mp", "ctx"), None))
    return jax.shard_map(
        per_device, mesh=mesh, in_specs=in_specs, out_specs=out_specs, check_vma=False
    )
```
